256 devices in a mesh: grp: 2 (over y_lo), gx: 32 (over z, x), gy: 4 (over y_hi, core).
Axes of the slice: x: 4, y: 4 (y_hi: 2, y_lo: 2; y = y_hi * 2 + y_lo), z: 8, core: 2. Of those that a mesh axis runs over, the one named last changes fastest.
Arguments:
- scalars: float32 [2, 32, 256, 128], P('grp', None, ('gx', 'gy')), may hold values from -9 to 9
- velocity: float32 [3, 32, 256, 128], P(None, None, ('gx', 'gy')), may hold values from -0.15 to 0.15
- w_lift: bfloat16 [64, 54], replicated, may hold values from -0.875 to 0.875
- b_lift: float32 [64], replicated, may hold values from -3 to 3
- w_mix: bfloat16 [64, 1728], replicated, may hold values from -0.15625 to 0.15625
- b_mix: float32 [64], replicated, may hold values from -3 to 3
- w_out: bfloat16 [2, 64], replicated, may hold values from -0.75 to 0.75
- b_out: float32 [2], replicated, may hold values from -3 to 3
Outputs:
- advanced: float32 [2, 32, 256, 128], P('grp', None, ('gx', 'gy'))
- lift_grad: float32 [64, 54], replicated
- liftbias_grad: float32 [64], replicated
- mix_grad: float32 [64, 1728], replicated
- mixbias_grad: float32 [64], replicated
- out_grad: float32 [2, 64], replicated
- outbias_grad: float32 [2], replicated
The draws below stay inside these ranges and needn't reach their ends.
All inputs are finite; a program needn't handle non-finite values.
Results may differ from the reference program's by a relative error of at most 0.0003.
Values may be sent and summed in bfloat16 or wider, within the bound.
A program may use at most 64 MiB of HBM per device.

```python
import math
import jax
import jax.numpy as jnp
from jax import lax

H = 64
DEPTH = 128
NX = 32
NY = 256


def draw_scalars(key, part):
    key = jax.random.fold_in(key, 11)
    base_key, rough_key = jax.random.split(key)
    rows = jnp.arange(NY, dtype=jnp.float32) / jnp.float32(max(NY - 1, 1))
    ramp = jnp.exp(rows * jnp.log(jnp.float32(3.0)))
    rough = jax.random.uniform(rough_key, (2, NX, 1, DEPTH), jnp.float32, 0.5, 1.5)
    base = jnp.clip(jax.random.normal(base_key, (2, NX, NY, DEPTH), jnp.float32), -4.0, 4.0)
    return (0.5 * base * rough * ramp[None, None, :, None]).astype(jnp.float32)


def levels(key, shape, cuts, least, top_value):
    level = 1.0
    for axis_at, blocks in cuts:
        heights = jax.random.uniform(jax.random.fold_in(jax.random.fold_in(key, 6), axis_at), (blocks,), jnp.float32, least / len(cuts), top_value / len(cuts))
        level = level * jnp.repeat(jnp.exp(heights), shape[axis_at] // blocks).reshape((-1,) + (1,) * (len(shape) - 1 - axis_at))
    return level


def gaussian(rng, shape, scale, limit, shards=(), held_as=jnp.bfloat16):
    values = jax.random.normal(rng, shape, jnp.float32) * scale
    if len(shards) > 0:
        values = levels(rng, shape, shards, -0.22, 0.18) * values
    return jnp.clip(values, min=-limit, max=limit).astype(held_as)


def setup_inputs(seed: int = 0) -> dict:
    keys = jax.random.split(jax.random.key(seed), 9)
    scalars = draw_scalars(jax.random.fold_in(keys[8], 71), 0)
    velocity = gaussian(keys[1], (3, NX, NY, DEPTH), 0.05, 0.15, ((2, 128),), jnp.float32)
    w_lift = gaussian(keys[2], (H, 2 * 27), 54 ** -0.5, 0.875)
    b_lift = gaussian(keys[3], (H,), 0.5, 3.0, (), jnp.float32)
    w_mix = gaussian(keys[4], (H, H * 27), (H * 27) ** -0.5, 0.15625)
    b_mix = gaussian(keys[5], (H,), 0.5, 3.0, (), jnp.float32)
    w_out = gaussian(keys[6], (2, H), H ** -0.5, 0.75)
    b_out = gaussian(keys[7], (2,), 0.5, 3.0, (), jnp.float32)
    return dict(scalars=scalars, velocity=velocity, w_lift=w_lift, b_lift=b_lift, w_mix=w_mix, b_mix=b_mix, w_out=w_out, b_out=b_out)


def stencil(padded, velocity, diffusivity):
    centre = padded[:, 1:-1, 1:-1, 1:-1]
    plus_x = padded[:, 2:, 1:-1, 1:-1]
    minus_x = padded[:, :-2, 1:-1, 1:-1]
    plus_y = padded[:, 1:-1, 2:, 1:-1]
    minus_y = padded[:, 1:-1, :-2, 1:-1]
    plus_z = padded[:, 1:-1, 1:-1, 2:]
    minus_z = padded[:, 1:-1, 1:-1, :-2]
    laplace = plus_x + minus_x + plus_y + minus_y + plus_z + minus_z - 6.0 * centre
    advect = velocity[0] * (plus_x - minus_x) + velocity[1] * (plus_y - minus_y) + velocity[2] * (plus_z - minus_z)
    return centre + diffusivity * laplace - 0.5 * advect

def advance(tracer, velocity, diffusivity):
    padded = jnp.pad(tracer, ((0, 0), (1, 1), (1, 1), (1, 1)))
    return stencil(padded, velocity, diffusivity)

def convolve(padded, kernel):
    result = lax.conv_general_dilated(padded[None], kernel, (1, 1, 1), ((0, 0), (0, 0), (1, 1)), dimension_numbers=('NCDHW', 'OIDHW', 'NCDHW'), preferred_element_type=jnp.float32)
    return result[0]

def kernel_grad(padded, cotangent):
    deepened = jnp.pad(padded, ((0, 0), (0, 0), (0, 0), (1, 1)))
    size_x, size_y, size_z = (cotangent.shape[1], cotangent.shape[2], cotangent.shape[3])
    cot_rows = cotangent.reshape(cotangent.shape[0], -1)
    pieces = []
    for offset_x in range(3):
        for offset_y in range(3):
            for offset_z in range(3):
                window = deepened[:, offset_x:offset_x + size_x, offset_y:offset_y + size_y, offset_z:offset_z + size_z]
                window = window.reshape(deepened.shape[0], -1)
                pieces.append(jnp.dot(cot_rows, window.T, preferred_element_type=jnp.float32))
    stacked = jnp.stack(pieces, axis=-1)
    return stacked.reshape(stacked.shape[0], -1)

def gelu_back(before, cotangent):
    return jax.vjp(jax.nn.gelu, before)[1](cotangent)[0]

def pad_sides(values):
    return jnp.pad(values, ((0, 0), (1, 1), (1, 1), (0, 0)))

def reference(scalars, velocity, w_lift, b_lift, w_mix, b_mix, w_out, b_out):
    diffusivity = jnp.array([0.08, 0.12], dtype=jnp.float32).reshape(2, 1, 1, 1)
    stepped = advance(scalars, velocity, diffusivity)
    advanced = advance(stepped, velocity, diffusivity)
    increment = advanced - stepped
    loss_scale = 2.0 / math.sqrt(NX * NY * DEPTH)
    hidden = w_mix.shape[0]
    lift_kernel = w_lift.reshape(hidden, 2, 3, 3, 3)
    mix_kernel = w_mix.reshape(hidden, hidden, 3, 3, 3)
    net_input = stepped.astype(jnp.bfloat16)
    input_rim = pad_sides(net_input)
    lift_pre = convolve(input_rim, lift_kernel) + b_lift[:, None, None, None]
    lifted = jax.nn.gelu(lift_pre).astype(jnp.bfloat16)
    lifted_rim = pad_sides(lifted)
    mix_pre = convolve(lifted_rim, mix_kernel) + b_mix[:, None, None, None]
    mixed = jax.nn.gelu(mix_pre).astype(jnp.bfloat16)
    predicted = jnp.einsum('kc,cxyz->kxyz', w_out.astype(jnp.float32), mixed.astype(jnp.float32)) + b_out[:, None, None, None]
    error_cot = (loss_scale * (predicted - increment)).astype(jnp.bfloat16)
    out_grad = jnp.einsum('kxyz,cxyz->kc', error_cot.astype(jnp.float32), mixed.astype(jnp.float32))
    outbias_grad = lax.optimization_barrier(jnp.sum(error_cot.astype(jnp.float32), axis=(1, 2, 3)))
    mixed_cot = jnp.einsum('kc,kxyz->cxyz', w_out.astype(jnp.float32), error_cot.astype(jnp.float32))
    mixpre_cot = gelu_back(mix_pre, mixed_cot).astype(jnp.bfloat16)
    mix_grad = kernel_grad(lifted_rim, mixpre_cot)
    mixbias_grad = lax.optimization_barrier(jnp.sum(mixpre_cot.astype(jnp.float32), axis=(1, 2, 3)))
    flipped = jnp.flip(mix_kernel, (2, 3, 4)).transpose(1, 0, 2, 3, 4)
    lifted_cot = convolve(pad_sides(mixpre_cot), flipped)
    liftpre_cot = gelu_back(lift_pre, lifted_cot).astype(jnp.bfloat16)
    lift_grad = kernel_grad(input_rim, liftpre_cot)
    liftbias_grad = lax.optimization_barrier(jnp.sum(liftpre_cot.astype(jnp.float32), axis=(1, 2, 3)))
    return (advanced, lift_grad, liftbias_grad, mix_grad, mixbias_grad, out_grad, outbias_grad)
```

```python
import math

import jax
import jax.numpy as jnp
from jax import lax
from jax.experimental import pallas as pl
from jax.experimental.pallas import tpu as pltpu
from jax.sharding import PartitionSpec as P


MESH = pl.DeviceIdType.MESH


def total_kernel(buf, out, from_core, mine, from_plane, from_z, s1, r1, s2, r2, s3, r3, s4, r4, s5, r5):
    y_lo = lax.axis_index("grp")
    gx = lax.axis_index("gx")
    gy = lax.axis_index("gy")
    z, x = gx // 4, gx % 4
    y_hi, core = gy // 2, gy % 2
    place = x * 4 + y_hi * 2 + y_lo
    sibling = (y_lo, gx, y_hi * 2 + 1 - core)

    def in_plane(other):
        return (other % 2, z * 4 + other // 4, ((other // 2) % 2) * 2 + core)

    def in_z(other):
        return (y_lo, other * 4 + x, gy)

    barrier = pltpu.get_barrier_semaphore()
    pl.semaphore_signal(barrier, inc=1, device_id=sibling, device_id_type=MESH)

    def greet_plane(j, _):
        pl.semaphore_signal(barrier, inc=1, device_id=in_plane((place + j) % 16), device_id_type=MESH)
        return 0

    def greet_z(j, _):
        pl.semaphore_signal(barrier, inc=1, device_id=in_z((z + j) % 8), device_id_type=MESH)
        return 0

    lax.fori_loop(1, 16, greet_plane, 0)
    lax.fori_loop(1, 8, greet_z, 0)
    pl.semaphore_wait(barrier, 23)

    theirs = pl.multiple_of((1 - core) * 16, 16)
    ours = pl.multiple_of(core * 16, 16)
    swap = pltpu.make_async_remote_copy(
        buf.at[pl.ds(theirs, 16)], from_core, s1, r1, device_id=sibling, device_id_type=MESH
    )
    swap.start()
    swap.wait()

    def add_core(j, _):
        mine[j] = buf[ours + j] + from_core[j]
        return 0

    lax.fori_loop(0, 16, add_core, 0)

    def to_plane(j):
        other = (place + j) % 16
        return pltpu.make_async_remote_copy(
            mine.at[other], from_plane.at[place], s2.at[other], r2.at[place],
            device_id=in_plane(other), device_id_type=MESH,
        )

    def of_plane(j):
        other = (place + j) % 16
        return pltpu.make_async_remote_copy(
            mine.at[other], from_plane.at[other], s2.at[other], r2.at[other],
            device_id=in_plane(other), device_id_type=MESH,
        )

    lax.fori_loop(1, 16, lambda j, _: (to_plane(j).start(), 0)[1], 0)
    from_plane[place] = mine[place]

    def wait_plane(j, _):
        of_plane(j).wait()
        return 0

    lax.fori_loop(1, 16, wait_plane, 0)
    total = from_plane[0]
    for j in range(1, 16):
        total = total + from_plane[j]
    from_z[z] = total

    def to_z(j):
        other = (z + j) % 8
        return pltpu.make_async_remote_copy(
            from_z.at[z], from_z.at[z], s3.at[other], r3.at[z], device_id=in_z(other), device_id_type=MESH
        )

    def of_z(j):
        other = (z + j) % 8
        return pltpu.make_async_remote_copy(
            from_z.at[other], from_z.at[other], s3.at[other], r3.at[other], device_id=in_z(other), device_id_type=MESH
        )

    lax.fori_loop(1, 8, lambda j, _: (to_z(j).start(), 0)[1], 0)

    def wait_z(j, _):
        of_z(j).wait()
        return 0

    lax.fori_loop(1, 8, wait_z, 0)
    total = from_z[0]
    for j in range(1, 8):
        total = total + from_z[j]
    out[ours + place] = total

    def gather(j):
        other = (place + j) % 16
        return pltpu.make_async_remote_copy(
            out.at[ours + place], out.at[ours + place], s4.at[other], r4.at[place],
            device_id=in_plane(other), device_id_type=MESH,
        )

    def gathered(j):
        other = (place + j) % 16
        return pltpu.make_async_remote_copy(
            out.at[ours + other], out.at[ours + other], s4.at[other], r4.at[other],
            device_id=in_plane(other), device_id_type=MESH,
        )

    def hand(j):
        other = (place + j) % 16
        return pltpu.make_async_remote_copy(
            out.at[ours + other], out.at[ours + other], s5.at[other], r5.at[other],
            device_id=sibling, device_id_type=MESH,
        )

    def handed(j):
        other = (place + j) % 16
        return pltpu.make_async_remote_copy(
            out.at[theirs + other], out.at[theirs + other], s5.at[other], r5.at[other],
            device_id=sibling, device_id_type=MESH,
        )

    lax.fori_loop(1, 16, lambda j, _: (gather(j).start(), 0)[1], 0)
    hand(0).start()

    def pass_on(j, _):
        gathered(j).wait_recv()
        hand(j).start()
        return 0

    lax.fori_loop(1, 16, pass_on, 0)

    def finish(j, _):
        handed(j).wait_recv()
        hand(j).wait_send()
        return 0

    lax.fori_loop(0, 16, finish, 0)
    lax.fori_loop(1, 16, lambda j, _: (gather(j).wait_send(), 0)[1], 0)


def all_total(buf):
    rows = buf.shape[1]
    chunk = (rows, 128)
    dma = pltpu.SemaphoreType.DMA
    vmem = pl.BlockSpec(memory_space=pltpu.VMEM)
    return pl.pallas_call(
        total_kernel,
        out_shape=jax.ShapeDtypeStruct(buf.shape, jnp.float32),
        in_specs=[vmem],
        out_specs=vmem,
        scratch_shapes=[
            pltpu.VMEM((16,) + chunk, jnp.float32),
            pltpu.VMEM((16,) + chunk, jnp.float32),
            pltpu.VMEM((16,) + chunk, jnp.float32),
            pltpu.VMEM((8,) + chunk, jnp.float32),
            dma, dma, dma((16,)), dma((16,)), dma((8,)), dma((8,)),
            dma((16,)), dma((16,)), dma((16,)), dma((16,)),
        ],
        compiler_params=pltpu.CompilerParams(collective_id=0, has_side_effects=True, vmem_limit_bytes=40 * 2**20),
        name="total",
    )(buf)


def extended(value, sides, width):
    for axis, dim in sides:
        size, length = (lax.axis_size(axis), value.shape[dim])
        up = [(i, (i + 1) % size) for i in range(size - 1)]
        down = [(j, i) for i, j in up]
        last = lax.slice_in_dim(value, length - width, length, axis=dim)
        leading = lax.slice_in_dim(value, 0, width, axis=dim)
        before = lax.ppermute(last, axis, up)
        after = lax.ppermute(leading, axis, down)
        value = jnp.concatenate([before, value, after], axis=dim)
    return value


def stencil(padded, velocity, diffusivity):
    centre = padded[:, 1:-1, 1:-1, 1:-1]
    plus_x = padded[:, 2:, 1:-1, 1:-1]
    minus_x = padded[:, :-2, 1:-1, 1:-1]
    plus_y = padded[:, 1:-1, 2:, 1:-1]
    minus_y = padded[:, 1:-1, :-2, 1:-1]
    plus_z = padded[:, 1:-1, 1:-1, 2:]
    minus_z = padded[:, 1:-1, 1:-1, :-2]
    laplace = plus_x + minus_x + plus_y + minus_y + plus_z + minus_z - 6.0 * centre
    advect = (
        velocity[0] * (plus_x - minus_x)
        + velocity[1] * (plus_y - minus_y)
        + velocity[2] * (plus_z - minus_z)
    )
    return centre + diffusivity * laplace - 0.5 * advect


def advance(tracer, velocity, diffusivity):
    widened = extended(tracer, ((("gx", "gy"), 2),), 1)
    padded = jnp.pad(widened, ((0, 0), (1, 1), (0, 0), (1, 1)))
    return stencil(padded, velocity, diffusivity)


def convolve(padded, kernel):
    result = lax.conv_general_dilated(
        padded[None],
        kernel,
        (1, 1, 1),
        ((0, 0), (0, 0), (1, 1)),
        dimension_numbers=("NCDHW", "OIDHW", "NCDHW"),
        preferred_element_type=jnp.float32,
    )
    return result[0]


def kernel_grad(padded, cotangent):
    deepened = jnp.pad(padded, ((0, 0), (0, 0), (0, 0), (1, 1)))
    size_x, size_y, size_z = (cotangent.shape[1], cotangent.shape[2], cotangent.shape[3])
    cot_rows = cotangent.reshape(cotangent.shape[0], -1)
    pieces = []
    for offset_x in range(3):
        for offset_y in range(3):
            for offset_z in range(3):
                window = deepened[
                    :,
                    offset_x : offset_x + size_x,
                    offset_y : offset_y + size_y,
                    offset_z : offset_z + size_z,
                ]
                window = window.reshape(deepened.shape[0], -1)
                pieces.append(
                    lax.dot_general(
                        cot_rows,
                        window,
                        (((1,), (1,)), ((), ())),
                        preferred_element_type=jnp.float32,
                    )
                )
    stacked = jnp.stack(pieces, axis=-1)
    return stacked.reshape(stacked.shape[0], -1)


def gelu_back(before, cotangent):
    return jax.vjp(jax.nn.gelu, before)[1](cotangent)[0]


def slab_rim(values):
    return extended(values, (("grp", 1), (("gx", "gy"), 2)), 1)


def learn(inputs, targets, w_lift, b_lift, w_mix, b_mix, w_out, b_out, loss_scale, add_rim):
    hidden = w_mix.shape[0]
    lift_kernel = w_lift.reshape(hidden, 2, 3, 3, 3)
    mix_kernel = w_mix.reshape(hidden, hidden, 3, 3, 3)
    net_input = inputs.astype(jnp.bfloat16)
    input_rim = add_rim(net_input)
    lift_pre = convolve(input_rim, lift_kernel) + b_lift[:, None, None, None]
    lifted = jax.nn.gelu(lift_pre).astype(jnp.bfloat16)
    lifted_rim = add_rim(lifted)
    mix_pre = convolve(lifted_rim, mix_kernel) + b_mix[:, None, None, None]
    mixed = jax.nn.gelu(mix_pre).astype(jnp.bfloat16)
    predicted = (
        jnp.einsum("kc,cxyz->kxyz", w_out, mixed, preferred_element_type=jnp.float32)
        + b_out[:, None, None, None]
    )
    error_cot = (loss_scale * (predicted - targets)).astype(jnp.bfloat16)
    out_grad = jnp.einsum("kxyz,cxyz->kc", error_cot, mixed, preferred_element_type=jnp.float32)
    outbias_grad = jnp.sum(error_cot, axis=(1, 2, 3), dtype=jnp.float32)
    mixed_cot = jnp.einsum("kc,kxyz->cxyz", w_out, error_cot, preferred_element_type=jnp.float32)
    mixpre_cot = gelu_back(mix_pre, mixed_cot).astype(jnp.bfloat16)
    mix_grad = kernel_grad(lifted_rim, mixpre_cot)
    mixbias_grad = jnp.sum(mixpre_cot, axis=(1, 2, 3), dtype=jnp.float32)
    flipped = jnp.flip(mix_kernel, (2, 3, 4)).transpose(1, 0, 2, 3, 4)
    lifted_cot = convolve(add_rim(mixpre_cot), flipped)
    liftpre_cot = gelu_back(lift_pre, lifted_cot).astype(jnp.bfloat16)
    lift_grad = kernel_grad(input_rim, liftpre_cot)
    liftbias_grad = jnp.sum(liftpre_cot, axis=(1, 2, 3), dtype=jnp.float32)
    return (lift_grad, liftbias_grad, mix_grad, mixbias_grad, out_grad, outbias_grad)


def on_device(scalars, velocity, w_lift, b_lift, w_mix, b_mix, w_out, b_out):
    diffusivity = jnp.where(lax.axis_index("grp") == 0, jnp.float32(0.08), jnp.float32(0.12))
    stepped = advance(scalars, velocity, diffusivity)
    advanced = advance(stepped, velocity, diffusivity)
    increment = advanced - stepped
    total_cells = scalars.size * lax.axis_size("gx") * lax.axis_size("gy")
    loss_scale = 2.0 / math.sqrt(total_cells)
    inputs, targets = (
        lax.all_to_all(stepped, "grp", split_axis=1, concat_axis=0, tiled=True),
        lax.all_to_all(increment, "grp", split_axis=1, concat_axis=0, tiled=True),
    )
    results = learn(
        inputs, targets, w_lift, b_lift, w_mix, b_mix, w_out, b_out, loss_scale, slab_rim
    )
    lift_grad, liftbias_grad, mix_grad, mixbias_grad, out_grad, outbias_grad = results
    parts = (lift_grad, liftbias_grad, mix_grad, mixbias_grad, out_grad, outbias_grad)
    flat = jnp.concatenate([part.reshape(-1) for part in parts])
    rows = -(-flat.size // (32 * 128))
    flat = jnp.pad(flat, (0, rows * 32 * 128 - flat.size))
    flat = all_total(flat.reshape(32, rows, 128)).reshape(-1)
    summed, at = [], 0
    for part in parts:
        summed.append(flat[at : at + part.size].reshape(part.shape))
        at += part.size
    return (advanced, summed[0], summed[1], summed[2], summed[3], summed[4], summed[5])


def solution(mesh):
    in_specs = (
        P("grp", None, ("gx", "gy"), None),
        P(None, None, ("gx", "gy"), None),
        P(),
        P(),
        P(),
        P(),
        P(),
        P(),
    )
    out_specs = (P("grp", None, ("gx", "gy"), None), P(), P(), P(), P(), P(), P())
    return jax.shard_map(
        on_device, mesh=mesh, in_specs=in_specs, out_specs=out_specs, check_vma=False
    )
```

```python
import functools
import math

import jax
import jax.numpy as jnp
import numpy as np
from jax import lax
from jax.experimental import pallas as pl
from jax.experimental.pallas import tpu as pltpu
from jax.sharding import PartitionSpec as P

MESH = pl.DeviceIdType.MESH
F32 = jnp.float32
BF16 = jnp.bfloat16
VMEM = pl.BlockSpec(memory_space=pltpu.VMEM)
VMEM_BYTES = 48 * 2**20


def place():
    return lax.axis_index("grp"), lax.axis_index("gx") * 4 + lax.axis_index("gy")


def roll_z(value, step):
    lane = lax.broadcasted_iota(jnp.int32, value.shape, value.ndim - 1)
    edge = 0 if step > 0 else 127
    return jnp.where(lane % 128 == edge, 0.0, pltpu.roll(value, step % 128, value.ndim - 1))


def solver_kernel(
    sc, vel, adv, net, tgt,
    halo, held, wide, seen, inc, gains,
    a_send, a_recv, b_send, b_recv, n_send, n_recv, c_send, c_recv,
):
    g, s = place()
    diffusivity = jnp.where(g == 0, jnp.float32(0.08), jnp.float32(0.12))

    def device(step, field):
        other = lax.rem(s + step + 128, 128)
        return (field, other // 4, lax.rem(other, 4))

    partners = [(d, f) for d in (-2, -1, 0, 1, 2) for f in (0, 1) if (d, f) != (0, 0)]
    def partner(d, f):
        return device(d, g if f == 0 else 1 - g)

    barrier = pltpu.get_barrier_semaphore()
    for d, f in partners:
        pl.semaphore_signal(barrier, inc=1, device_id=partner(d, f), device_id_type=MESH)
    pl.semaphore_wait(barrier, len(partners))

    def send(src, dst, ssem, rsem, d, f):
        return pltpu.make_async_remote_copy(
            src, dst, ssem, rsem, device_id=partner(d, f), device_id_type=MESH
        )

    first = [
        send(sc, halo.at[0], a_send.at[0], a_recv.at[0], 1, 0),
        send(sc, halo.at[1], a_send.at[1], a_recv.at[1], -1, 0),
    ]
    for copy in first:
        copy.start()

    speed = [[vel[pl.ds(64 * d + y, 32, stride=2), :] for y in range(2)] for d in range(3)]
    row = lax.broadcasted_iota(jnp.int32, (32, 128), 0)

    def step(centre, below, above, y):
        plus_x = jnp.where(row == 31, 0.0, pltpu.roll(centre, 31, 0))
        minus_x = jnp.where(row == 0, 0.0, pltpu.roll(centre, 1, 0))
        plus_z = roll_z(centre, -1)
        minus_z = roll_z(centre, 1)
        laplace = plus_x + minus_x + above + below + plus_z + minus_z - 6.0 * centre
        advect = (
            speed[0][y] * (plus_x - minus_x)
            + speed[1][y] * (above - below)
            + speed[2][y] * (plus_z - minus_z)
        )
        return centre + diffusivity * laplace - 0.5 * advect

    own = [sc[pl.ds(y, 32, stride=2), :] for y in range(2)]
    for copy in first:
        copy.wait_recv()
    below = jnp.where(s == 0, 0.0, halo[0, pl.ds(1, 32, stride=2), :])
    above = jnp.where(s == 127, 0.0, halo[1, pl.ds(0, 32, stride=2), :])
    stepped = [step(own[0], below, own[1], 0), step(own[1], own[0], above, 1)]
    for y in range(2):
        held[y] = stepped[y]
        wide[y] = stepped[y].astype(BF16)

    second = [
        send(held.at[1], gains.at[0], b_send.at[0], b_recv.at[0], 1, 0),
        send(held.at[0], gains.at[1], b_send.at[1], b_recv.at[1], -1, 0),
    ]
    third = []
    for index, (d, f) in enumerate(partners):
        field = g
        if abs(d) == 2:
            y = 1 if d > 0 else 0
            src, dst = wide.at[y], seen.at[2 - d, field, y]
        else:
            src, dst = wide, seen.at[2 - d, field]
        third.append(send(src, dst, n_send.at[index], n_recv.at[index], d, f))
    arrivals = []
    for index, (d, f) in enumerate(partners):
        field = g if f == 0 else 1 - g
        if abs(d) == 2:
            y = 1 if d > 0 else 0
            src, dst = wide.at[y], seen.at[2 - d, field, y]
        else:
            src, dst = wide, seen.at[2 - d, field]
        arrivals.append(send(src, dst, n_send.at[index], n_recv.at[index], d, f))
    for copy in second:
        copy.start()
    for copy in third:
        copy.start()
    for y in range(2):
        seen[2, g, y] = wide[y]
    net[pl.ds(0, 48), :] = jnp.zeros((48, 128), F32)
    net[pl.ds(35 * 16, 48), :] = jnp.zeros((48, 128), F32)
    tgt[pl.ds(0, 8), :] = jnp.zeros((8, 128), F32)
    tgt[pl.ds(33 * 8, 8), :] = jnp.zeros((8, 128), F32)

    for copy in second:
        copy.wait_recv()
    below = jnp.where(s == 0, 0.0, gains[0])
    above = jnp.where(s == 127, 0.0, gains[1])
    advanced = [
        step(stepped[0], below, stepped[1], 0),
        step(stepped[1], stepped[0], above, 1),
    ]
    for y in range(2):
        adv[pl.ds(y, 32, stride=2), :] = advanced[y]
        inc[g, 1 + y] = advanced[y] - stepped[y]
    fourth, landings = [], []
    for index, (d, f) in enumerate([(0, 1), (1, 0), (1, 1), (-1, 0), (-1, 1)]):
        def ends(field):
            if d == 0:
                return inc.at[g, pl.ds(1, 2)], inc.at[field, pl.ds(1, 2)]
            if d == 1:
                return inc.at[g, 2], inc.at[field, 0]
            return inc.at[g, 1], inc.at[field, 3]
        fourth.append(send(*ends(g), c_send.at[index], c_recv.at[index], d, f))
        landings.append(
            send(*ends(g if f == 0 else 1 - g), c_send.at[index], c_recv.at[index], d, f)
        )
    for copy in fourth:
        copy.start()

    for copy in arrivals:
        copy.wait_recv()
    for field in range(2):
        for yy in range(8):
            slab, y = (yy + 1) // 2, (yy + 1) % 2
            y_at = 2 * s - 3 + yy
            inside = (y_at >= 0) & (y_at < 256)
            value = jnp.where(inside, seen[slab, field, y].astype(F32), 0.0)
            net[pl.ds(48 + field * 8 + yy, 32, stride=16), :] = value
    for copy in landings:
        copy.wait_recv()
    for field in range(2):
        for yy in range(4):
            tgt[pl.ds(8 + yy * 2 + field, 32, stride=8), :] = inc[field, yy]
    for copy in first + second + third + fourth:
        copy.wait_send()


def solve(scalars, velocity):
    dma = pltpu.SemaphoreType.DMA
    return pl.pallas_call(
        solver_kernel,
        out_shape=(
            jax.ShapeDtypeStruct((64, 128), F32),
            jax.ShapeDtypeStruct((38 * 16, 128), F32),
            jax.ShapeDtypeStruct((34 * 8, 128), F32),
        ),
        in_specs=[VMEM, VMEM],
        out_specs=(VMEM, VMEM, VMEM),
        scratch_shapes=[
            pltpu.VMEM((2, 64, 128), F32),
            pltpu.VMEM((2, 32, 128), F32),
            pltpu.VMEM((2, 32, 128), BF16),
            pltpu.VMEM((5, 2, 2, 32, 128), BF16),
            pltpu.VMEM((2, 4, 32, 128), F32),
            pltpu.VMEM((2, 32, 128), F32),
            dma((2,)), dma((2,)), dma((2,)), dma((2,)),
            dma((9,)), dma((9,)), dma((5,)), dma((5,)),
        ],
        compiler_params=pltpu.CompilerParams(
            collective_id=0, has_side_effects=True, vmem_limit_bytes=VMEM_BYTES
        ),
        name="solver",
    )(scalars, velocity)


def gelu_parts(v):
    c = math.sqrt(2.0 / math.pi)
    square = v * v
    t = jnp.tanh(v * (c + (c * 0.044715) * square))
    half = 0.5 + 0.5 * t
    value = v * half
    slope = half + (0.5 * v) * (1.0 - t * t) * (c + (3.0 * c * 0.044715) * square)
    return value, slope


def rows_dot(a, b):
    return lax.dot_general(a, b, (((1,), (1,)), ((), ())), preferred_element_type=F32)


def net_kernel(
    loss_scale,
    net, tgt, w_lift, b_lift, w_mix, w_back, b_mix, w_out, w_outt, b_out, pick,
    packed,
    v3, lifted, slope1, cot, total, total_lift, total_out, sums,
):
    g, s = place()
    x0 = g * 16

    def fill(x, _):
        rows = net[pl.ds(pl.multiple_of((x0 + x) * 16, 16), 16), :]
        v3[x, pl.ds(0, 16), :] = roll_z(rows, 1).astype(BF16)
        v3[x, pl.ds(16, 16), :] = rows.astype(BF16)
        v3[x, pl.ds(32, 16), :] = roll_z(rows, -1).astype(BF16)
        return 0

    lax.fori_loop(0, 22, fill, 0)

    bias1 = jnp.broadcast_to(b_lift[...], (64, 128))
    bias1 = jnp.concatenate([bias1] * 6, axis=0)

    def lift(x, _):
        seen = jnp.concatenate(
            [v3[pl.ds(2 * x, 3)].reshape(144, 128), v3[pl.ds(2 * x + 1, 3)].reshape(144, 128)], axis=1
        )
        pre = jnp.dot(w_lift[...], seen, preferred_element_type=F32)
        for half in range(2):
            value, slope = gelu_parts(pre[:, half * 128 : half * 128 + 128] + bias1)
            lifted[2 * x + half] = value.astype(BF16)
            slope1[2 * x + half] = slope[128:256]
        return 0

    lax.fori_loop(0, 10, lift, 0)

    def clear(ref, first_x, last_x, first_y, last_y):
        @pl.when(g == 0)
        def _():
            for x in first_x:
                ref[x] = jnp.zeros(ref.shape[1:], BF16)

        @pl.when(g == 1)
        def _():
            for x in last_x:
                ref[x] = jnp.zeros(ref.shape[1:], BF16)

        def wipe(rows):
            def body(x, _):
                ref[x, rows, :] = jnp.zeros((rows.size, 128), BF16)
                return 0
            lax.fori_loop(0, ref.shape[0], body, 0)

        @pl.when(s == 0)
        def _():
            wipe(first_y)

        @pl.when(s == 127)
        def _():
            wipe(last_y)

    clear(lifted, (0, 1), (18, 19), pl.ds(0, 128), pl.ds(256, 128))

    bias2 = jnp.broadcast_to(b_mix[...], (64, 128))
    bias_out = jnp.broadcast_to(b_out[...], (16, 128))
    total[...] = jnp.zeros_like(total)
    total_lift[...] = jnp.zeros_like(total_lift)
    total_out[...] = jnp.zeros_like(total_out)
    sums[...] = jnp.zeros_like(sums)

    def gathered(parts):
        return parts[:64] , parts[64:128], parts[128:]

    def summed_z(u):
        before, here, after = gathered(u)
        return roll_z(before, 1) + here + roll_z(after, -1)

    def mix(x, _):
        pieces = [lifted[x + ox] for ox in range(3)]
        seen = jnp.concatenate(
            [
                jnp.concatenate([piece[64 * y : 64 * y + 192] for piece in pieces], axis=0)
                for y in range(4)
            ],
            axis=1,
        )
        u = jnp.dot(w_mix[...], seen, preferred_element_type=F32)
        values, slopes = [], []
        for y in range(4):
            value, slope = gelu_parts(summed_z(u[:, 128 * y : 128 * y + 128]) + bias2)
            values.append(value.astype(BF16))
            slopes.append(slope)
        mixed = jnp.concatenate(values, axis=0)
        slope = jnp.concatenate(slopes, axis=0)
        predicted = jnp.dot(w_out[...], mixed, preferred_element_type=F32) + bias_out
        goal = tgt[pl.ds(pl.multiple_of((x0 + x) * 8, 8), 8), :]
        goal = jnp.concatenate([goal, jnp.zeros((8, 128), F32)], axis=0)
        error = (loss_scale * (predicted - goal)).astype(BF16)
        back = jnp.dot(w_outt[...], error, preferred_element_type=F32)
        cot[x] = (back * slope).astype(BF16)
        own = (x >= 1) & (x <= 16)
        error = jnp.where(own, error.astype(F32), 0.0)
        sums[pl.ds(0, 16), :] += error
        total_out[...] += rows_dot(mixed[64:192], error.astype(BF16))
        return 0

    lax.fori_loop(0, 18, mix, 0)
    clear(cot, (0,), (17,), pl.ds(0, 64), pl.ds(192, 64))

    def grads(x, _):
        near = [lifted[x + 1 + ox] for ox in range(3)]
        mine = cot[x + 1, pl.ds(64, 128), :].astype(F32)
        sums[pl.ds(16, 128), :] += mine
        before = roll_z(mine, -1).astype(BF16)
        after = roll_z(mine, 1).astype(BF16)
        here = cot[x + 1, pl.ds(64, 128), :]
        seen = jnp.concatenate(
            [
                jnp.concatenate([piece[64 * y + 64 : 64 * y + 256] for piece in near], axis=0)
                for y in range(2)
            ],
            axis=1,
        )
        theirs = jnp.concatenate(
            [
                jnp.concatenate([part[64 * y : 64 * y + 64] for part in (before, here, after)], axis=0)
                for y in range(2)
            ],
            axis=1,
        )
        total[...] += rows_dot(seen, theirs)
        pieces = [cot[x + ox] for ox in range(3)]
        seen = jnp.concatenate(
            [
                jnp.concatenate([piece[64 * y : 64 * y + 192] for piece in pieces], axis=0)
                for y in range(2)
            ],
            axis=1,
        )
        u = jnp.dot(w_back[...], seen, preferred_element_type=F32)
        back = jnp.concatenate([summed_z(u[:, :128]), summed_z(u[:, 128:])], axis=0)
        down = (back * slope1[x + 2]).astype(BF16)
        sums[pl.ds(144, 128), :] += down.astype(F32)
        total_lift[...] += rows_dot(down, v3[pl.ds(x + 2, 3)].reshape(144, 128))
        return 0

    lax.fori_loop(0, 16, grads, 0)

    packed[pl.ds(0, 576), :] = total[:, 0:128]
    packed[pl.ds(576, 288), :] = jnp.concatenate(
        [total[pl.ds(0, 288), 128:192], total[pl.ds(288, 288), 128:192]], axis=1
    )
    lift_grad = jnp.zeros((64, 128), F32)
    for y in range(2):
        lift_grad += jnp.dot(
            total_lift[pl.ds(64 * y, 64), :], pick[y],
            preferred_element_type=F32, precision=lax.Precision.HIGHEST,
        )
    def row_sum(first):
        both = sums[pl.ds(first, 64), :] + sums[pl.ds(first + 64, 64), :]
        return jnp.sum(both, axis=1, keepdims=True)

    lane = lax.broadcasted_iota(jnp.int32, (64, 128), 1)
    small = lift_grad
    small = jnp.where(lane == 54, row_sum(144), small)
    small = jnp.where(lane == 55, row_sum(16), small)
    for k in range(2):
        piece = total_out[pl.ds(0, 64), 2 + k : 3 + k] + total_out[pl.ds(64, 64), 4 + k : 5 + k]
        small = jnp.where(lane == 56 + k, piece, small)
    per_row = jnp.sum(sums[pl.ds(0, 8), :], axis=1, keepdims=True)
    pair = per_row[2:4] + per_row[4:6]
    row = lax.broadcasted_iota(jnp.int32, (64, 128), 0)
    for k in range(2):
        small = jnp.where((lane == 58) & (row == k), pair[k : k + 1], small)
    packed[pl.ds(864, 32), :] = jnp.concatenate([small[:32, :64], small[32:, :64]], axis=1)


def local_grads(loss_scale, net, tgt, weights):
    return pl.pallas_call(
        functools.partial(net_kernel, loss_scale),
        out_shape=jax.ShapeDtypeStruct((896, 128), F32),
        in_specs=[VMEM] * (2 + len(weights)),
        out_specs=VMEM,
        scratch_shapes=[
            pltpu.VMEM((22, 48, 128), BF16),
            pltpu.VMEM((20, 384, 128), BF16),
            pltpu.VMEM((20, 128, 128), F32),
            pltpu.VMEM((18, 256, 128), BF16),
            pltpu.VMEM((576, 192), F32),
            pltpu.VMEM((128, 144), F32),
            pltpu.VMEM((128, 16), F32),
            pltpu.VMEM((272, 128), F32),
        ],
        compiler_params=pltpu.CompilerParams(vmem_limit_bytes=VMEM_BYTES),
        name="network",
    )(net, tgt, *weights)


def picks():
    grad = np.zeros((2, 144, 128), np.float32)
    ahead = np.zeros((6, 54, 144), np.float32)
    for ox in range(3):
        for oz in range(3):
            for ch in range(2):
                for oy in range(3):
                    tap = 27 * ch + 9 * ox + 3 * oy + oz
                    for y in range(2):
                        grad[y, ((ox * 3 + oz) * 2 + ch) * 8 + 2 + y + oy, tap] = 1
                    for y in range(6):
                        ahead[y, tap, ((ox * 3 + oz) * 2 + ch) * 8 + y + oy] = 1
    return grad, ahead


def layouts(w_lift, b_lift, w_mix, b_mix, w_out, b_out):
    grad, ahead = picks()
    lift = jnp.einsum("oj,yjc->yoc", w_lift, jnp.asarray(ahead, BF16)).reshape(384, 144)
    taps = w_mix.reshape(64, 64, 9, 3)
    mix = taps.transpose(3, 0, 2, 1).reshape(192, 576)
    back = taps[:, :, ::-1, ::-1].transpose(3, 1, 2, 0).reshape(192, 576)
    out = jnp.zeros((16, 256), BF16)
    for y in range(4):
        out = lax.dynamic_update_slice(out, w_out, (2 * y, 64 * y))
    bias = jnp.tile(b_out, 8)[:, None]
    return (
        lift, b_lift[:, None], mix, back, b_mix[:, None], out, out.T, bias, jnp.asarray(grad),
    )


def total_kernel(buf, out, from_core, mine, from_plane, from_z, s1, r1, s2, r2, s3, r3, s4, r4, s5, r5):
    y_lo = lax.axis_index("grp")
    gx = lax.axis_index("gx")
    gy = lax.axis_index("gy")
    z, x = gx // 4, gx % 4
    y_hi, core = gy // 2, gy % 2
    place = x * 4 + y_hi * 2 + y_lo
    sibling = (y_lo, gx, y_hi * 2 + 1 - core)

    def in_plane(other):
        return (other % 2, z * 4 + other // 4, ((other // 2) % 2) * 2 + core)

    def in_z(other):
        return (y_lo, other * 4 + x, gy)

    barrier = pltpu.get_barrier_semaphore()
    pl.semaphore_signal(barrier, inc=1, device_id=sibling, device_id_type=MESH)

    def greet_plane(j, _):
        pl.semaphore_signal(barrier, inc=1, device_id=in_plane((place + j) % 16), device_id_type=MESH)
        return 0

    def greet_z(j, _):
        pl.semaphore_signal(barrier, inc=1, device_id=in_z((z + j) % 8), device_id_type=MESH)
        return 0

    lax.fori_loop(1, 16, greet_plane, 0)
    lax.fori_loop(1, 8, greet_z, 0)
    pl.semaphore_wait(barrier, 23)

    theirs = pl.multiple_of((1 - core) * 16, 16)
    ours = pl.multiple_of(core * 16, 16)
    swap = pltpu.make_async_remote_copy(
        buf.at[pl.ds(theirs, 16)], from_core, s1, r1, device_id=sibling, device_id_type=MESH
    )
    swap.start()
    swap.wait()

    def add_core(j, _):
        mine[j] = buf[ours + j] + from_core[j]
        return 0

    lax.fori_loop(0, 16, add_core, 0)

    def to_plane(j):
        other = (place + j) % 16
        return pltpu.make_async_remote_copy(
            mine.at[other], from_plane.at[place], s2.at[other], r2.at[place],
            device_id=in_plane(other), device_id_type=MESH,
        )

    def of_plane(j):
        other = (place + j) % 16
        return pltpu.make_async_remote_copy(
            mine.at[other], from_plane.at[other], s2.at[other], r2.at[other],
            device_id=in_plane(other), device_id_type=MESH,
        )

    lax.fori_loop(1, 16, lambda j, _: (to_plane(j).start(), 0)[1], 0)
    from_plane[place] = mine[place]

    def wait_plane(j, _):
        of_plane(j).wait()
        return 0

    lax.fori_loop(1, 16, wait_plane, 0)
    total = from_plane[0]
    for j in range(1, 16):
        total = total + from_plane[j]
    from_z[z] = total

    def to_z(j):
        other = (z + j) % 8
        return pltpu.make_async_remote_copy(
            from_z.at[z], from_z.at[z], s3.at[other], r3.at[z], device_id=in_z(other), device_id_type=MESH
        )

    def of_z(j):
        other = (z + j) % 8
        return pltpu.make_async_remote_copy(
            from_z.at[other], from_z.at[other], s3.at[other], r3.at[other], device_id=in_z(other), device_id_type=MESH
        )

    lax.fori_loop(1, 8, lambda j, _: (to_z(j).start(), 0)[1], 0)

    def wait_z(j, _):
        of_z(j).wait()
        return 0

    lax.fori_loop(1, 8, wait_z, 0)
    total = from_z[0]
    for j in range(1, 8):
        total = total + from_z[j]
    out[ours + place] = total

    def gather(j):
        other = (place + j) % 16
        return pltpu.make_async_remote_copy(
            out.at[ours + place], out.at[ours + place], s4.at[other], r4.at[place],
            device_id=in_plane(other), device_id_type=MESH,
        )

    def gathered(j):
        other = (place + j) % 16
        return pltpu.make_async_remote_copy(
            out.at[ours + other], out.at[ours + other], s4.at[other], r4.at[other],
            device_id=in_plane(other), device_id_type=MESH,
        )

    def hand(j):
        other = (place + j) % 16
        return pltpu.make_async_remote_copy(
            out.at[ours + other], out.at[ours + other], s5.at[other], r5.at[other],
            device_id=sibling, device_id_type=MESH,
        )

    def handed(j):
        other = (place + j) % 16
        return pltpu.make_async_remote_copy(
            out.at[theirs + other], out.at[theirs + other], s5.at[other], r5.at[other],
            device_id=sibling, device_id_type=MESH,
        )

    lax.fori_loop(1, 16, lambda j, _: (gather(j).start(), 0)[1], 0)
    hand(0).start()

    def pass_on(j, _):
        gathered(j).wait_recv()
        hand(j).start()
        return 0

    lax.fori_loop(1, 16, pass_on, 0)

    def finish(j, _):
        handed(j).wait_recv()
        hand(j).wait_send()
        return 0

    lax.fori_loop(0, 16, finish, 0)
    lax.fori_loop(1, 16, lambda j, _: (gather(j).wait_send(), 0)[1], 0)


def all_total(buf):
    chunk = buf.shape[1:]
    dma = pltpu.SemaphoreType.DMA
    vmem = pl.BlockSpec(memory_space=pltpu.VMEM)
    return pl.pallas_call(
        total_kernel,
        out_shape=jax.ShapeDtypeStruct(buf.shape, jnp.float32),
        in_specs=[vmem],
        out_specs=vmem,
        scratch_shapes=[
            pltpu.VMEM((16,) + chunk, jnp.float32),
            pltpu.VMEM((16,) + chunk, jnp.float32),
            pltpu.VMEM((16,) + chunk, jnp.float32),
            pltpu.VMEM((8,) + chunk, jnp.float32),
            dma, dma, dma((16,)), dma((16,)), dma((8,)), dma((8,)),
            dma((16,)), dma((16,)), dma((16,)), dma((16,)),
        ],
        compiler_params=pltpu.CompilerParams(collective_id=1, has_side_effects=True, vmem_limit_bytes=40 * 2**20),
        name="total",
    )(buf)


def on_device(scalars, velocity, w_lift, b_lift, w_mix, b_mix, w_out, b_out):
    total_cells = scalars.size * lax.axis_size("gx") * lax.axis_size("gy")
    loss_scale = 2.0 / math.sqrt(total_cells)
    advanced, net, target = solve(scalars.reshape(64, 128), velocity.reshape(192, 128))
    weights = layouts(w_lift, b_lift, w_mix, b_mix, w_out, b_out)
    packed = local_grads(loss_scale, net, target, weights)
    summed = all_total(packed.reshape(32, 7, 4, 128)).reshape(896, 128)
    first = summed[:576].reshape(9, 64, 2, 64)
    last = summed[576:864].reshape(288, 2, 64).transpose(1, 0, 2).reshape(9, 64, 1, 64)
    mix_grad = jnp.concatenate([first, last], axis=2).transpose(3, 1, 0, 2).reshape(64, 1728)
    small = summed[864:].reshape(32, 2, 64).transpose(1, 0, 2).reshape(64, 64)
    return (
        advanced.reshape(scalars.shape),
        small[:, :54],
        small[:, 54],
        mix_grad,
        small[:, 55],
        small[:, 56:58].T,
        small[:2, 58],
    )


def solution(mesh):
    cells = P("grp", None, ("gx", "gy"), None)
    in_specs = (cells, P(None, None, ("gx", "gy"), None)) + (P(),) * 6
    out_specs = (cells,) + (P(),) * 6
    return jax.shard_map(
        on_device, mesh=mesh, in_specs=in_specs, out_specs=out_specs, check_vma=False
    )
```

```python
import functools
import math

import jax
import jax.numpy as jnp
import numpy as np
from jax import lax
from jax.experimental import pallas as pl
from jax.experimental.pallas import tpu as pltpu
from jax.sharding import PartitionSpec as P

MESH = pl.DeviceIdType.MESH
F32 = jnp.float32
BF16 = jnp.bfloat16
VMEM = pl.BlockSpec(memory_space=pltpu.VMEM)
VMEM_BYTES = 62 * 2**20


def place():
    return lax.axis_index("grp"), lax.axis_index("gx") * 4 + lax.axis_index("gy")


def roll_z(value, step):
    lane = lax.broadcasted_iota(jnp.int32, value.shape, value.ndim - 1)
    edge = 0 if step > 0 else 127
    return jnp.where(lane % 128 == edge, 0.0, pltpu.roll(value, step % 128, value.ndim - 1))


def solver(
    ring, prepare_mix, prepare_lift, prepare_back,
    sc, vel, adv, net, tgt,
    halo, held, wide, seen, inc, gains,
    a_send, a_recv, b_send, b_recv, n_send, n_recv, c_send, c_recv,
):
    g, s = place()
    diffusivity = jnp.where(g == 0, jnp.float32(0.08), jnp.float32(0.12))

    def device(step, field):
        other = lax.rem(s + step + 128, 128)
        return (field, other // 4, lax.rem(other, 4))

    partners = [(d, f) for d in (-2, -1, 0, 1, 2) for f in (0, 1) if (d, f) != (0, 0)]
    def partner(d, f):
        return device(d, g if f == 0 else 1 - g)

    barrier = pltpu.get_barrier_semaphore()
    for d, f in partners:
        pl.semaphore_signal(barrier, inc=1, device_id=partner(d, f), device_id_type=MESH)
    ring.greet(barrier)
    prepare_mix()
    pl.semaphore_wait(barrier, len(partners) + 23)

    def send(src, dst, ssem, rsem, d, f):
        return pltpu.make_async_remote_copy(
            src, dst, ssem, rsem, device_id=partner(d, f), device_id_type=MESH
        )

    first = [
        send(sc, halo.at[0], a_send.at[0], a_recv.at[0], 1, 0),
        send(sc, halo.at[1], a_send.at[1], a_recv.at[1], -1, 0),
    ]
    for copy in first:
        copy.start()

    speed = [[vel[pl.ds(64 * d + y, 32, stride=2), :] for y in range(2)] for d in range(3)]
    row = lax.broadcasted_iota(jnp.int32, (32, 128), 0)

    def step(centre, below, above, y):
        plus_x = jnp.where(row == 31, 0.0, pltpu.roll(centre, 31, 0))
        minus_x = jnp.where(row == 0, 0.0, pltpu.roll(centre, 1, 0))
        plus_z = roll_z(centre, -1)
        minus_z = roll_z(centre, 1)
        laplace = plus_x + minus_x + above + below + plus_z + minus_z - 6.0 * centre
        advect = (
            speed[0][y] * (plus_x - minus_x)
            + speed[1][y] * (above - below)
            + speed[2][y] * (plus_z - minus_z)
        )
        return centre + diffusivity * laplace - 0.5 * advect

    prepare_lift()
    own = [sc[pl.ds(y, 32, stride=2), :] for y in range(2)]
    for copy in first:
        copy.wait_recv()
    below = jnp.where(s == 0, 0.0, halo[0, pl.ds(1, 32, stride=2), :])
    above = jnp.where(s == 127, 0.0, halo[1, pl.ds(0, 32, stride=2), :])
    stepped = [step(own[0], below, own[1], 0), step(own[1], own[0], above, 1)]
    for y in range(2):
        held[y] = stepped[y]
        wide[y] = stepped[y].astype(BF16)

    second = [
        send(held.at[1], gains.at[0], b_send.at[0], b_recv.at[0], 1, 0),
        send(held.at[0], gains.at[1], b_send.at[1], b_recv.at[1], -1, 0),
    ]
    third = []
    for index, (d, f) in enumerate(partners):
        field = g
        if abs(d) == 2:
            y = 1 if d > 0 else 0
            src, dst = wide.at[y], seen.at[2 - d, field, y]
        else:
            src, dst = wide, seen.at[2 - d, field]
        third.append(send(src, dst, n_send.at[index], n_recv.at[index], d, f))
    arrivals = []
    for index, (d, f) in enumerate(partners):
        field = g if f == 0 else 1 - g
        if abs(d) == 2:
            y = 1 if d > 0 else 0
            src, dst = wide.at[y], seen.at[2 - d, field, y]
        else:
            src, dst = wide, seen.at[2 - d, field]
        arrivals.append(send(src, dst, n_send.at[index], n_recv.at[index], d, f))
    for copy in second:
        copy.start()
    for copy in third:
        copy.start()
    for y in range(2):
        seen[2, g, y] = wide[y]
    net[pl.ds(0, 48), :] = jnp.zeros((48, 128), F32)
    net[pl.ds(35 * 16, 48), :] = jnp.zeros((48, 128), F32)
    tgt[pl.ds(0, 8), :] = jnp.zeros((8, 128), F32)
    tgt[pl.ds(33 * 8, 8), :] = jnp.zeros((8, 128), F32)

    prepare_back()
    for copy in second:
        copy.wait_recv()
    below = jnp.where(s == 0, 0.0, gains[0])
    above = jnp.where(s == 127, 0.0, gains[1])
    advanced = [
        step(stepped[0], below, stepped[1], 0),
        step(stepped[1], stepped[0], above, 1),
    ]
    for y in range(2):
        adv[pl.ds(y, 32, stride=2), :] = advanced[y]
        inc[g, 1 + y] = advanced[y] - stepped[y]
    fourth, landings = [], []
    for index, (d, f) in enumerate([(0, 1), (1, 0), (1, 1), (-1, 0), (-1, 1)]):
        def ends(field):
            if d == 0:
                return inc.at[g, pl.ds(1, 2)], inc.at[field, pl.ds(1, 2)]
            if d == 1:
                return inc.at[g, 2], inc.at[field, 0]
            return inc.at[g, 1], inc.at[field, 3]
        fourth.append(send(*ends(g), c_send.at[index], c_recv.at[index], d, f))
        landings.append(
            send(*ends(g if f == 0 else 1 - g), c_send.at[index], c_recv.at[index], d, f)
        )
    for copy in fourth:
        copy.start()

    for copy in arrivals:
        copy.wait_recv()
    for field in range(2):
        for yy in range(8):
            slab, y = (yy + 1) // 2, (yy + 1) % 2
            y_at = 2 * s - 3 + yy
            inside = (y_at >= 0) & (y_at < 256)
            value = jnp.where(inside, seen[slab, field, y].astype(F32), 0.0)
            net[pl.ds(48 + field * 8 + yy, 32, stride=16), :] = value
    for copy in landings:
        copy.wait_recv()
    for field in range(2):
        for yy in range(4):
            tgt[pl.ds(8 + yy * 2 + field, 32, stride=8), :] = inc[field, yy]
    return first + second + third + fourth


def gelu_parts(v):
    c = math.sqrt(2.0 / math.pi)
    square = v * v
    t = jnp.tanh(v * (c + (c * 0.044715) * square))
    half = 0.5 + 0.5 * t
    value = v * half
    slope = half + (0.5 * v) * (1.0 - t * t) * (c + (3.0 * c * 0.044715) * square)
    return value, slope


def rows_dot(a, b):
    return lax.dot_general(a, b, (((1,), (1,)), ((), ())), preferred_element_type=F32)


class Prepared:
    def __init__(self, w_lift, b_lift, w_mix, b_mix, w_out, b_out, ahead, spread, lift, mix, back, out, outt, bias):
        self.__dict__.update(locals())

    def mix_form(self):
        wide = jnp.concatenate([self.w_mix[...].astype(F32), jnp.zeros((64, 64), F32)], axis=1)
        turned = [wide] + [pltpu.roll(wide, 1792 - oz, 1) for oz in (1, 2)]
        turned = jnp.concatenate([t[:, :1728] for t in turned], axis=0).astype(BF16)
        self.mix[...] = jnp.dot(turned, self.spread[...], preferred_element_type=F32).astype(BF16)

    def lift_form(self):
        flat = self.w_lift[...].astype(F32).T.astype(BF16)
        for y in range(6):
            band = jnp.dot(flat, self.ahead[y], preferred_element_type=F32)
            self.lift[pl.ds(64 * y, 64), :] = band.astype(BF16)
        for index, ref in enumerate((self.b_lift, self.b_mix)):
            self.bias[index] = jnp.broadcast_to(ref[...], (128, 64)).T
        four = jnp.concatenate([self.w_out[...].astype(F32)] * 4, axis=1)
        row = lax.broadcasted_iota(jnp.int32, (16, 256), 0)
        lane = lax.broadcasted_iota(jnp.int32, (16, 256), 1)
        both = jnp.where(row % 2 == 0, four[0:1], four[1:2])
        both = jnp.where(row // 2 == lane // 64, both, 0.0)
        self.out[...] = both.astype(BF16)
        self.outt[...] = both.T.astype(BF16)

    def back_form(self):
        flat = self.mix[...].astype(F32).T
        for oz in range(3):
            tiles = [flat[64 * m : 64 * m + 64, 64 * oz : 64 * oz + 64] for m in range(8, -1, -1)]
            self.back[pl.ds(64 * (2 - oz), 64), :] = jnp.concatenate(tiles, axis=1).astype(BF16)

def network(loss_scale, net, tgt, prepared, unspread_ref, pick, v3, lifted, slope1, mixed, slope2, cot, down, errors, total, buf):
    g, s = place()
    x0 = g * 16

    def fill(x, _):
        rows = net[pl.ds(pl.multiple_of((x0 + x) * 16, 16), 16), :]
        v3[x, pl.ds(0, 16), :] = roll_z(rows, 1).astype(BF16)
        v3[x, pl.ds(16, 16), :] = rows.astype(BF16)
        v3[x, pl.ds(32, 16), :] = roll_z(rows, -1).astype(BF16)
        return 0

    lax.fori_loop(0, 22, fill, 0, unroll=11)

    def lift(x, _):
        seen = jnp.concatenate(
            [v3[pl.ds(2 * x, 3)].reshape(144, 128), v3[pl.ds(2 * x + 1, 3)].reshape(144, 128)], axis=1
        )
        pre = jnp.dot(prepared.lift[...], seen, preferred_element_type=F32)
        bias = jnp.concatenate([prepared.bias[0]] * 6, axis=0)
        for half in range(2):
            value, slope = gelu_parts(pre[:, half * 128 : half * 128 + 128] + bias)
            lifted[2 * x + half] = value.astype(BF16)
            slope1[2 * x + half] = slope[128:256]
        return 0

    lax.fori_loop(0, 10, lift, 0, unroll=5)

    def clear(ref, first_x, last_x, first_y, last_y):
        @pl.when(g == 0)
        def _():
            for x in first_x:
                ref[x] = jnp.zeros(ref.shape[1:], BF16)

        @pl.when(g == 1)
        def _():
            for x in last_x:
                ref[x] = jnp.zeros(ref.shape[1:], BF16)

        def wipe(rows):
            def body(x, _):
                ref[x, rows, :] = jnp.zeros((rows.size, 128), BF16)
                return 0
            lax.fori_loop(0, ref.shape[0], body, 0)

        @pl.when(s == 0)
        def _():
            wipe(first_y)

        @pl.when(s == 127)
        def _():
            wipe(last_y)

    clear(lifted, (0, 1), (18, 19), pl.ds(0, 128), pl.ds(256, 128))

    def summed_z(u):
        return roll_z(u[:64], 1) + u[64:128] + roll_z(u[128:], -1)

    def around(ref, x, first, rows):
        pieces = [ref[x + ox] for ox in range(3)]
        return jnp.concatenate(
            [
                jnp.concatenate([piece[64 * y : 64 * y + 192] for piece in pieces], axis=0)
                for y in range(first, first + rows)
            ],
            axis=1,
        )

    def mix(x, _):
        u = jnp.dot(prepared.mix[...], around(lifted, x, 0, 4), preferred_element_type=F32)
        for y in range(4):
            value, slope = gelu_parts(summed_z(u[:, 128 * y : 128 * y + 128]) + prepared.bias[1])
            mixed[x, pl.ds(64 * y, 64), :] = value.astype(BF16)
            slope2[x, pl.ds(64 * y, 64), :] = slope
        return 0

    lax.fori_loop(0, 18, mix, 0, unroll=3)

    def compare(batch, _):
        first = 6 * batch
        seen = jnp.concatenate([mixed[first + j] for j in range(6)], axis=1)
        row = lax.broadcasted_iota(jnp.int32, (16, 768), 0)
        bias = jnp.where(row % 2 == 0, prepared.b_out[:, 0:1], prepared.b_out[:, 1:2])
        predicted = jnp.dot(prepared.out[...], seen, preferred_element_type=F32) + bias
        goal = jnp.concatenate(
            [tgt[pl.ds(pl.multiple_of((x0 + first + j) * 8, 8), 8), :] for j in range(6)], axis=1
        )
        goal = jnp.concatenate([goal, jnp.zeros((8, 768), F32)], axis=0)
        error = (loss_scale * (predicted - goal)).astype(BF16)
        back = jnp.dot(prepared.outt[...], error, preferred_element_type=F32)
        for j in range(6):
            cot[first + j] = (back[:, 128 * j : 128 * j + 128] * slope2[first + j]).astype(BF16)
            errors[first + j] = error[:, 128 * j : 128 * j + 128]
        return 0

    lax.fori_loop(0, 3, compare, 0)
    clear(cot, (0,), (17,), pl.ds(0, 64), pl.ds(192, 64))
    total[...] = jnp.zeros_like(total)

    def mix_grad(x, mixbias):
        here = cot[x + 1, pl.ds(64, 128), :]
        mine = here.astype(F32)
        before = roll_z(mine, -1).astype(BF16)
        after = roll_z(mine, 1).astype(BF16)
        seen = around(lifted, x + 1, 1, 2)
        theirs = jnp.concatenate(
            [
                jnp.concatenate([part[64 * y : 64 * y + 64] for part in (before, here, after)], axis=0)
                for y in range(2)
            ],
            axis=1,
        )
        total[...] += rows_dot(seen, theirs)
        u = jnp.dot(prepared.back[...], around(cot, x, 0, 2), preferred_element_type=F32)
        back = jnp.concatenate([summed_z(u[:, :128]), summed_z(u[:, 128:])], axis=0)
        down[x] = (back * slope1[x + 2]).astype(BF16)
        return mixbias + mine[:64] + mine[64:]

    mixbias = lax.fori_loop(0, 16, mix_grad, jnp.zeros((64, 128), F32), unroll=4)

    liftbias = jnp.zeros((64, 128), F32)
    outbias = jnp.zeros((8, 128), F32)
    lift_total = jnp.zeros((128, 144), F32)
    out_total = jnp.zeros((128, 16), F32)
    for batch in range(4):
        xs = range(4 * batch, 4 * batch + 4)
        lows = [down[x] for x in xs]
        for low in lows:
            low = low.astype(F32)
            liftbias = liftbias + low[:64] + low[64:]
        ins = jnp.concatenate([v3[x + 2 : x + 5].reshape(144, 128) for x in xs], axis=1)
        lift_total += rows_dot(jnp.concatenate(lows, axis=1), ins)
        errs = [errors[x + 1] for x in xs]
        for err in errs:
            outbias = outbias + err.astype(F32)[:8]
        out_total += rows_dot(
            jnp.concatenate([mixed[x + 1, pl.ds(64, 128), :] for x in xs], axis=1),
            jnp.concatenate(errs, axis=1),
        )

    flat = total[...].T
    high = flat.astype(BF16)
    low = (flat - high.astype(F32)).astype(BF16)
    placed = jnp.dot(jnp.concatenate([high, low], axis=0), unspread_ref[...], preferred_element_type=F32)
    placed = placed[:192] + placed[192:]
    full = placed[:64] + pltpu.roll(placed[64:128], 1, 1) + pltpu.roll(placed[128:], 2, 1)

    small = jnp.zeros((64, 128), F32)
    for y in range(2):
        small += jnp.dot(
            lift_total[64 * y : 64 * y + 64], pick[y],
            preferred_element_type=F32, precision=lax.Precision.HIGHEST,
        )
    lane = lax.broadcasted_iota(jnp.int32, (64, 128), 1)
    row = lax.broadcasted_iota(jnp.int32, (64, 128), 0)
    small = jnp.where(lane == 118, jnp.sum(liftbias, axis=1, keepdims=True), small)
    small = jnp.where(lane == 119, jnp.sum(mixbias, axis=1, keepdims=True), small)
    for k in range(2):
        piece = out_total[:64, 2 + k : 3 + k] + out_total[64:, 4 + k : 5 + k]
        small = jnp.where(lane == 120 + k, piece, small)
    per_row = jnp.sum(outbias, axis=1, keepdims=True)
    pair = per_row[2:4] + per_row[4:6]
    for k in range(2):
        small = jnp.where((lane == 122) & (row == k), pair[k : k + 1], small)
    full = jnp.concatenate([full[:, :1664], full[:, 1664:] + small], axis=1)
    for c in range(32):
        at, half = 4 * (c // 2), 896 * (c % 2)
        buf[c] = full[at : at + 4, half : half + 896]

class Ring:
    def __init__(self):
        y_lo = lax.axis_index("grp")
        gx = lax.axis_index("gx")
        gy = lax.axis_index("gy")
        self.z, self.x = gx // 4, gx % 4
        self.y_hi, self.core = gy // 2, gy % 2
        self.y_lo, self.gx, self.gy = y_lo, gx, gy
        self.place = self.x * 4 + self.y_hi * 2 + y_lo
        self.sibling = (y_lo, gx, self.y_hi * 2 + 1 - self.core)

    def in_plane(self, other):
        return (other % 2, self.z * 4 + other // 4, ((other // 2) % 2) * 2 + self.core)

    def in_z(self, other):
        return (self.y_lo, other * 4 + self.x, self.gy)

    def greet(self, barrier):
        pl.semaphore_signal(barrier, inc=1, device_id=self.sibling, device_id_type=MESH)

        def greet_plane(j, _):
            other = self.in_plane((self.place + j) % 16)
            pl.semaphore_signal(barrier, inc=1, device_id=other, device_id_type=MESH)
            return 0

        def greet_z(j, _):
            other = self.in_z((self.z + j) % 8)
            pl.semaphore_signal(barrier, inc=1, device_id=other, device_id_type=MESH)
            return 0

        lax.fori_loop(1, 16, greet_plane, 0)
        lax.fori_loop(1, 8, greet_z, 0)


def all_sum(ring, buf, out, from_core, mine, from_plane, from_z, s1, r1, s2, r2, s3, r3, s4, r4, s5, r5):
    place, z, core, sibling = ring.place, ring.z, ring.core, ring.sibling
    in_plane, in_z = ring.in_plane, ring.in_z
    theirs = pl.multiple_of((1 - core) * 16, 16)
    ours = pl.multiple_of(core * 16, 16)
    swap = pltpu.make_async_remote_copy(
        buf.at[pl.ds(theirs, 16)], from_core, s1, r1, device_id=sibling, device_id_type=MESH
    )
    swap.start()
    swap.wait()

    def add_core(j, _):
        mine[j] = buf[ours + j] + from_core[j]
        return 0

    lax.fori_loop(0, 16, add_core, 0)

    def to_plane(j):
        other = (place + j) % 16
        return pltpu.make_async_remote_copy(
            mine.at[other], from_plane.at[place], s2.at[other], r2.at[place],
            device_id=in_plane(other), device_id_type=MESH,
        )

    def of_plane(j):
        other = (place + j) % 16
        return pltpu.make_async_remote_copy(
            mine.at[other], from_plane.at[other], s2.at[other], r2.at[other],
            device_id=in_plane(other), device_id_type=MESH,
        )

    lax.fori_loop(1, 16, lambda j, _: (to_plane(j).start(), 0)[1], 0)
    from_plane[place] = mine[place]

    def wait_plane(j, _):
        of_plane(j).wait()
        return 0

    lax.fori_loop(1, 16, wait_plane, 0)
    total = from_plane[0]
    for j in range(1, 16):
        total = total + from_plane[j]
    from_z[z] = total

    def to_z(j):
        other = (z + j) % 8
        return pltpu.make_async_remote_copy(
            from_z.at[z], from_z.at[z], s3.at[other], r3.at[z], device_id=in_z(other), device_id_type=MESH
        )

    def of_z(j):
        other = (z + j) % 8
        return pltpu.make_async_remote_copy(
            from_z.at[other], from_z.at[other], s3.at[other], r3.at[other], device_id=in_z(other), device_id_type=MESH
        )

    lax.fori_loop(1, 8, lambda j, _: (to_z(j).start(), 0)[1], 0)

    def wait_z(j, _):
        of_z(j).wait()
        return 0

    lax.fori_loop(1, 8, wait_z, 0)
    total = from_z[0]
    for j in range(1, 8):
        total = total + from_z[j]
    out[ours + place] = total

    def gather(j):
        other = (place + j) % 16
        return pltpu.make_async_remote_copy(
            out.at[ours + place], out.at[ours + place], s4.at[other], r4.at[place],
            device_id=in_plane(other), device_id_type=MESH,
        )

    def gathered(j):
        other = (place + j) % 16
        return pltpu.make_async_remote_copy(
            out.at[ours + other], out.at[ours + other], s4.at[other], r4.at[other],
            device_id=in_plane(other), device_id_type=MESH,
        )

    def hand(j):
        other = (place + j) % 16
        return pltpu.make_async_remote_copy(
            out.at[ours + other], out.at[ours + other], s5.at[other], r5.at[other],
            device_id=sibling, device_id_type=MESH,
        )

    def handed(j):
        other = (place + j) % 16
        return pltpu.make_async_remote_copy(
            out.at[theirs + other], out.at[theirs + other], s5.at[other], r5.at[other],
            device_id=sibling, device_id_type=MESH,
        )

    lax.fori_loop(1, 16, lambda j, _: (gather(j).start(), 0)[1], 0)
    hand(0).start()

    def pass_on(j, _):
        gathered(j).wait_recv()
        hand(j).start()
        return 0

    lax.fori_loop(1, 16, pass_on, 0)

    def finish(j, _):
        handed(j).wait_recv()
        hand(j).wait_send()
        return 0

    lax.fori_loop(0, 16, finish, 0)
    lax.fori_loop(1, 16, lambda j, _: (gather(j).wait_send(), 0)[1], 0)


def picks():
    grad = np.zeros((2, 144, 128), np.float32)
    ahead = np.zeros((6, 54, 144), np.float32)
    for ox in range(3):
        for oz in range(3):
            for ch in range(2):
                for oy in range(3):
                    tap = 27 * ch + 9 * ox + 3 * oy + oz
                    for y in range(2):
                        grad[y, ((ox * 3 + oz) * 2 + ch) * 8 + 2 + y + oy, 64 + tap] = 1
                    for y in range(6):
                        ahead[y, tap, ((ox * 3 + oz) * 2 + ch) * 8 + y + oy] = 1
    return grad, ahead


def main_kernel(
    loss_scale,
    sc_hbm, vel_hbm, w_mix_hbm, spread_hbm, w_lift_hbm, ahead_hbm, b_lift_hbm, b_mix_hbm, w_out_hbm, b_out_hbm,
    unspread_hbm, pick_hbm,
    adv, out,
    sc, vel, w_mix, spread, w_lift, ahead, b_lift, b_mix, w_out, b_out, unspread, pick,
    load, lift_w, mix_w, back_w, out_w, outt_w, bias,
    net, tgt, halo, held, wide, seen, inc, gains,
    v3, lifted, slope1, mixed, slope2, cot, down, errors, total, buf,
    from_core, mine, from_plane, from_z,
    a_send, a_recv, b_send, b_recv, n_send, n_recv, c_send, c_recv,
    *sums,
):
    pairs = (
        (sc_hbm, sc), (vel_hbm, vel), (w_mix_hbm, w_mix), (spread_hbm, spread), (w_lift_hbm, w_lift),
        (ahead_hbm, ahead), (b_lift_hbm, b_lift), (b_mix_hbm, b_mix), (w_out_hbm, w_out), (b_out_hbm, b_out),
        (unspread_hbm, unspread), (pick_hbm, pick),
    )
    loads = [pltpu.make_async_copy(*pair, load.at[j]) for j, pair in enumerate(pairs)]
    for copy in loads:
        copy.start()
    ring = Ring()
    prepared = Prepared(
        w_lift, b_lift, w_mix, b_mix, w_out, b_out, ahead, spread, lift_w, mix_w, back_w, out_w, outt_w, bias
    )

    def prepare_mix():
        for copy in loads[2:4]:
            copy.wait()
        prepared.mix_form()
        for copy in loads[:2]:
            copy.wait()

    def prepare_lift():
        for copy in loads[4:10]:
            copy.wait()
        prepared.lift_form()

    sent = solver(
        ring, prepare_mix, prepare_lift, prepared.back_form,
        sc, vel, adv, net, tgt, halo, held, wide, seen, inc, gains,
        a_send, a_recv, b_send, b_recv, n_send, n_recv, c_send, c_recv,
    )
    for copy in loads[10:]:
        copy.wait()
    network(
        loss_scale, net, tgt, prepared, unspread, pick,
        v3, lifted, slope1, mixed, slope2, cot, down, errors, total, buf,
    )
    for copy in sent:
        copy.wait_send()
    all_sum(ring, buf, out, from_core, mine, from_plane, from_z, *sums)


def finish_kernel(adv_in, out, adv, mix, lift, liftbias, mixbias, out_grad, outbias):
    adv[...] = adv_in[...]
    for r in range(16):
        mix[pl.ds(4 * r, 4), pl.ds(0, 896)] = out[2 * r]
        mix[pl.ds(4 * r, 4), pl.ds(896, 832)] = out[2 * r + 1][:, :832]
    last = jnp.concatenate([out[2 * r + 1][:, 768:] for r in range(16)], axis=0)
    turned = last.T
    lift[...] = turned[64:118]
    liftbias[...] = turned[118:119]
    mixbias[...] = turned[119:120]
    out_grad[...] = turned[120:122]
    outbias[...] = turned[122:123, :2]


def train(loss_scale, scalars, velocity, w_lift, b_lift, w_mix, b_mix, w_out, b_out):
    dma = pltpu.SemaphoreType.DMA
    hbm = pl.BlockSpec(memory_space=pltpu.HBM)
    pick, ahead = picks()
    spread = np.zeros((64, 9, 3, 9, 64), np.float32)
    for m in range(9):
        for i in range(64):
            spread[i, m, 0, m, i] = 1
    spread = spread.reshape(1728, 576)
    unspread = np.zeros((576, 1792), np.float32)
    unspread[:, :1728] = spread.T
    chunk = (4, 896)

    def vmem(*shape, dtype=F32):
        return pltpu.VMEM(shape, dtype)

    adv, out = pl.pallas_call(
        functools.partial(main_kernel, loss_scale),
        out_shape=(jax.ShapeDtypeStruct((64, 128), F32), jax.ShapeDtypeStruct((32,) + chunk, F32)),
        in_specs=[hbm] * 12,
        out_specs=(VMEM, VMEM),
        scratch_shapes=[
            vmem(64, 128), vmem(192, 128), vmem(64, 1728, dtype=BF16), vmem(1728, 576, dtype=BF16),
            vmem(54, 64, dtype=BF16), vmem(6, 54, 144, dtype=BF16), vmem(1, 64), vmem(1, 64),
            vmem(2, 64, dtype=BF16), vmem(1, 2), vmem(576, 1792, dtype=BF16), vmem(2, 144, 128), dma((12,)),
            vmem(384, 144, dtype=BF16), vmem(192, 576, dtype=BF16), vmem(192, 576, dtype=BF16),
            vmem(16, 256, dtype=BF16), vmem(256, 16, dtype=BF16), vmem(2, 64, 128),
            vmem(38 * 16, 128), vmem(34 * 8, 128),
            vmem(2, 64, 128), vmem(2, 32, 128), vmem(2, 32, 128, dtype=BF16),
            vmem(5, 2, 2, 32, 128, dtype=BF16), vmem(2, 4, 32, 128), vmem(2, 32, 128),
            vmem(22, 48, 128, dtype=BF16), vmem(20, 384, 128, dtype=BF16), vmem(20, 128, 128),
            vmem(18, 256, 128, dtype=BF16), vmem(18, 256, 128), vmem(18, 256, 128, dtype=BF16),
            vmem(16, 128, 128, dtype=BF16), vmem(18, 16, 128, dtype=BF16), vmem(576, 192),
            vmem(32, *chunk), vmem(16, *chunk), vmem(16, *chunk), vmem(16, *chunk), vmem(8, *chunk),
            dma((2,)), dma((2,)), dma((2,)), dma((2,)),
            dma((9,)), dma((9,)), dma((5,)), dma((5,)),
            dma, dma, dma((16,)), dma((16,)), dma((8,)), dma((8,)),
            dma((16,)), dma((16,)), dma((16,)), dma((16,)),
        ],
        compiler_params=pltpu.CompilerParams(
            collective_id=0, has_side_effects=True, vmem_limit_bytes=VMEM_BYTES
        ),
        name="train",
    )(
        scalars, velocity, w_mix, jnp.asarray(spread, BF16), w_lift.T, jnp.asarray(ahead, BF16),
        b_lift[None], b_mix[None], w_out, b_out[None], jnp.asarray(unspread, BF16), jnp.asarray(pick),
    )
    shapes = ((64, 128), (64, 1728), (54, 64), (1, 64), (1, 64), (2, 64), (1, 2))
    return pl.pallas_call(
        finish_kernel,
        out_shape=tuple(jax.ShapeDtypeStruct(shape, F32) for shape in shapes),
        in_specs=[VMEM] * 2,
        out_specs=(VMEM,) * 7,
        compiler_params=pltpu.CompilerParams(vmem_limit_bytes=8 * 2**20),
        name="finish",
    )(adv, out)


def on_device(scalars, velocity, w_lift, b_lift, w_mix, b_mix, w_out, b_out):
    total_cells = scalars.size * lax.axis_size("gx") * lax.axis_size("gy")
    loss_scale = 2.0 / math.sqrt(total_cells)
    adv, mix, lift, liftbias, mixbias, out_grad, outbias = train(
        loss_scale, scalars.reshape(64, 128), velocity.reshape(192, 128),
        w_lift, b_lift, w_mix, b_mix, w_out, b_out,
    )
    return (
        adv.reshape(scalars.shape), lift.T, liftbias[0], mix, mixbias[0], out_grad, outbias[0],
    )


def solution(mesh):
    cells = P("grp", None, ("gx", "gy"), None)
    in_specs = (cells, P(None, None, ("gx", "gy"), None)) + (P(),) * 6
    out_specs = (cells,) + (P(),) * 6
    return jax.shard_map(
        on_device, mesh=mesh, in_specs=in_specs, out_specs=out_specs, check_vma=False
    )
```

```python
import functools
import math

import jax
import jax.numpy as jnp
import numpy as np
from jax import lax
from jax.experimental import pallas as pl
from jax.experimental.pallas import tpu as pltpu
from jax.sharding import PartitionSpec as P

MESH = pl.DeviceIdType.MESH
F32 = jnp.float32
BF16 = jnp.bfloat16
VMEM = pl.BlockSpec(memory_space=pltpu.VMEM)
VMEM_BYTES = 62 * 2**20


def place():
    return lax.axis_index("grp"), lax.axis_index("gx") * 4 + lax.axis_index("gy")


def roll_z(value, step):
    lane = lax.broadcasted_iota(jnp.int32, value.shape, value.ndim - 1)
    edge = 0 if step > 0 else 127
    return jnp.where(lane % 128 == edge, 0.0, pltpu.roll(value, step % 128, value.ndim - 1))


def solver(
    ring, prepare_mix, prepare_lift, prepare_back,
    sc, vel, adv, net, tgt,
    halo, held, wide, seen, inc, gains,
    a_send, a_recv, b_send, b_recv, n_send, n_recv, c_send, c_recv,
):
    g, s = place()
    diffusivity = jnp.where(g == 0, jnp.float32(0.08), jnp.float32(0.12))

    def device(step, field):
        other = lax.rem(s + step + 128, 128)
        return (field, other // 4, lax.rem(other, 4))

    partners = [(d, f) for d in (-2, -1, 0, 1, 2) for f in (0, 1) if (d, f) != (0, 0)]
    def partner(d, f):
        return device(d, g if f == 0 else 1 - g)

    barrier = pltpu.get_barrier_semaphore()
    for d, f in partners:
        pl.semaphore_signal(barrier, inc=1, device_id=partner(d, f), device_id_type=MESH)
    ring.greet(barrier)
    prepare_mix()
    pl.semaphore_wait(barrier, len(partners) + 23)

    def send(src, dst, ssem, rsem, d, f):
        return pltpu.make_async_remote_copy(
            src, dst, ssem, rsem, device_id=partner(d, f), device_id_type=MESH
        )

    first = [
        send(sc, halo.at[0], a_send, a_recv, 1, 0),
        send(sc, halo.at[1], a_send, a_recv, -1, 0),
    ]
    first_all = send(halo, halo, a_send, a_recv, 1, 0)
    for copy in first:
        copy.start()

    speed = [[vel[pl.ds(64 * d + y, 32, stride=2), :] for y in range(2)] for d in range(3)]
    row = lax.broadcasted_iota(jnp.int32, (32, 128), 0)

    def step(centre, below, above, y):
        plus_x = jnp.where(row == 31, 0.0, pltpu.roll(centre, 31, 0))
        minus_x = jnp.where(row == 0, 0.0, pltpu.roll(centre, 1, 0))
        plus_z = roll_z(centre, -1)
        minus_z = roll_z(centre, 1)
        laplace = plus_x + minus_x + above + below + plus_z + minus_z - 6.0 * centre
        advect = (
            speed[0][y] * (plus_x - minus_x)
            + speed[1][y] * (above - below)
            + speed[2][y] * (plus_z - minus_z)
        )
        return centre + diffusivity * laplace - 0.5 * advect

    prepare_lift()
    own = [sc[pl.ds(y, 32, stride=2), :] for y in range(2)]
    first_all.wait_recv()
    below = jnp.where(s == 0, 0.0, halo[0, pl.ds(1, 32, stride=2), :])
    above = jnp.where(s == 127, 0.0, halo[1, pl.ds(0, 32, stride=2), :])
    stepped = [step(own[0], below, own[1], 0), step(own[1], own[0], above, 1)]
    for y in range(2):
        held[y] = stepped[y]
        wide[y] = stepped[y].astype(BF16)

    second = [
        send(held.at[1], gains.at[0], b_send, b_recv, 1, 0),
        send(held.at[0], gains.at[1], b_send, b_recv, -1, 0),
    ]
    second_all = send(gains, gains, b_send, b_recv, 1, 0)
    third = []
    for d, f in partners:
        slot = 2 * (2 - d) + g
        if abs(d) == 2:
            y = 1 if d > 0 else 0
            third.append(send(wide.at[y], seen.at[slot, y], n_send, n_recv, d, f))
        else:
            third.append(send(wide, seen.at[slot], n_send, n_recv, d, f))
    third_all = send(seen.at[pl.ds(0, 7)], seen.at[pl.ds(0, 7)], n_send, n_recv, 1, 0)
    for copy in second:
        copy.start()
    for copy in third:
        copy.start()
    for y in range(2):
        seen[4 + g, y] = wide[y]
    net[pl.ds(0, 48), :] = jnp.zeros((48, 128), F32)
    net[pl.ds(35 * 16, 48), :] = jnp.zeros((48, 128), F32)
    prepare_back()
    third_all.wait_recv()
    for field in range(2):
        for yy in range(8):
            slab, y = (yy + 1) // 2, (yy + 1) % 2
            y_at = 2 * s - 3 + yy
            inside = (y_at >= 0) & (y_at < 256)
            value = jnp.where(inside, seen[2 * slab + field, y].astype(F32), 0.0)
            net[pl.ds(48 + field * 8 + yy, 32, stride=16), :] = value

    def increments():
        second_all.wait_recv()
        below = jnp.where(s == 0, 0.0, gains[0])
        above = jnp.where(s == 127, 0.0, gains[1])
        advanced = [
            step(stepped[0], below, stepped[1], 0),
            step(stepped[1], stepped[0], above, 1),
        ]
        for y in range(2):
            adv[pl.ds(y, 32, stride=2), :] = advanced[y]
            inc[4 * g + 1 + y] = advanced[y] - stepped[y]
        for d, f in [(0, 1), (1, 0), (1, 1), (-1, 0), (-1, 1)]:
            if d == 0:
                part = inc.at[pl.ds(4 * g + 1, 2)]
                send(part, part, c_send, c_recv, d, f).start()
            elif d == 1:
                send(inc.at[4 * g + 2], inc.at[4 * g], c_send, c_recv, d, f).start()
            else:
                send(inc.at[4 * g + 1], inc.at[4 * g + 3], c_send, c_recv, d, f).start()

    fourth_all = send(inc.at[pl.ds(0, 6)], inc.at[pl.ds(0, 6)], c_send, c_recv, 1, 0)

    def targets():
        fourth_all.wait_recv()
        tgt[pl.ds(0, 8), :] = jnp.zeros((8, 128), F32)
        tgt[pl.ds(33 * 8, 8), :] = jnp.zeros((8, 128), F32)
        for field in range(2):
            for yy in range(4):
                tgt[pl.ds(8 + yy * 2 + field, 32, stride=8), :] = inc[4 * field + yy]

    return increments, targets, (first_all, second_all, third_all, fourth_all)


def gelu_parts(v):
    c = math.sqrt(2.0 / math.pi)
    square = v * v
    t = jnp.tanh(v * (c + (c * 0.044715) * square))
    half = 0.5 + 0.5 * t
    value = v * half
    slope = half + (0.5 * v) * (1.0 - t * t) * (c + (3.0 * c * 0.044715) * square)
    return value, slope


def rows_dot(a, b):
    return lax.dot_general(a, b, (((1,), (1,)), ((), ())), preferred_element_type=F32)


class Prepared:
    def __init__(self, w_lift, b_lift, w_mix, b_mix, w_out, b_out, ahead, spread, lift, mix, back, out, outt, bias):
        self.__dict__.update(locals())

    def mix_form(self):
        wide = jnp.concatenate([self.w_mix[...].astype(F32), jnp.zeros((64, 64), F32)], axis=1)
        turned = [wide] + [pltpu.roll(wide, 1792 - oz, 1) for oz in (1, 2)]
        turned = jnp.concatenate([t[:, :1728] for t in turned], axis=0).astype(BF16)
        self.mix[...] = jnp.dot(turned, self.spread[...], preferred_element_type=F32).astype(BF16)

    def lift_form(self):
        flat = self.w_lift[...].astype(F32).T.astype(BF16)
        for y in range(6):
            band = jnp.dot(flat, self.ahead[y], preferred_element_type=F32)
            self.lift[pl.ds(64 * y, 64), :] = band.astype(BF16)
        for index, ref in enumerate((self.b_lift, self.b_mix)):
            self.bias[index] = jnp.broadcast_to(ref[...], (128, 64)).T
        four = jnp.concatenate([self.w_out[...].astype(F32)] * 4, axis=1)
        row = lax.broadcasted_iota(jnp.int32, (16, 256), 0)
        lane = lax.broadcasted_iota(jnp.int32, (16, 256), 1)
        both = jnp.where(row % 2 == 0, four[0:1], four[1:2])
        both = jnp.where(row // 2 == lane // 64, both, 0.0)
        self.out[...] = both.astype(BF16)
        self.outt[...] = both.T.astype(BF16)

    def back_form(self):
        flat = self.mix[...].astype(F32).T
        for oz in range(3):
            tiles = [flat[64 * m : 64 * m + 64, 64 * oz : 64 * oz + 64] for m in range(8, -1, -1)]
            self.back[pl.ds(64 * (2 - oz), 64), :] = jnp.concatenate(tiles, axis=1).astype(BF16)

def network(
    loss_scale, increments, targets, summing, net, tgt, prepared, unspread_ref, pick,
    v3, lifted, slope1, mixed, slope2, cot, down, errors, total, buf, small_buf,
):
    g, s = place()
    x0 = g * 16

    def fill(x, _):
        rows = net[pl.ds(pl.multiple_of((x0 + x) * 16, 16), 16), :]
        v3[x, pl.ds(0, 16), :] = roll_z(rows, 1).astype(BF16)
        v3[x, pl.ds(16, 16), :] = rows.astype(BF16)
        v3[x, pl.ds(32, 16), :] = roll_z(rows, -1).astype(BF16)
        return 0

    lax.fori_loop(0, 22, fill, 0, unroll=11)

    def lift(x, _):
        seen = jnp.concatenate(
            [v3[pl.ds(2 * x, 3)].reshape(144, 128), v3[pl.ds(2 * x + 1, 3)].reshape(144, 128)], axis=1
        )
        pre = jnp.dot(prepared.lift[...], seen, preferred_element_type=F32)
        bias = jnp.concatenate([prepared.bias[0]] * 6, axis=0)
        for half in range(2):
            value, slope = gelu_parts(pre[:, half * 128 : half * 128 + 128] + bias)
            lifted[2 * x + half] = value.astype(BF16)
            slope1[2 * x + half] = slope[128:256]
        return 0

    lax.fori_loop(0, 10, lift, 0, unroll=5)

    def clear(ref, first_x, last_x, first_y, last_y):
        @pl.when(g == 0)
        def _():
            for x in first_x:
                ref[x] = jnp.zeros(ref.shape[1:], BF16)

        @pl.when(g == 1)
        def _():
            for x in last_x:
                ref[x] = jnp.zeros(ref.shape[1:], BF16)

        def wipe(rows):
            def body(x, _):
                ref[x, rows, :] = jnp.zeros((rows.size, 128), BF16)
                return 0
            lax.fori_loop(0, ref.shape[0], body, 0)

        @pl.when(s == 0)
        def _():
            wipe(first_y)

        @pl.when(s == 127)
        def _():
            wipe(last_y)

    clear(lifted, (0, 1), (18, 19), pl.ds(0, 128), pl.ds(256, 128))
    increments()

    def summed_z(u):
        return roll_z(u[:64], 1) + u[64:128] + roll_z(u[128:], -1)

    def around(ref, x, first, rows):
        pieces = [ref[x + ox] for ox in range(3)]
        return jnp.concatenate(
            [
                jnp.concatenate([piece[64 * y : 64 * y + 192] for piece in pieces], axis=0)
                for y in range(first, first + rows)
            ],
            axis=1,
        )

    def mix(x, _):
        u = jnp.dot(prepared.mix[...], around(lifted, x, 0, 4), preferred_element_type=F32)
        for y in range(4):
            value, slope = gelu_parts(summed_z(u[:, 128 * y : 128 * y + 128]) + prepared.bias[1])
            mixed[x, pl.ds(64 * y, 64), :] = value.astype(BF16)
            slope2[x, pl.ds(64 * y, 64), :] = slope
        return 0

    lax.fori_loop(0, 18, mix, 0, unroll=3)

    targets()

    def compare(batch, _):
        first = 6 * batch
        seen = jnp.concatenate([mixed[first + j] for j in range(6)], axis=1)
        row = lax.broadcasted_iota(jnp.int32, (16, 768), 0)
        bias = jnp.where(row % 2 == 0, prepared.b_out[:, 0:1], prepared.b_out[:, 1:2])
        predicted = jnp.dot(prepared.out[...], seen, preferred_element_type=F32) + bias
        goal = jnp.concatenate(
            [tgt[pl.ds(pl.multiple_of((x0 + first + j) * 8, 8), 8), :] for j in range(6)], axis=1
        )
        goal = jnp.concatenate([goal, jnp.zeros((8, 768), F32)], axis=0)
        error = (loss_scale * (predicted - goal)).astype(BF16)
        back = jnp.dot(prepared.outt[...], error, preferred_element_type=F32)
        for j in range(6):
            cot[first + j] = (back[:, 128 * j : 128 * j + 128] * slope2[first + j]).astype(BF16)
            errors[first + j] = error[:, 128 * j : 128 * j + 128]
        return 0

    lax.fori_loop(0, 3, compare, 0)
    clear(cot, (0,), (17,), pl.ds(0, 64), pl.ds(192, 64))
    total[...] = jnp.zeros_like(total)

    def mix_grad(x, mixbias):
        here = cot[x + 1, pl.ds(64, 128), :]
        mine = here.astype(F32)
        before = roll_z(mine, -1).astype(BF16)
        after = roll_z(mine, 1).astype(BF16)
        seen = around(lifted, x + 1, 1, 2)
        theirs = jnp.concatenate(
            [
                jnp.concatenate([part[64 * y : 64 * y + 64] for part in (before, here, after)], axis=0)
                for y in range(2)
            ],
            axis=1,
        )
        total[...] += rows_dot(seen, theirs)
        return mixbias + mine[:64] + mine[64:]

    mixbias = lax.fori_loop(0, 16, mix_grad, jnp.zeros((64, 128), F32), unroll=4)

    flat = total[...].T
    high = flat.astype(BF16)
    low = (flat - high.astype(F32)).astype(BF16)
    placed = jnp.dot(jnp.concatenate([high, low], axis=0), unspread_ref[...], preferred_element_type=F32)
    placed = placed[:192] + placed[192:]
    full = placed[:64] + pltpu.roll(placed[64:128], 1, 1) + pltpu.roll(placed[128:], 2, 1)
    for c in range(32):
        at, half = 4 * (c // 2), 896 * (c % 2)
        buf[c] = full[at : at + 4, half : half + 896]
    summing.begin()

    def backward(x, _):
        u = jnp.dot(prepared.back[...], around(cot, x, 0, 2), preferred_element_type=F32)
        back = jnp.concatenate([summed_z(u[:, :128]), summed_z(u[:, 128:])], axis=0)
        down[x] = (back * slope1[x + 2]).astype(BF16)
        return 0

    lax.fori_loop(0, 16, backward, 0, unroll=4)
    summing.plane()

    liftbias = jnp.zeros((64, 128), F32)
    outbias = jnp.zeros((8, 128), F32)
    lift_total = jnp.zeros((128, 144), F32)
    out_total = jnp.zeros((128, 16), F32)
    for batch in range(4):
        xs = range(4 * batch, 4 * batch + 4)
        lows = [down[x] for x in xs]
        for low in lows:
            low = low.astype(F32)
            liftbias = liftbias + low[:64] + low[64:]
        ins = jnp.concatenate([v3[x + 2 : x + 5].reshape(144, 128) for x in xs], axis=1)
        lift_total += rows_dot(jnp.concatenate(lows, axis=1), ins)
        errs = [errors[x + 1] for x in xs]
        for err in errs:
            outbias = outbias + err.astype(F32)[:8]
        out_total += rows_dot(
            jnp.concatenate([mixed[x + 1, pl.ds(64, 128), :] for x in xs], axis=1),
            jnp.concatenate(errs, axis=1),
        )

    small = jnp.zeros((64, 128), F32)
    for y in range(2):
        small += jnp.dot(
            lift_total[64 * y : 64 * y + 64], pick[y],
            preferred_element_type=F32, precision=lax.Precision.HIGHEST,
        )
    lane = lax.broadcasted_iota(jnp.int32, (64, 128), 1)
    row = lax.broadcasted_iota(jnp.int32, (64, 128), 0)
    small = jnp.where(lane == 54, jnp.sum(liftbias, axis=1, keepdims=True), small)
    small = jnp.where(lane == 55, jnp.sum(mixbias, axis=1, keepdims=True), small)
    for k in range(2):
        piece = out_total[:64, 2 + k : 3 + k] + out_total[64:, 4 + k : 5 + k]
        small = jnp.where(lane == 56 + k, piece, small)
    per_row = jnp.sum(outbias, axis=1, keepdims=True)
    pair = per_row[2:4] + per_row[4:6]
    for k in range(2):
        small = jnp.where((lane == 58) & (row == k), pair[k : k + 1], small)
    small = jnp.concatenate([small[:32, :64], small[32:, :64]], axis=1)
    for c in range(16):
        small_buf[c] = small[2 * c : 2 * c + 2]
    summing.small_plane()


class Ring:
    def __init__(self):
        y_lo = lax.axis_index("grp")
        gx = lax.axis_index("gx")
        gy = lax.axis_index("gy")
        self.z, self.x = gx // 4, gx % 4
        self.y_hi, self.core = gy // 2, gy % 2
        self.y_lo, self.gx, self.gy = y_lo, gx, gy
        self.place = self.x * 4 + self.y_hi * 2 + y_lo
        self.sibling = (y_lo, gx, self.y_hi * 2 + 1 - self.core)

    def in_plane(self, other):
        return (other % 2, self.z * 4 + other // 4, ((other // 2) % 2) * 2 + self.core)

    def in_z(self, other):
        return (self.y_lo, other * 4 + self.x, self.gy)

    def greet(self, barrier):
        pl.semaphore_signal(barrier, inc=1, device_id=self.sibling, device_id_type=MESH)

        def greet_plane(j, _):
            other = self.in_plane((self.place + j) % 16)
            pl.semaphore_signal(barrier, inc=1, device_id=other, device_id_type=MESH)
            return 0

        def greet_z(j, _):
            other = self.in_z((self.z + j) % 8)
            pl.semaphore_signal(barrier, inc=1, device_id=other, device_id_type=MESH)
            return 0

        lax.fori_loop(1, 16, greet_plane, 0)
        lax.fori_loop(1, 8, greet_z, 0)


class Summing:
    def __init__(self, ring, buf, out, from_core, mine, from_plane, from_z, small, s_plane, s_z, s_out, s_core, sems):
        self.__dict__.update(locals())
        self.ours = pl.multiple_of(ring.core * 16, 16)
        self.theirs = pl.multiple_of((1 - ring.core) * 16, 16)

    def copy(self, src, dst, pair, device):
        return pltpu.make_async_remote_copy(
            src, dst, self.sems.at[2 * pair], self.sems.at[2 * pair + 1], device_id=device, device_id_type=MESH
        )

    def begin(self):
        self.swap = self.copy(self.buf.at[pl.ds(self.theirs, 16)], self.from_core, 0, self.ring.sibling)
        self.swap.start()

    def spread_plane(self, source, target, pair):
        ring = self.ring

        def start(j, _):
            other = lax.rem(ring.place + j, 16)
            self.copy(source(other), target, pair, ring.in_plane(other)).start()
            return 0

        lax.fori_loop(1, 16, start, 0)

    def spread_z(self, ref, pair):
        ring = self.ring
        own = ref.at[ring.z]

        def start(j, _):
            self.copy(own, own, pair, ring.in_z(lax.rem(ring.z + j, 8))).start()
            return 0

        lax.fori_loop(1, 8, start, 0)

    def finish(self, ref, first, count, pair):
        part = ref.at[pl.ds(first, count)]
        self.copy(part, part, pair, self.ring.sibling).wait()

    def plane(self):
        self.swap.wait()
        buf, mine, ours = self.buf, self.mine, self.ours

        def add_core(j, _):
            mine[j] = buf[ours + j] + self.from_core[j]
            return 0

        lax.fori_loop(0, 16, add_core, 0, unroll=4)
        place = self.ring.place
        self.spread_plane(lambda other: mine.at[other], self.from_plane.at[place], 1)
        self.from_plane[place] = mine[place]

    def small_plane(self):
        place = self.ring.place
        self.spread_plane(lambda other: self.small.at[other], self.s_plane.at[place], 2)
        self.s_plane[place] = self.small[place]

    def rest(self):
        place, z = self.ring.place, self.ring.z

        def total(ref, count):
            value = ref[0]
            for j in range(1, count):
                value = value + ref[j]
            return value

        self.finish(self.from_plane, 0, 15, 1)
        self.from_z[z] = total(self.from_plane, 16)
        self.spread_z(self.from_z, 3)
        self.finish(self.s_plane, 0, 15, 2)
        self.s_z[z] = total(self.s_plane, 16)
        self.spread_z(self.s_z, 4)

        self.finish(self.from_z, 0, 7, 3)
        own = self.out.at[self.ours + place]
        self.out[self.ours + place] = total(self.from_z, 8)
        self.spread_plane(lambda other: own, own, 5)
        self.finish(self.s_z, 0, 7, 4)
        small = self.s_out.at[place]
        self.s_out[place] = total(self.s_z, 8)
        self.spread_plane(lambda other: small, small, 6)

        self.finish(self.out, 0, 15, 5)
        half = self.out.at[pl.ds(self.ours, 16)]
        hand = self.copy(half, half, 7, self.ring.sibling)
        hand.start()
        self.finish(self.s_out, 0, 15, 6)
        swap = self.copy(self.s_out, self.s_core, 8, self.ring.sibling)
        swap.start()
        swap.wait()
        both = self.s_out[...] + self.s_core[...]
        for c in range(16):
            at = 16 + c // 2
            self.out[32 + at // 7, pl.ds(2 * (c % 2), 2), pl.ds(128 * (at % 7), 128)] = both[c]
        hand.wait()


def picks():
    grad = np.zeros((2, 144, 128), np.float32)
    ahead = np.zeros((6, 54, 144), np.float32)
    for ox in range(3):
        for oz in range(3):
            for ch in range(2):
                for oy in range(3):
                    tap = 27 * ch + 9 * ox + 3 * oy + oz
                    for y in range(2):
                        grad[y, ((ox * 3 + oz) * 2 + ch) * 8 + 2 + y + oy, tap] = 1
                    for y in range(6):
                        ahead[y, tap, ((ox * 3 + oz) * 2 + ch) * 8 + y + oy] = 1
    return grad, ahead


def main_kernel(
    loss_scale,
    sc_hbm, vel_hbm, w_mix_hbm, spread_hbm, w_lift_hbm, ahead_hbm, b_lift_hbm, b_mix_hbm, w_out_hbm, b_out_hbm,
    unspread_hbm, pick_hbm,
    out,
    adv, sc, vel, w_mix, spread, w_lift, ahead, b_lift, b_mix, w_out, b_out, unspread, pick,
    load, lift_w, mix_w, back_w, out_w, outt_w, bias,
    net, tgt, halo, held, wide, seen, inc, gains,
    v3, lifted, slope1, mixed, slope2, cot, down, errors, total, buf,
    from_core, mine, from_plane, from_z, small, s_plane, s_z, s_out, s_core,
    a_send, a_recv, b_send, b_recv, n_send, n_recv, c_send, c_recv, sums,
):
    pairs = (
        (sc_hbm, sc), (vel_hbm, vel), (w_mix_hbm, w_mix), (spread_hbm, spread), (w_lift_hbm, w_lift),
        (ahead_hbm, ahead), (b_lift_hbm, b_lift), (b_mix_hbm, b_mix), (w_out_hbm, w_out), (b_out_hbm, b_out),
        (unspread_hbm, unspread), (pick_hbm, pick),
    )
    loads = [pltpu.make_async_copy(*pair, load.at[j]) for j, pair in enumerate(pairs)]
    for copy in loads:
        copy.start()
    ring = Ring()
    prepared = Prepared(
        w_lift, b_lift, w_mix, b_mix, w_out, b_out, ahead, spread, lift_w, mix_w, back_w, out_w, outt_w, bias
    )

    def prepare_mix():
        for copy in loads[2:4]:
            copy.wait()
        prepared.mix_form()
        for copy in loads[:2]:
            copy.wait()

    def prepare_lift():
        for copy in loads[4:10]:
            copy.wait()
        prepared.lift_form()

    increments, targets, sent = solver(
        ring, prepare_mix, prepare_lift, prepared.back_form,
        sc, vel, adv, net, tgt, halo, held, wide, seen, inc, gains,
        a_send, a_recv, b_send, b_recv, n_send, n_recv, c_send, c_recv,
    )
    for copy in loads[10:]:
        copy.wait()
    summing = Summing(
        ring, buf, out, from_core, mine, from_plane, from_z, small, s_plane, s_z, s_out, s_core, sums
    )
    network(
        loss_scale, increments, targets, summing, net, tgt, prepared, unspread, pick,
        v3, lifted, slope1, mixed, slope2, cot, down, errors, total, buf, small,
    )
    for copy in sent:
        copy.wait_send()
    for block in range(16):
        out[32 + block // 7, :, pl.ds(128 * (block % 7), 128)] = adv[pl.ds(4 * block, 4), :]
    summing.rest()


def finish_kernel(out, adv, mix, lift, liftbias, mixbias, out_grad, outbias):
    def block(at):
        return out[32 + at // 7, :, pl.ds(128 * (at % 7), 128)]

    for at in range(16):
        adv[pl.ds(4 * at, 4), :] = block(at)
    for r in range(16):
        mix[pl.ds(4 * r, 4), pl.ds(0, 896)] = out[2 * r]
        mix[pl.ds(4 * r, 4), pl.ds(896, 832)] = out[2 * r + 1][:, :832]
    small = jnp.concatenate([block(16 + at) for at in range(8)], axis=0)
    turned = small.T
    turned = jnp.concatenate([turned[:64], turned[64:]], axis=1)
    lift[...] = turned[:54]
    liftbias[...] = turned[54:55]
    mixbias[...] = turned[55:56]
    out_grad[...] = turned[56:58]
    outbias[...] = turned[58:59, :2]


def train(loss_scale, scalars, velocity, w_lift, b_lift, w_mix, b_mix, w_out, b_out):
    dma = pltpu.SemaphoreType.DMA
    hbm = pl.BlockSpec(memory_space=pltpu.HBM)
    pick, ahead = picks()
    spread = np.zeros((64, 9, 3, 9, 64), np.float32)
    for m in range(9):
        for i in range(64):
            spread[i, m, 0, m, i] = 1
    spread = spread.reshape(1728, 576)
    unspread = np.zeros((576, 1792), np.float32)
    unspread[:, :1728] = spread.T
    chunk = (4, 896)

    def vmem(*shape, dtype=F32):
        return pltpu.VMEM(shape, dtype)

    out = pl.pallas_call(
        functools.partial(main_kernel, loss_scale),
        out_shape=jax.ShapeDtypeStruct((36,) + chunk, F32),
        in_specs=[hbm] * 12,
        out_specs=VMEM,
        scratch_shapes=[
            vmem(64, 128),
            vmem(64, 128), vmem(192, 128), vmem(64, 1728, dtype=BF16), vmem(1728, 576, dtype=BF16),
            vmem(54, 64, dtype=BF16), vmem(6, 54, 144, dtype=BF16), vmem(1, 64), vmem(1, 64),
            vmem(2, 64, dtype=BF16), vmem(1, 2), vmem(576, 1792, dtype=BF16), vmem(2, 144, 128), dma((12,)),
            vmem(384, 144, dtype=BF16), vmem(192, 576, dtype=BF16), vmem(192, 576, dtype=BF16),
            vmem(16, 256, dtype=BF16), vmem(256, 16, dtype=BF16), vmem(2, 64, 128),
            vmem(38 * 16, 128), vmem(34 * 8, 128),
            vmem(2, 64, 128), vmem(2, 32, 128), vmem(2, 32, 128, dtype=BF16),
            vmem(10, 2, 32, 128, dtype=BF16), vmem(8, 32, 128), vmem(2, 32, 128),
            vmem(22, 48, 128, dtype=BF16), vmem(20, 384, 128, dtype=BF16), vmem(20, 128, 128),
            vmem(18, 256, 128, dtype=BF16), vmem(18, 256, 128), vmem(18, 256, 128, dtype=BF16),
            vmem(16, 128, 128, dtype=BF16), vmem(18, 16, 128, dtype=BF16), vmem(576, 192),
            vmem(32, *chunk), vmem(16, *chunk), vmem(16, *chunk), vmem(16, *chunk), vmem(8, *chunk),
            vmem(16, 2, 128), vmem(16, 2, 128), vmem(8, 2, 128), vmem(16, 2, 128), vmem(16, 2, 128),
            dma, dma, dma, dma, dma, dma, dma, dma, dma((18,)),
        ],
        compiler_params=pltpu.CompilerParams(
            collective_id=0, has_side_effects=True, vmem_limit_bytes=VMEM_BYTES
        ),
        name="train",
    )(
        scalars, velocity, w_mix, jnp.asarray(spread, BF16), w_lift.T, jnp.asarray(ahead, BF16),
        b_lift[None], b_mix[None], w_out, b_out[None], jnp.asarray(unspread, BF16), jnp.asarray(pick),
    )
    shapes = ((64, 128), (64, 1728), (54, 64), (1, 64), (1, 64), (2, 64), (1, 2))
    return pl.pallas_call(
        finish_kernel,
        out_shape=tuple(jax.ShapeDtypeStruct(shape, F32) for shape in shapes),
        in_specs=[VMEM],
        out_specs=(VMEM,) * 7,
        compiler_params=pltpu.CompilerParams(vmem_limit_bytes=8 * 2**20),
        name="finish",
    )(out)


def on_device(scalars, velocity, w_lift, b_lift, w_mix, b_mix, w_out, b_out):
    total_cells = scalars.size * lax.axis_size("gx") * lax.axis_size("gy")
    loss_scale = 2.0 / math.sqrt(total_cells)
    adv, mix, lift, liftbias, mixbias, out_grad, outbias = train(
        loss_scale, scalars.reshape(64, 128), velocity.reshape(192, 128),
        w_lift, b_lift, w_mix, b_mix, w_out, b_out,
    )
    return (
        adv.reshape(scalars.shape), lift.T, liftbias[0], mix, mixbias[0], out_grad, outbias[0],
    )


def solution(mesh):
    cells = P("grp", None, ("gx", "gy"), None)
    in_specs = (cells, P(None, None, ("gx", "gy"), None)) + (P(),) * 6
    out_specs = (cells,) + (P(),) * 6
    return jax.shard_map(
        on_device, mesh=mesh, in_specs=in_specs, out_specs=out_specs, check_vma=False
    )
```

```python
import functools
import math

import jax
import jax.numpy as jnp
import numpy as np
from jax import lax
from jax.experimental import pallas as pl
from jax.experimental.pallas import tpu as pltpu
from jax.sharding import PartitionSpec as P

MESH = pl.DeviceIdType.MESH
F32 = jnp.float32
BF16 = jnp.bfloat16
VMEM = pl.BlockSpec(memory_space=pltpu.VMEM)
VMEM_BYTES = 62 * 2**20


def place():
    return lax.axis_index("grp"), lax.axis_index("gx") * 4 + lax.axis_index("gy")


def roll_z(value, step):
    lane = lax.broadcasted_iota(jnp.int32, value.shape, value.ndim - 1)
    edge = 0 if step > 0 else 127
    return jnp.where(lane % 128 == edge, 0.0, pltpu.roll(value, step % 128, value.ndim - 1))


def solver(
    ring, prepare_mix, prepare_lift, prepare_back,
    sc_hbm, sc, vel, adv, net, tgt,
    halo, held, wide, seen, inc, gains,
    a_send, a_recv, b_send, b_recv, n_send, n_recv, c_send, c_recv,
):
    g, s = place()
    diffusivity = jnp.where(g == 0, jnp.float32(0.08), jnp.float32(0.12))

    def device(step, field):
        other = lax.rem(s + step + 128, 128)
        return (field, other // 4, lax.rem(other, 4))

    partners = [(d, f) for d in (-2, -1, 0, 1, 2) for f in (0, 1) if (d, f) != (0, 0)]
    def partner(d, f):
        return device(d, g if f == 0 else 1 - g)

    barrier = pltpu.get_barrier_semaphore()
    for d, f in partners:
        pl.semaphore_signal(barrier, inc=1, device_id=partner(d, f), device_id_type=MESH)
    ring.greet(barrier)
    pl.semaphore_wait(barrier, len(partners) + 23)

    def send(src, dst, ssem, rsem, d, f):
        return pltpu.make_async_remote_copy(
            src, dst, ssem, rsem, device_id=partner(d, f), device_id_type=MESH
        )

    first = [
        send(sc_hbm, halo.at[0], a_send, a_recv, 1, 0),
        send(sc_hbm, halo.at[1], a_send, a_recv, -1, 0),
    ]
    first_all = send(halo, halo, a_send, a_recv, 1, 0)
    for copy in first:
        copy.start()

    prepare_mix()
    speed = [[vel[pl.ds(64 * d + y, 32, stride=2), :] for y in range(2)] for d in range(3)]
    row = lax.broadcasted_iota(jnp.int32, (32, 128), 0)

    def step(centre, below, above, y):
        plus_x = jnp.where(row == 31, 0.0, pltpu.roll(centre, 31, 0))
        minus_x = jnp.where(row == 0, 0.0, pltpu.roll(centre, 1, 0))
        plus_z = roll_z(centre, -1)
        minus_z = roll_z(centre, 1)
        laplace = plus_x + minus_x + above + below + plus_z + minus_z - 6.0 * centre
        advect = (
            speed[0][y] * (plus_x - minus_x)
            + speed[1][y] * (above - below)
            + speed[2][y] * (plus_z - minus_z)
        )
        return centre + diffusivity * laplace - 0.5 * advect

    own = [sc[pl.ds(y, 32, stride=2), :] for y in range(2)]
    first_all.wait_recv()
    below = jnp.where(s == 0, 0.0, halo[0, pl.ds(1, 32, stride=2), :])
    above = jnp.where(s == 127, 0.0, halo[1, pl.ds(0, 32, stride=2), :])
    stepped = [step(own[0], below, own[1], 0), step(own[1], own[0], above, 1)]
    for y in range(2):
        held[y] = stepped[y]
        wide[y] = stepped[y].astype(BF16)

    second = [
        send(held.at[1], gains.at[0], b_send, b_recv, 1, 0),
        send(held.at[0], gains.at[1], b_send, b_recv, -1, 0),
    ]
    second_all = send(gains, gains, b_send, b_recv, 1, 0)
    third = []
    for d, f in partners:
        slot = 2 * (2 - d) + g
        if abs(d) == 2:
            y = 1 if d > 0 else 0
            third.append(send(wide.at[y], seen.at[slot, y], n_send, n_recv, d, f))
        else:
            third.append(send(wide, seen.at[slot], n_send, n_recv, d, f))
    third_all = send(seen.at[pl.ds(0, 7)], seen.at[pl.ds(0, 7)], n_send, n_recv, 1, 0)
    for copy in second:
        copy.start()
    for copy in third:
        copy.start()
    for y in range(2):
        seen[4 + g, y] = wide[y]
    net[pl.ds(0, 48), :] = jnp.zeros((48, 128), F32)
    net[pl.ds(35 * 16, 48), :] = jnp.zeros((48, 128), F32)
    prepare_lift()
    prepare_back()
    second_all.wait_recv()
    below = jnp.where(s == 0, 0.0, gains[0])
    above = jnp.where(s == 127, 0.0, gains[1])
    advanced = [
        step(stepped[0], below, stepped[1], 0),
        step(stepped[1], stepped[0], above, 1),
    ]
    for y in range(2):
        adv[pl.ds(y, 32, stride=2), :] = advanced[y]
        inc[4 * g + 1 + y] = advanced[y] - stepped[y]
    for d, f in [(0, 1), (1, 0), (1, 1), (-1, 0), (-1, 1)]:
        if d == 0:
            part = inc.at[pl.ds(4 * g + 1, 2)]
            send(part, part, c_send, c_recv, d, f).start()
        elif d == 1:
            send(inc.at[4 * g + 2], inc.at[4 * g], c_send, c_recv, d, f).start()
        else:
            send(inc.at[4 * g + 1], inc.at[4 * g + 3], c_send, c_recv, d, f).start()

    fourth_all = send(inc.at[pl.ds(0, 6)], inc.at[pl.ds(0, 6)], c_send, c_recv, 1, 0)


    third_all.wait_recv()
    for field in range(2):
        for yy in range(8):
            slab, y = (yy + 1) // 2, (yy + 1) % 2
            y_at = 2 * s - 3 + yy
            inside = (y_at >= 0) & (y_at < 256)
            value = jnp.where(inside, seen[2 * slab + field, y].astype(F32), 0.0)
            net[pl.ds(48 + field * 8 + yy, 32, stride=16), :] = value

    def targets():
        fourth_all.wait_recv()
        tgt[pl.ds(0, 8), :] = jnp.zeros((8, 128), F32)
        tgt[pl.ds(33 * 8, 8), :] = jnp.zeros((8, 128), F32)
        for field in range(2):
            for yy in range(4):
                tgt[pl.ds(8 + yy * 2 + field, 32, stride=8), :] = inc[4 * field + yy]

    return targets, (first_all, second_all, third_all, fourth_all)


def gelu_parts(v):
    c = math.sqrt(2.0 / math.pi)
    square = v * v
    t = jnp.tanh(v * (c + (c * 0.044715) * square))
    half = 0.5 + 0.5 * t
    value = v * half
    slope = half + (0.5 * v) * (1.0 - t * t) * (c + (3.0 * c * 0.044715) * square)
    return value, slope


def rows_dot(a, b):
    return lax.dot_general(a, b, (((1,), (1,)), ((), ())), preferred_element_type=F32)


class Prepared:
    def __init__(self, w_lift, b_lift, w_mix, b_mix, w_out, b_out, ahead, spread, lift, mix, back, out, outt, bias):
        self.__dict__.update(locals())

    def mix_form(self):
        wide = jnp.concatenate([self.w_mix[...].astype(F32), jnp.zeros((64, 64), F32)], axis=1)
        turned = [wide] + [pltpu.roll(wide, 1792 - oz, 1) for oz in (1, 2)]
        turned = jnp.concatenate([t[:, :1728] for t in turned], axis=0).astype(BF16)
        self.mix[...] = jnp.dot(turned, self.spread[...], preferred_element_type=F32).astype(BF16)

    def lift_form(self):
        flat = self.w_lift[...].astype(F32).T.astype(BF16)
        for y in range(6):
            band = jnp.dot(flat, self.ahead[y], preferred_element_type=F32)
            self.lift[pl.ds(64 * y, 64), :] = band.astype(BF16)
        for index, ref in enumerate((self.b_lift, self.b_mix)):
            self.bias[index] = jnp.broadcast_to(ref[...], (128, 64)).T
        four = jnp.concatenate([self.w_out[...].astype(F32)] * 4, axis=1)
        row = lax.broadcasted_iota(jnp.int32, (16, 256), 0)
        lane = lax.broadcasted_iota(jnp.int32, (16, 256), 1)
        both = jnp.where(row % 2 == 0, four[0:1], four[1:2])
        both = jnp.where(row // 2 == lane // 64, both, 0.0)
        self.out[...] = both.astype(BF16)
        self.outt[...] = both.T.astype(BF16)

    def back_form(self):
        flat = self.mix[...].astype(F32).T
        for oz in range(3):
            tiles = [flat[64 * m : 64 * m + 64, 64 * oz : 64 * oz + 64] for m in range(8, -1, -1)]
            self.back[pl.ds(64 * (2 - oz), 64), :] = jnp.concatenate(tiles, axis=1).astype(BF16)

def network(
    loss_scale, targets, summing, net, tgt, prepared, pick,
    v3, lifted, slope1, mixed, slope2, cot, down, errors, total, small_buf,
):
    g, s = place()
    x0 = g * 16

    def fill(x, _):
        rows = net[pl.ds(pl.multiple_of((x0 + x) * 16, 16), 16), :]
        v3[x, pl.ds(0, 16), :] = roll_z(rows, 1).astype(BF16)
        v3[x, pl.ds(16, 16), :] = rows.astype(BF16)
        v3[x, pl.ds(32, 16), :] = roll_z(rows, -1).astype(BF16)
        return 0

    lax.fori_loop(0, 22, fill, 0, unroll=11)

    def lift(x, _):
        seen = jnp.concatenate(
            [v3[pl.ds(2 * x, 3)].reshape(144, 128), v3[pl.ds(2 * x + 1, 3)].reshape(144, 128)], axis=1
        )
        pre = jnp.dot(prepared.lift[...], seen, preferred_element_type=F32)
        bias = jnp.concatenate([prepared.bias[0]] * 6, axis=0)
        for half in range(2):
            value, slope = gelu_parts(pre[:, half * 128 : half * 128 + 128] + bias)
            lifted[2 * x + half] = value.astype(BF16)
            slope1[2 * x + half] = slope[128:256]
        return 0

    lax.fori_loop(0, 10, lift, 0, unroll=5)

    def clear(ref, first_x, last_x, first_y, last_y):
        @pl.when(g == 0)
        def _():
            for x in first_x:
                ref[x] = jnp.zeros(ref.shape[1:], BF16)

        @pl.when(g == 1)
        def _():
            for x in last_x:
                ref[x] = jnp.zeros(ref.shape[1:], BF16)

        def wipe(rows):
            def body(x, _):
                ref[x, rows, :] = jnp.zeros((rows.size, 128), BF16)
                return 0
            lax.fori_loop(0, ref.shape[0], body, 0)

        @pl.when(s == 0)
        def _():
            wipe(first_y)

        @pl.when(s == 127)
        def _():
            wipe(last_y)

    clear(lifted, (0, 1), (18, 19), pl.ds(0, 128), pl.ds(256, 128))

    def summed_z(u):
        return roll_z(u[:64], 1) + u[64:128] + roll_z(u[128:], -1)

    def around(ref, x, first, rows):
        pieces = [ref[x + ox] for ox in range(3)]
        return jnp.concatenate(
            [
                jnp.concatenate([piece[64 * y : 64 * y + 192] for piece in pieces], axis=0)
                for y in range(first, first + rows)
            ],
            axis=1,
        )

    def mix(x, _):
        u = jnp.dot(prepared.mix[...], around(lifted, x, 0, 4), preferred_element_type=F32)
        for y in range(4):
            value, slope = gelu_parts(summed_z(u[:, 128 * y : 128 * y + 128]) + prepared.bias[1])
            mixed[x, pl.ds(64 * y, 64), :] = value.astype(BF16)
            slope2[x, pl.ds(64 * y, 64), :] = slope
        return 0

    lax.fori_loop(0, 18, mix, 0, unroll=3)

    targets()

    def compare(batch, _):
        first = 6 * batch
        seen = jnp.concatenate([mixed[first + j] for j in range(6)], axis=1)
        row = lax.broadcasted_iota(jnp.int32, (16, 768), 0)
        bias = jnp.where(row % 2 == 0, prepared.b_out[:, 0:1], prepared.b_out[:, 1:2])
        predicted = jnp.dot(prepared.out[...], seen, preferred_element_type=F32) + bias
        goal = jnp.concatenate(
            [tgt[pl.ds(pl.multiple_of((x0 + first + j) * 8, 8), 8), :] for j in range(6)], axis=1
        )
        goal = jnp.concatenate([goal, jnp.zeros((8, 768), F32)], axis=0)
        error = (loss_scale * (predicted - goal)).astype(BF16)
        back = jnp.dot(prepared.outt[...], error, preferred_element_type=F32)
        for j in range(6):
            cot[first + j] = (back[:, 128 * j : 128 * j + 128] * slope2[first + j]).astype(BF16)
            errors[first + j] = error[:, 128 * j : 128 * j + 128]
        return 0

    lax.fori_loop(0, 3, compare, 0, unroll=3)
    clear(cot, (0,), (17,), pl.ds(0, 64), pl.ds(192, 64))
    total[...] = jnp.zeros_like(total)

    def mix_grad(x, mixbias):
        here = cot[x + 1, pl.ds(64, 128), :]
        mine = here.astype(F32)
        before = roll_z(mine, -1).astype(BF16)
        after = roll_z(mine, 1).astype(BF16)
        seen = around(lifted, x + 1, 1, 2)
        theirs = jnp.concatenate(
            [
                jnp.concatenate(
                    [
                        part[64 * y + 32 * half : 64 * y + 32 * half + 32]
                        for half in range(2)
                        for part in (before, here, after)
                    ],
                    axis=0,
                )
                for y in range(2)
            ],
            axis=1,
        )
        total[:, pl.ds(0, 576)] += rows_dot(theirs, seen)
        return mixbias + mine[:64] + mine[64:]

    mixbias = lax.fori_loop(0, 16, mix_grad, jnp.zeros((64, 128), F32), unroll=4)

    summing.begin()

    def backward(x, _):
        u = jnp.dot(prepared.back[...], around(cot, x, 0, 2), preferred_element_type=F32)
        back = jnp.concatenate([summed_z(u[:, :128]), summed_z(u[:, 128:])], axis=0)
        down[x] = (back * slope1[x + 2]).astype(BF16)
        return 0

    lax.fori_loop(0, 8, backward, 0, unroll=4)
    summing.plane()
    lax.fori_loop(8, 16, backward, 0, unroll=4)

    liftbias = jnp.zeros((64, 128), F32)
    outbias = jnp.zeros((8, 128), F32)
    lift_total = jnp.zeros((128, 144), F32)
    out_total = jnp.zeros((128, 16), F32)
    for batch in range(4):
        xs = range(4 * batch, 4 * batch + 4)
        lows = [down[x] for x in xs]
        for low in lows:
            low = low.astype(F32)
            liftbias = liftbias + low[:64] + low[64:]
        ins = jnp.concatenate([v3[x + 2 : x + 5].reshape(144, 128) for x in xs], axis=1)
        lift_total += rows_dot(jnp.concatenate(lows, axis=1), ins)
        errs = [errors[x + 1] for x in xs]
        for err in errs:
            outbias = outbias + err.astype(F32)[:8]
        out_total += rows_dot(
            jnp.concatenate([mixed[x + 1, pl.ds(64, 128), :] for x in xs], axis=1),
            jnp.concatenate(errs, axis=1),
        )

    small = jnp.zeros((64, 128), F32)
    for y in range(2):
        small += jnp.dot(
            lift_total[64 * y : 64 * y + 64], pick[y],
            preferred_element_type=F32, precision=lax.Precision.HIGHEST,
        )
    lane = lax.broadcasted_iota(jnp.int32, (64, 128), 1)
    row = lax.broadcasted_iota(jnp.int32, (64, 128), 0)
    small = jnp.where(lane == 54, jnp.sum(liftbias, axis=1, keepdims=True), small)
    small = jnp.where(lane == 55, jnp.sum(mixbias, axis=1, keepdims=True), small)
    for k in range(2):
        piece = out_total[:64, 2 + k : 3 + k] + out_total[64:, 4 + k : 5 + k]
        small = jnp.where(lane == 56 + k, piece, small)
    per_row = jnp.sum(outbias, axis=1, keepdims=True)
    pair = per_row[2:4] + per_row[4:6]
    for k in range(2):
        small = jnp.where((lane == 58) & (row == k), pair[k : k + 1], small)
    small = jnp.concatenate([small[:32, :64], small[32:, :64]], axis=1)
    for c in range(16):
        small_buf[c] = small[2 * c : 2 * c + 2]
    summing.small_plane()


class Ring:
    def __init__(self):
        y_lo = lax.axis_index("grp")
        gx = lax.axis_index("gx")
        gy = lax.axis_index("gy")
        self.z, self.x = gx // 4, gx % 4
        self.y_hi, self.core = gy // 2, gy % 2
        self.y_lo, self.gx, self.gy = y_lo, gx, gy
        self.place = self.x * 4 + self.y_hi * 2 + y_lo
        self.sibling = (y_lo, gx, self.y_hi * 2 + 1 - self.core)

    def in_plane(self, other):
        return (other % 2, self.z * 4 + other // 4, ((other // 2) % 2) * 2 + self.core)

    def in_z(self, other):
        return (self.y_lo, other * 4 + self.x, self.gy)

    def greet(self, barrier):
        pl.semaphore_signal(barrier, inc=1, device_id=self.sibling, device_id_type=MESH)

        def greet_plane(j, _):
            other = self.in_plane((self.place + j) % 16)
            pl.semaphore_signal(barrier, inc=1, device_id=other, device_id_type=MESH)
            return 0

        def greet_z(j, _):
            other = self.in_z((self.z + j) % 8)
            pl.semaphore_signal(barrier, inc=1, device_id=other, device_id_type=MESH)
            return 0

        lax.fori_loop(1, 16, greet_plane, 0)
        lax.fori_loop(1, 8, greet_z, 0)


class Summing:
    def __init__(self, ring, total, unspread, out, from_core, mine, from_plane, from_z, small, s_plane, s_z, s_out, s_core, sems):
        self.__dict__.update(locals())
        self.ours = pl.multiple_of(ring.core * 16, 16)

    def copy(self, src, dst, pair, device):
        return pltpu.make_async_remote_copy(
            src, dst, self.sems.at[2 * pair], self.sems.at[2 * pair + 1], device_id=device, device_id_type=MESH
        )

    def begin(self):
        self.swap = self.copy(
            self.total.at[pl.ds(pl.multiple_of((1 - self.ring.core) * 96, 96), 96)], self.from_core, 0, self.ring.sibling
        )
        self.swap.start()

    def spread_plane(self, source, target, pair):
        ring = self.ring

        def start(j, _):
            other = lax.rem(ring.place + j, 16)
            self.copy(source(other), target, pair, ring.in_plane(other)).start()
            return 0

        lax.fori_loop(1, 16, start, 0)

    def spread_z(self, ref, pair):
        ring = self.ring
        own = ref.at[ring.z]

        def start(j, _):
            self.copy(own, own, pair, ring.in_z(lax.rem(ring.z + j, 8))).start()
            return 0

        lax.fori_loop(1, 8, start, 0)

    def finish(self, ref, first, count, pair):
        part = ref.at[pl.ds(first, count)]
        self.copy(part, part, pair, self.ring.sibling).wait()

    def plane(self):
        self.swap.wait()
        mine = self.mine
        own = self.total[pl.ds(pl.multiple_of(self.ring.core * 96, 96), 96), pl.ds(0, 576)]
        flat = own + self.from_core[:, pl.ds(0, 576)]
        high = flat.astype(BF16)
        low = (flat - high.astype(F32)).astype(BF16)
        placed = jnp.dot(
            jnp.concatenate([high, low], axis=0), self.unspread[...], preferred_element_type=F32
        )
        placed = placed[:96] + placed[96:]
        full = placed[:32] + pltpu.roll(placed[32:64], 1, 1) + pltpu.roll(placed[64:], 2, 1)
        for c in range(16):
            at, half = 4 * (c // 2), 896 * (c % 2)
            mine[c] = full[at : at + 4, half : half + 896]
        place = self.ring.place
        self.spread_plane(lambda other: mine.at[other], self.from_plane.at[place], 1)
        self.from_plane[place] = mine[place]

    def small_plane(self):
        place = self.ring.place
        self.spread_plane(lambda other: self.small.at[other], self.s_plane.at[place], 2)
        self.s_plane[place] = self.small[place]

    def rest(self):
        place, z = self.ring.place, self.ring.z

        def total(ref, count):
            value = ref[0]
            for j in range(1, count):
                value = value + ref[j]
            return value

        self.finish(self.from_plane, 0, 15, 1)
        self.from_z[z] = total(self.from_plane, 16)
        self.spread_z(self.from_z, 3)
        self.finish(self.s_plane, 0, 15, 2)
        self.s_z[z] = total(self.s_plane, 16)
        self.spread_z(self.s_z, 4)

        self.finish(self.from_z, 0, 7, 3)
        own = self.out.at[self.ours + place]
        self.out[self.ours + place] = total(self.from_z, 8)
        self.spread_plane(lambda other: own, own, 5)
        self.finish(self.s_z, 0, 7, 4)
        small = self.s_out.at[place]
        self.s_out[place] = total(self.s_z, 8)
        self.spread_plane(lambda other: small, small, 6)

        self.finish(self.out, 0, 15, 5)
        half = self.out.at[pl.ds(self.ours, 16)]
        hand = self.copy(half, half, 7, self.ring.sibling)
        hand.start()
        self.finish(self.s_out, 0, 15, 6)
        swap = self.copy(self.s_out, self.s_core, 8, self.ring.sibling)
        swap.start()
        swap.wait()
        both = self.s_out[...] + self.s_core[...]
        for c in range(16):
            at = 16 + c // 2
            self.out[32 + at // 7, pl.ds(2 * (c % 2), 2), pl.ds(128 * (at % 7), 128)] = both[c]
        hand.wait()


def picks():
    grad = np.zeros((2, 144, 128), np.float32)
    ahead = np.zeros((6, 54, 144), np.float32)
    for ox in range(3):
        for oz in range(3):
            for ch in range(2):
                for oy in range(3):
                    tap = 27 * ch + 9 * ox + 3 * oy + oz
                    for y in range(2):
                        grad[y, ((ox * 3 + oz) * 2 + ch) * 8 + 2 + y + oy, tap] = 1
                    for y in range(6):
                        ahead[y, tap, ((ox * 3 + oz) * 2 + ch) * 8 + y + oy] = 1
    return grad, ahead


def main_kernel(
    loss_scale,
    sc_hbm, vel_hbm, w_mix_hbm, spread_hbm, w_lift_hbm, ahead_hbm, b_lift_hbm, b_mix_hbm, w_out_hbm, b_out_hbm,
    unspread_hbm, pick_hbm,
    out,
    adv, sc, vel, w_mix, spread, w_lift, ahead, b_lift, b_mix, w_out, b_out, unspread, pick,
    load, lift_w, mix_w, back_w, out_w, outt_w, bias,
    net, tgt, halo, held, wide, seen, inc, gains,
    v3, lifted, slope1, mixed, slope2, cot, down, errors, total,
    from_core, mine, from_plane, from_z, small, s_plane, s_z, s_out, s_core,
    a_send, a_recv, b_send, b_recv, n_send, n_recv, c_send, c_recv, sums,
):
    pairs = (
        (sc_hbm, sc), (vel_hbm, vel), (w_mix_hbm, w_mix), (spread_hbm, spread), (w_lift_hbm, w_lift),
        (ahead_hbm, ahead), (b_lift_hbm, b_lift), (b_mix_hbm, b_mix), (w_out_hbm, w_out), (b_out_hbm, b_out),
        (unspread_hbm, unspread), (pick_hbm, pick),
    )
    loads = [pltpu.make_async_copy(*pair, load.at[j]) for j, pair in enumerate(pairs)]
    for copy in loads:
        copy.start()
    ring = Ring()
    prepared = Prepared(
        w_lift, b_lift, w_mix, b_mix, w_out, b_out, ahead, spread, lift_w, mix_w, back_w, out_w, outt_w, bias
    )

    def prepare_mix():
        for copy in loads[2:4]:
            copy.wait()
        prepared.mix_form()
        for copy in loads[:2]:
            copy.wait()

    def prepare_lift():
        for copy in loads[4:10]:
            copy.wait()
        prepared.lift_form()

    targets, sent = solver(
        ring, prepare_mix, prepare_lift, prepared.back_form,
        sc_hbm, sc, vel, adv, net, tgt, halo, held, wide, seen, inc, gains,
        a_send, a_recv, b_send, b_recv, n_send, n_recv, c_send, c_recv,
    )
    for copy in loads[10:]:
        copy.wait()
    summing = Summing(
        ring, total, unspread, out, from_core, mine, from_plane, from_z, small, s_plane, s_z, s_out, s_core, sums
    )
    network(
        loss_scale, targets, summing, net, tgt, prepared, pick,
        v3, lifted, slope1, mixed, slope2, cot, down, errors, total, small,
    )
    for copy in sent:
        copy.wait_send()
    for block in range(16):
        out[32 + block // 7, :, pl.ds(128 * (block % 7), 128)] = adv[pl.ds(4 * block, 4), :]
    summing.rest()


def finish_kernel(out, adv, mix, lift, liftbias, mixbias, out_grad, outbias):
    def block(at):
        return out[32 + at // 7, :, pl.ds(128 * (at % 7), 128)]

    for at in range(16):
        adv[pl.ds(4 * at, 4), :] = block(at)
    for r in range(16):
        mix[pl.ds(4 * r, 4), pl.ds(0, 896)] = out[2 * r]
        mix[pl.ds(4 * r, 4), pl.ds(896, 832)] = out[2 * r + 1][:, :832]
    small = jnp.concatenate([block(16 + at) for at in range(8)], axis=0)
    turned = small.T
    turned = jnp.concatenate([turned[:64], turned[64:]], axis=1)
    lift[...] = turned[:54]
    liftbias[...] = turned[54:55]
    mixbias[...] = turned[55:56]
    out_grad[...] = turned[56:58]
    outbias[...] = turned[58:59, :2]


def train(loss_scale, scalars, velocity, w_lift, b_lift, w_mix, b_mix, w_out, b_out):
    dma = pltpu.SemaphoreType.DMA
    hbm = pl.BlockSpec(memory_space=pltpu.HBM)
    pick, ahead = picks()
    spread = np.zeros((64, 9, 3, 9, 64), np.float32)
    for m in range(9):
        for i in range(64):
            spread[i, m, 0, m, i] = 1
    spread = spread.reshape(1728, 576)
    unspread = np.zeros((576, 1792), np.float32)
    unspread[:, :1728] = spread.T
    chunk = (4, 896)

    def vmem(*shape, dtype=F32):
        return pltpu.VMEM(shape, dtype)

    out = pl.pallas_call(
        functools.partial(main_kernel, loss_scale),
        out_shape=jax.ShapeDtypeStruct((36,) + chunk, F32),
        in_specs=[hbm] * 12,
        out_specs=VMEM,
        scratch_shapes=[
            vmem(64, 128),
            vmem(64, 128), vmem(192, 128), vmem(64, 1728, dtype=BF16), vmem(1728, 576, dtype=BF16),
            vmem(54, 64, dtype=BF16), vmem(6, 54, 144, dtype=BF16), vmem(1, 64), vmem(1, 64),
            vmem(2, 64, dtype=BF16), vmem(1, 2), vmem(576, 1792, dtype=BF16), vmem(2, 144, 128), dma((12,)),
            vmem(384, 144, dtype=BF16), vmem(192, 576, dtype=BF16), vmem(192, 576, dtype=BF16),
            vmem(16, 256, dtype=BF16), vmem(256, 16, dtype=BF16), vmem(2, 64, 128),
            vmem(38 * 16, 128), vmem(34 * 8, 128),
            vmem(2, 64, 128), vmem(2, 32, 128), vmem(2, 32, 128, dtype=BF16),
            vmem(10, 2, 32, 128, dtype=BF16), vmem(8, 32, 128), vmem(2, 32, 128),
            vmem(22, 48, 128, dtype=BF16), vmem(20, 384, 128, dtype=BF16), vmem(20, 128, 128),
            vmem(18, 256, 128, dtype=BF16), vmem(18, 256, 128), vmem(18, 256, 128, dtype=BF16),
            vmem(16, 128, 128, dtype=BF16), vmem(18, 16, 128, dtype=BF16), vmem(192, 640),
            vmem(96, 640), vmem(16, *chunk), vmem(16, *chunk), vmem(8, *chunk),
            vmem(16, 2, 128), vmem(16, 2, 128), vmem(8, 2, 128), vmem(16, 2, 128), vmem(16, 2, 128),
            dma, dma, dma, dma, dma, dma, dma, dma, dma((18,)),
        ],
        compiler_params=pltpu.CompilerParams(
            collective_id=0, has_side_effects=True, vmem_limit_bytes=VMEM_BYTES
        ),
        name="train",
    )(
        scalars, velocity, w_mix, jnp.asarray(spread, BF16), w_lift.T, jnp.asarray(ahead, BF16),
        b_lift[None], b_mix[None], w_out, b_out[None], jnp.asarray(unspread, BF16), jnp.asarray(pick),
    )
    shapes = ((64, 128), (64, 1728), (54, 64), (1, 64), (1, 64), (2, 64), (1, 2))
    return pl.pallas_call(
        finish_kernel,
        out_shape=tuple(jax.ShapeDtypeStruct(shape, F32) for shape in shapes),
        in_specs=[VMEM],
        out_specs=(VMEM,) * 7,
        compiler_params=pltpu.CompilerParams(vmem_limit_bytes=8 * 2**20),
        name="finish",
    )(out)


def on_device(scalars, velocity, w_lift, b_lift, w_mix, b_mix, w_out, b_out):
    total_cells = scalars.size * lax.axis_size("gx") * lax.axis_size("gy")
    loss_scale = 2.0 / math.sqrt(total_cells)
    adv, mix, lift, liftbias, mixbias, out_grad, outbias = train(
        loss_scale, scalars.reshape(64, 128), velocity.reshape(192, 128),
        w_lift, b_lift, w_mix, b_mix, w_out, b_out,
    )
    return (
        adv.reshape(scalars.shape), lift.T, liftbias[0], mix, mixbias[0], out_grad, outbias[0],
    )


def solution(mesh):
    cells = P("grp", None, ("gx", "gy"), None)
    in_specs = (cells, P(None, None, ("gx", "gy"), None)) + (P(),) * 6
    out_specs = (cells,) + (P(),) * 6
    return jax.shard_map(
        on_device, mesh=mesh, in_specs=in_specs, out_specs=out_specs, check_vma=False
    )
```

```python
import functools
import math

import jax
import jax.numpy as jnp
import numpy as np
from jax import lax
from jax.experimental import pallas as pl
from jax.experimental.pallas import tpu as pltpu
from jax.sharding import PartitionSpec as P

MESH = pl.DeviceIdType.MESH
F32 = jnp.float32
BF16 = jnp.bfloat16
VMEM = pl.BlockSpec(memory_space=pltpu.VMEM)
VMEM_BYTES = 62 * 2**20


def place():
    return lax.axis_index("grp"), lax.axis_index("gx") * 4 + lax.axis_index("gy")


def roll_z(value, step):
    lane = lax.broadcasted_iota(jnp.int32, value.shape, value.ndim - 1)
    edge = 0 if step > 0 else 127
    return jnp.where(lane % 128 == edge, 0.0, pltpu.roll(value, step % 128, value.ndim - 1))


def solver(
    ring, prepare_mix, prepare_lift, prepare_back,
    sc_hbm, sc, vel, adv, net, tgt,
    halo, held, wide, seen, inc, gains,
    a_send, a_recv, b_send, b_recv, n_send, n_recv, c_send, c_recv,
):
    g, s = place()
    diffusivity = jnp.where(g == 0, jnp.float32(0.08), jnp.float32(0.12))

    def device(step, field):
        other = lax.rem(s + step + 128, 128)
        return (field, other // 4, lax.rem(other, 4))

    partners = [(d, f) for d in (-2, 2, -1, 1, 0) for f in (1, 0) if (d, f) != (0, 0)]
    def partner(d, f):
        return device(d, g if f == 0 else 1 - g)

    barrier = pltpu.get_barrier_semaphore()
    ring.greet(barrier)
    for d, f in partners:
        pl.semaphore_signal(barrier, inc=1, device_id=partner(d, f), device_id_type=MESH)
    pl.semaphore_wait(barrier, len(partners) + 23)

    def send(src, dst, ssem, rsem, d, f):
        return pltpu.make_async_remote_copy(
            src, dst, ssem, rsem, device_id=partner(d, f), device_id_type=MESH
        )

    first = [
        send(sc_hbm, halo.at[0], a_send, a_recv, 1, 0),
        send(sc_hbm, halo.at[1], a_send, a_recv, -1, 0),
    ]
    first_all = send(halo, halo, a_send, a_recv, 1, 0)
    for copy in first:
        copy.start()

    prepare_mix()
    speed = [[vel[pl.ds(64 * d + y, 32, stride=2), :] for y in range(2)] for d in range(3)]
    row = lax.broadcasted_iota(jnp.int32, (32, 128), 0)

    def step(centre, below, above, y):
        plus_x = jnp.where(row == 31, 0.0, pltpu.roll(centre, 31, 0))
        minus_x = jnp.where(row == 0, 0.0, pltpu.roll(centre, 1, 0))
        plus_z = roll_z(centre, -1)
        minus_z = roll_z(centre, 1)
        laplace = plus_x + minus_x + above + below + plus_z + minus_z - 6.0 * centre
        advect = (
            speed[0][y] * (plus_x - minus_x)
            + speed[1][y] * (above - below)
            + speed[2][y] * (plus_z - minus_z)
        )
        return centre + diffusivity * laplace - 0.5 * advect

    own = [sc[pl.ds(y, 32, stride=2), :] for y in range(2)]
    first_all.wait_recv()
    below = jnp.where(s == 0, 0.0, halo[0, pl.ds(1, 32, stride=2), :])
    above = jnp.where(s == 127, 0.0, halo[1, pl.ds(0, 32, stride=2), :])
    stepped = [step(own[0], below, own[1], 0), step(own[1], own[0], above, 1)]
    for y in range(2):
        held[y] = stepped[y]
        wide[y] = stepped[y].astype(BF16)

    second = [
        send(held.at[1], gains.at[0], b_send, b_recv, 1, 0),
        send(held.at[0], gains.at[1], b_send, b_recv, -1, 0),
    ]
    second_all = send(gains, gains, b_send, b_recv, 1, 0)
    third = []
    for d, f in partners:
        slot = 2 * (2 - d) + g
        if abs(d) == 2:
            y = 1 if d > 0 else 0
            third.append(send(wide.at[y], seen.at[slot, y], n_send, n_recv, d, f))
        else:
            third.append(send(wide, seen.at[slot], n_send, n_recv, d, f))
    third_all = send(seen.at[pl.ds(0, 7)], seen.at[pl.ds(0, 7)], n_send, n_recv, 1, 0)
    for copy in second:
        copy.start()
    for copy in third:
        copy.start()
    for y in range(2):
        seen[4 + g, y] = wide[y]
    net[pl.ds(0, 48), :] = jnp.zeros((48, 128), F32)
    net[pl.ds(35 * 16, 48), :] = jnp.zeros((48, 128), F32)
    prepare_lift()
    prepare_back()
    second_all.wait_recv()
    below = jnp.where(s == 0, 0.0, gains[0])
    above = jnp.where(s == 127, 0.0, gains[1])
    advanced = [
        step(stepped[0], below, stepped[1], 0),
        step(stepped[1], stepped[0], above, 1),
    ]
    for y in range(2):
        adv[pl.ds(y, 32, stride=2), :] = advanced[y]
        inc[4 * g + 1 + y] = advanced[y] - stepped[y]
    for d, f in [(0, 1), (1, 0), (1, 1), (-1, 0), (-1, 1)]:
        if d == 0:
            part = inc.at[pl.ds(4 * g + 1, 2)]
            send(part, part, c_send, c_recv, d, f).start()
        elif d == 1:
            send(inc.at[4 * g + 2], inc.at[4 * g], c_send, c_recv, d, f).start()
        else:
            send(inc.at[4 * g + 1], inc.at[4 * g + 3], c_send, c_recv, d, f).start()

    fourth_all = send(inc.at[pl.ds(0, 6)], inc.at[pl.ds(0, 6)], c_send, c_recv, 1, 0)


    third_all.wait_recv()
    for field in range(2):
        for yy in range(8):
            slab, y = (yy + 1) // 2, (yy + 1) % 2
            y_at = 2 * s - 3 + yy
            inside = (y_at >= 0) & (y_at < 256)
            value = jnp.where(inside, seen[2 * slab + field, y].astype(F32), 0.0)
            net[pl.ds(48 + field * 8 + yy, 32, stride=16), :] = value

    def targets():
        fourth_all.wait_recv()
        tgt[pl.ds(0, 8), :] = jnp.zeros((8, 128), F32)
        tgt[pl.ds(33 * 8, 8), :] = jnp.zeros((8, 128), F32)
        for field in range(2):
            for yy in range(4):
                tgt[pl.ds(8 + yy * 2 + field, 32, stride=8), :] = inc[4 * field + yy]

    return targets, (first_all, second_all, third_all, fourth_all)


def gelu_parts(v):
    c = math.sqrt(2.0 / math.pi)
    square = v * v
    t = jnp.tanh(v * (c + (c * 0.044715) * square))
    half = 0.5 + 0.5 * t
    value = v * half
    slope = half + (0.5 * v) * (1.0 - t * t) * (c + (3.0 * c * 0.044715) * square)
    return value, slope


def rows_dot(a, b):
    return lax.dot_general(a, b, (((1,), (1,)), ((), ())), preferred_element_type=F32)


class Prepared:
    def __init__(self, w_lift, b_lift, w_mix, b_mix, w_out, b_out, ahead, spread, lift, mix, back, out, outt, bias):
        self.__dict__.update(locals())

    def mix_form(self):
        wide = jnp.concatenate([self.w_mix[...].astype(F32), jnp.zeros((64, 64), F32)], axis=1)
        turned = [wide] + [pltpu.roll(wide, 1792 - oz, 1) for oz in (1, 2)]
        turned = jnp.concatenate([t[:, :1728] for t in turned], axis=0).astype(BF16)
        self.mix[...] = jnp.dot(turned, self.spread[...], preferred_element_type=F32).astype(BF16)

    def lift_form(self):
        flat = self.w_lift[...].astype(F32).T.astype(BF16)
        for y in range(6):
            band = jnp.dot(flat, self.ahead[y], preferred_element_type=F32)
            self.lift[pl.ds(64 * y, 64), :] = band.astype(BF16)
        for index, ref in enumerate((self.b_lift, self.b_mix)):
            self.bias[index] = jnp.broadcast_to(ref[...], (128, 64)).T
        four = jnp.concatenate([self.w_out[...].astype(F32)] * 4, axis=1)
        row = lax.broadcasted_iota(jnp.int32, (16, 256), 0)
        lane = lax.broadcasted_iota(jnp.int32, (16, 256), 1)
        both = jnp.where(row % 2 == 0, four[0:1], four[1:2])
        both = jnp.where(row // 2 == lane // 64, both, 0.0)
        self.out[...] = both.astype(BF16)
        self.outt[...] = both.T.astype(BF16)

    def back_form(self):
        flat = self.mix[...].astype(F32).T
        for oz in range(3):
            tiles = [flat[64 * m : 64 * m + 64, 64 * oz : 64 * oz + 64] for m in range(8, -1, -1)]
            self.back[pl.ds(64 * (2 - oz), 64), :] = jnp.concatenate(tiles, axis=1).astype(BF16)

def network(
    loss_scale, targets, summing, net, tgt, prepared, pick,
    v3, lifted, slope1, mixed, slope2, cot, down, errors, total, small_buf,
):
    g, s = place()
    x0 = g * 16

    def fill(x, _):
        rows = net[pl.ds(pl.multiple_of((x0 + x) * 16, 16), 16), :]
        v3[x, pl.ds(0, 16), :] = roll_z(rows, 1).astype(BF16)
        v3[x, pl.ds(16, 16), :] = rows.astype(BF16)
        v3[x, pl.ds(32, 16), :] = roll_z(rows, -1).astype(BF16)
        return 0

    lax.fori_loop(0, 22, fill, 0, unroll=11)

    def lift(x, _):
        seen = jnp.concatenate(
            [v3[pl.ds(2 * x, 3)].reshape(144, 128), v3[pl.ds(2 * x + 1, 3)].reshape(144, 128)], axis=1
        )
        pre = jnp.dot(prepared.lift[...], seen, preferred_element_type=F32)
        bias = jnp.concatenate([prepared.bias[0]] * 6, axis=0)
        for half in range(2):
            value, slope = gelu_parts(pre[:, half * 128 : half * 128 + 128] + bias)
            lifted[2 * x + half] = value.astype(BF16)
            slope1[2 * x + half] = slope[128:256]
        return 0

    lax.fori_loop(0, 10, lift, 0, unroll=5)

    def clear(ref, first_x, last_x, first_y, last_y):
        @pl.when(g == 0)
        def _():
            for x in first_x:
                ref[x] = jnp.zeros(ref.shape[1:], BF16)

        @pl.when(g == 1)
        def _():
            for x in last_x:
                ref[x] = jnp.zeros(ref.shape[1:], BF16)

        def wipe(rows):
            def body(x, _):
                ref[x, rows, :] = jnp.zeros((rows.size, 128), BF16)
                return 0
            lax.fori_loop(0, ref.shape[0], body, 0)

        @pl.when(s == 0)
        def _():
            wipe(first_y)

        @pl.when(s == 127)
        def _():
            wipe(last_y)

    clear(lifted, (0, 1), (18, 19), pl.ds(0, 128), pl.ds(256, 128))

    def summed_z(u):
        return roll_z(u[:64], 1) + u[64:128] + roll_z(u[128:], -1)

    def around(ref, x, first, rows):
        pieces = [ref[x + ox] for ox in range(3)]
        return jnp.concatenate(
            [
                jnp.concatenate([piece[64 * y : 64 * y + 192] for piece in pieces], axis=0)
                for y in range(first, first + rows)
            ],
            axis=1,
        )

    def mix(x, _):
        u = jnp.dot(prepared.mix[...], around(lifted, x, 0, 4), preferred_element_type=F32)
        for y in range(4):
            value, slope = gelu_parts(summed_z(u[:, 128 * y : 128 * y + 128]) + prepared.bias[1])
            mixed[x, pl.ds(64 * y, 64), :] = value.astype(BF16)
            slope2[x, pl.ds(64 * y, 64), :] = slope
        return 0

    lax.fori_loop(0, 18, mix, 0, unroll=6)

    targets()

    def compare(batch, _):
        first = 6 * batch
        seen = jnp.concatenate([mixed[first + j] for j in range(6)], axis=1)
        row = lax.broadcasted_iota(jnp.int32, (16, 768), 0)
        bias = jnp.where(row % 2 == 0, prepared.b_out[:, 0:1], prepared.b_out[:, 1:2])
        predicted = jnp.dot(prepared.out[...], seen, preferred_element_type=F32) + bias
        goal = jnp.concatenate(
            [tgt[pl.ds(pl.multiple_of((x0 + first + j) * 8, 8), 8), :] for j in range(6)], axis=1
        )
        goal = jnp.concatenate([goal, jnp.zeros((8, 768), F32)], axis=0)
        error = (loss_scale * (predicted - goal)).astype(BF16)
        back = jnp.dot(prepared.outt[...], error, preferred_element_type=F32)
        for j in range(6):
            cot[first + j] = (back[:, 128 * j : 128 * j + 128] * slope2[first + j]).astype(BF16)
            errors[first + j] = error[:, 128 * j : 128 * j + 128]
        return 0

    lax.fori_loop(0, 3, compare, 0, unroll=3)
    clear(cot, (0,), (17,), pl.ds(0, 64), pl.ds(192, 64))
    total[...] = jnp.zeros_like(total)

    def mix_grad(x, mixbias):
        here = cot[x + 1, pl.ds(64, 128), :]
        mine = here.astype(F32)
        before = roll_z(mine, -1).astype(BF16)
        after = roll_z(mine, 1).astype(BF16)
        seen = around(lifted, x + 1, 1, 2)
        theirs = jnp.concatenate(
            [
                jnp.concatenate(
                    [
                        part[64 * y + 32 * half : 64 * y + 32 * half + 32]
                        for half in range(2)
                        for part in (before, here, after)
                    ],
                    axis=0,
                )
                for y in range(2)
            ],
            axis=1,
        )
        total[:, pl.ds(0, 576)] += rows_dot(theirs, seen)
        return mixbias + mine[:64] + mine[64:]

    mixbias = lax.fori_loop(0, 16, mix_grad, jnp.zeros((64, 128), F32), unroll=8)

    summing.begin()

    def backward(x, _):
        u = jnp.dot(prepared.back[...], around(cot, x, 0, 2), preferred_element_type=F32)
        back = jnp.concatenate([summed_z(u[:, :128]), summed_z(u[:, 128:])], axis=0)
        down[x] = (back * slope1[x + 2]).astype(BF16)
        return 0

    lax.fori_loop(0, 8, backward, 0, unroll=4)
    summing.plane()
    lax.fori_loop(8, 16, backward, 0, unroll=4)

    liftbias = jnp.zeros((64, 128), F32)
    outbias = jnp.zeros((8, 128), F32)
    lift_total = jnp.zeros((128, 144), F32)
    out_total = jnp.zeros((128, 16), F32)
    for batch in range(4):
        xs = range(4 * batch, 4 * batch + 4)
        lows = [down[x] for x in xs]
        for low in lows:
            low = low.astype(F32)
            liftbias = liftbias + low[:64] + low[64:]
        ins = jnp.concatenate([v3[x + 2 : x + 5].reshape(144, 128) for x in xs], axis=1)
        lift_total += rows_dot(jnp.concatenate(lows, axis=1), ins)
        errs = [errors[x + 1] for x in xs]
        for err in errs:
            outbias = outbias + err.astype(F32)[:8]
        out_total += rows_dot(
            jnp.concatenate([mixed[x + 1, pl.ds(64, 128), :] for x in xs], axis=1),
            jnp.concatenate(errs, axis=1),
        )

    small = jnp.zeros((64, 128), F32)
    for y in range(2):
        small += jnp.dot(
            lift_total[64 * y : 64 * y + 64], pick[y],
            preferred_element_type=F32, precision=lax.Precision.HIGHEST,
        )
    lane = lax.broadcasted_iota(jnp.int32, (64, 128), 1)
    row = lax.broadcasted_iota(jnp.int32, (64, 128), 0)
    small = jnp.where(lane == 54, jnp.sum(liftbias, axis=1, keepdims=True), small)
    small = jnp.where(lane == 55, jnp.sum(mixbias, axis=1, keepdims=True), small)
    for k in range(2):
        piece = out_total[:64, 2 + k : 3 + k] + out_total[64:, 4 + k : 5 + k]
        small = jnp.where(lane == 56 + k, piece, small)
    per_row = jnp.sum(outbias, axis=1, keepdims=True)
    pair = per_row[2:4] + per_row[4:6]
    for k in range(2):
        small = jnp.where((lane == 58) & (row == k), pair[k : k + 1], small)
    small = jnp.concatenate([small[:32, :64], small[32:, :64]], axis=1)
    for c in range(16):
        small_buf[c] = small[2 * c : 2 * c + 2]
    summing.small_plane()


class Ring:
    def __init__(self):
        y_lo = lax.axis_index("grp")
        gx = lax.axis_index("gx")
        gy = lax.axis_index("gy")
        self.z, x = lax.div(gx, 4), lax.rem(gx, 4)
        y_hi, core = lax.div(gy, 2), lax.rem(gy, 2)
        self.core, self.place = core, x * 4 + y_hi * 2 + y_lo
        self.sibling = (y_lo, gx, y_hi * 2 + 1 - core)

        def along(at, size):
            steps = [jnp.where(at + j >= size, at + j - size, at + j) for j in range(1, size)]
            return [(0, at)] + [(min(j, size - j), step) for j, step in enumerate(steps, 1)]

        plane = []
        for far_x, to_x in along(x, 4):
            for far_y, to_y in along(y_hi * 2 + y_lo, 4):
                to = (lax.rem(to_y, 2), self.z * 4 + to_x, lax.div(to_y, 2) * 2 + core)
                plane.append((far_x + far_y, to_x * 4 + to_y, to))
        rows = [(far, to_z, (y_lo, to_z * 4 + x, gy)) for far, to_z in along(self.z, 8)]
        self.plane = sorted(plane, key=lambda entry: -entry[0])[:-1]
        self.rows = sorted(rows, key=lambda entry: -entry[0])[:-1]

    def greet(self, barrier):
        for _, _, to in self.rows + self.plane:
            pl.semaphore_signal(barrier, inc=1, device_id=to, device_id_type=MESH)
        pl.semaphore_signal(barrier, inc=1, device_id=self.sibling, device_id_type=MESH)


class Summing:
    def __init__(self, ring, total, unspread, out, from_core, mine, from_plane, from_z, small, s_plane, s_z, s_out, s_core, sems):
        self.__dict__.update(locals())
        self.ours = pl.multiple_of(ring.core * 16, 16)

    def copy(self, src, dst, pair, device):
        return pltpu.make_async_remote_copy(
            src, dst, self.sems.at[2 * pair], self.sems.at[2 * pair + 1], device_id=device, device_id_type=MESH
        )

    def begin(self):
        self.swap = self.copy(
            self.total.at[pl.ds(pl.multiple_of((1 - self.ring.core) * 96, 96), 96)], self.from_core, 0, self.ring.sibling
        )
        self.swap.start()

    def spread_plane(self, source, target, pair):
        for _, other, to in self.ring.plane:
            self.copy(source(other), target, pair, to).start()

    def spread_z(self, ref, pair):
        own = ref.at[self.ring.z]
        for _, _, to in self.ring.rows:
            self.copy(own, own, pair, to).start()

    def finish(self, ref, first, count, pair):
        part = ref.at[pl.ds(first, count)]
        self.copy(part, part, pair, self.ring.sibling).wait()

    def plane(self):
        self.swap.wait()
        mine = self.mine
        own = self.total[pl.ds(pl.multiple_of(self.ring.core * 96, 96), 96), pl.ds(0, 576)]
        flat = own + self.from_core[:, pl.ds(0, 576)]
        high = flat.astype(BF16)
        low = (flat - high.astype(F32)).astype(BF16)
        placed = jnp.dot(
            jnp.concatenate([high, low], axis=0), self.unspread[...], preferred_element_type=F32
        )
        placed = placed[:96] + placed[96:]
        full = placed[:32] + pltpu.roll(placed[32:64], 1, 1) + pltpu.roll(placed[64:], 2, 1)
        for c in range(16):
            at, half = 4 * (c // 2), 896 * (c % 2)
            mine[c] = full[at : at + 4, half : half + 896]
        place = self.ring.place
        self.spread_plane(lambda other: mine.at[other], self.from_plane.at[place], 1)
        self.from_plane[place] = mine[place]

    def small_plane(self):
        place = self.ring.place
        self.spread_plane(lambda other: self.small.at[other], self.s_plane.at[place], 2)
        self.s_plane[place] = self.small[place]

    def rest(self):
        place, z = self.ring.place, self.ring.z

        def total(ref, count):
            value = ref[0]
            for j in range(1, count):
                value = value + ref[j]
            return value

        self.finish(self.from_plane, 0, 15, 1)
        self.from_z[z] = total(self.from_plane, 16)
        self.spread_z(self.from_z, 3)
        self.finish(self.s_plane, 0, 15, 2)
        self.s_z[z] = total(self.s_plane, 16)
        self.spread_z(self.s_z, 4)

        self.finish(self.from_z, 0, 7, 3)
        own = self.out.at[self.ours + place]
        self.out[self.ours + place] = total(self.from_z, 8)
        self.spread_plane(lambda other: own, own, 5)
        self.finish(self.s_z, 0, 7, 4)
        small = self.s_out.at[place]
        self.s_out[place] = total(self.s_z, 8)
        self.spread_plane(lambda other: small, small, 6)

        self.finish(self.out, 0, 15, 5)
        half = self.out.at[pl.ds(self.ours, 16)]
        hand = self.copy(half, half, 7, self.ring.sibling)
        hand.start()
        self.finish(self.s_out, 0, 15, 6)
        swap = self.copy(self.s_out, self.s_core, 8, self.ring.sibling)
        swap.start()
        swap.wait()
        both = self.s_out[...] + self.s_core[...]
        for c in range(16):
            at = 16 + c // 2
            self.out[32 + at // 7, pl.ds(2 * (c % 2), 2), pl.ds(128 * (at % 7), 128)] = both[c]
        hand.wait()


def picks():
    grad = np.zeros((2, 144, 128), np.float32)
    ahead = np.zeros((6, 54, 144), np.float32)
    for ox in range(3):
        for oz in range(3):
            for ch in range(2):
                for oy in range(3):
                    tap = 27 * ch + 9 * ox + 3 * oy + oz
                    for y in range(2):
                        grad[y, ((ox * 3 + oz) * 2 + ch) * 8 + 2 + y + oy, tap] = 1
                    for y in range(6):
                        ahead[y, tap, ((ox * 3 + oz) * 2 + ch) * 8 + y + oy] = 1
    return grad, ahead


def main_kernel(
    loss_scale,
    sc_hbm, vel_hbm, w_mix_hbm, spread_hbm, w_lift_hbm, ahead_hbm, b_lift_hbm, b_mix_hbm, w_out_hbm, b_out_hbm,
    unspread_hbm, pick_hbm,
    out,
    adv, sc, vel, w_mix, spread, w_lift, ahead, b_lift, b_mix, w_out, b_out, unspread, pick,
    load, lift_w, mix_w, back_w, out_w, outt_w, bias,
    net, tgt, halo, held, wide, seen, inc, gains,
    v3, lifted, slope1, mixed, slope2, cot, down, errors, total,
    from_core, mine, from_plane, from_z, small, s_plane, s_z, s_out, s_core,
    a_send, a_recv, b_send, b_recv, n_send, n_recv, c_send, c_recv, sums,
):
    pairs = (
        (sc_hbm, sc), (vel_hbm, vel), (w_mix_hbm, w_mix), (spread_hbm, spread), (w_lift_hbm, w_lift),
        (ahead_hbm, ahead), (b_lift_hbm, b_lift), (b_mix_hbm, b_mix), (w_out_hbm, w_out), (b_out_hbm, b_out),
        (unspread_hbm, unspread), (pick_hbm, pick),
    )
    loads = [pltpu.make_async_copy(*pair, load.at[j]) for j, pair in enumerate(pairs)]
    for copy in loads:
        copy.start()
    ring = Ring()
    prepared = Prepared(
        w_lift, b_lift, w_mix, b_mix, w_out, b_out, ahead, spread, lift_w, mix_w, back_w, out_w, outt_w, bias
    )

    def prepare_mix():
        for copy in loads[2:4]:
            copy.wait()
        prepared.mix_form()
        for copy in loads[:2]:
            copy.wait()

    def prepare_lift():
        for copy in loads[4:10]:
            copy.wait()
        prepared.lift_form()

    targets, sent = solver(
        ring, prepare_mix, prepare_lift, prepared.back_form,
        sc_hbm, sc, vel, adv, net, tgt, halo, held, wide, seen, inc, gains,
        a_send, a_recv, b_send, b_recv, n_send, n_recv, c_send, c_recv,
    )
    for copy in loads[10:]:
        copy.wait()
    summing = Summing(
        ring, total, unspread, out, from_core, mine, from_plane, from_z, small, s_plane, s_z, s_out, s_core, sums
    )
    network(
        loss_scale, targets, summing, net, tgt, prepared, pick,
        v3, lifted, slope1, mixed, slope2, cot, down, errors, total, small,
    )
    for copy in sent:
        copy.wait_send()
    for block in range(16):
        out[32 + block // 7, :, pl.ds(128 * (block % 7), 128)] = adv[pl.ds(4 * block, 4), :]
    summing.rest()


def finish_kernel(out, adv, mix, lift, liftbias, mixbias, out_grad, outbias):
    def block(at):
        return out[32 + at // 7, :, pl.ds(128 * (at % 7), 128)]

    for at in range(16):
        adv[pl.ds(4 * at, 4), :] = block(at)
    for r in range(16):
        mix[pl.ds(4 * r, 4), pl.ds(0, 896)] = out[2 * r]
        mix[pl.ds(4 * r, 4), pl.ds(896, 832)] = out[2 * r + 1][:, :832]
    small = jnp.concatenate([block(16 + at) for at in range(8)], axis=0)
    turned = small.T
    turned = jnp.concatenate([turned[:64], turned[64:]], axis=1)
    lift[...] = turned[:54]
    liftbias[...] = turned[54:55]
    mixbias[...] = turned[55:56]
    out_grad[...] = turned[56:58]
    outbias[...] = turned[58:59, :2]


def train(loss_scale, scalars, velocity, w_lift, b_lift, w_mix, b_mix, w_out, b_out):
    dma = pltpu.SemaphoreType.DMA
    hbm = pl.BlockSpec(memory_space=pltpu.HBM)
    pick, ahead = picks()
    spread = np.zeros((64, 9, 3, 9, 64), np.float32)
    for m in range(9):
        for i in range(64):
            spread[i, m, 0, m, i] = 1
    spread = spread.reshape(1728, 576)
    unspread = np.zeros((576, 1792), np.float32)
    unspread[:, :1728] = spread.T
    chunk = (4, 896)

    def vmem(*shape, dtype=F32):
        return pltpu.VMEM(shape, dtype)

    out = pl.pallas_call(
        functools.partial(main_kernel, loss_scale),
        out_shape=jax.ShapeDtypeStruct((36,) + chunk, F32),
        in_specs=[hbm] * 12,
        out_specs=VMEM,
        scratch_shapes=[
            vmem(64, 128),
            vmem(64, 128), vmem(192, 128), vmem(64, 1728, dtype=BF16), vmem(1728, 576, dtype=BF16),
            vmem(54, 64, dtype=BF16), vmem(6, 54, 144, dtype=BF16), vmem(1, 64), vmem(1, 64),
            vmem(2, 64, dtype=BF16), vmem(1, 2), vmem(576, 1792, dtype=BF16), vmem(2, 144, 128), dma((12,)),
            vmem(384, 144, dtype=BF16), vmem(192, 576, dtype=BF16), vmem(192, 576, dtype=BF16),
            vmem(16, 256, dtype=BF16), vmem(256, 16, dtype=BF16), vmem(2, 64, 128),
            vmem(38 * 16, 128), vmem(34 * 8, 128),
            vmem(2, 64, 128), vmem(2, 32, 128), vmem(2, 32, 128, dtype=BF16),
            vmem(10, 2, 32, 128, dtype=BF16), vmem(8, 32, 128), vmem(2, 32, 128),
            vmem(22, 48, 128, dtype=BF16), vmem(20, 384, 128, dtype=BF16), vmem(20, 128, 128),
            vmem(18, 256, 128, dtype=BF16), vmem(18, 256, 128), vmem(18, 256, 128, dtype=BF16),
            vmem(16, 128, 128, dtype=BF16), vmem(18, 16, 128, dtype=BF16), vmem(192, 640),
            vmem(96, 640), vmem(16, *chunk), vmem(16, *chunk), vmem(8, *chunk),
            vmem(16, 2, 128), vmem(16, 2, 128), vmem(8, 2, 128), vmem(16, 2, 128), vmem(16, 2, 128),
            dma, dma, dma, dma, dma, dma, dma, dma, dma((18,)),
        ],
        compiler_params=pltpu.CompilerParams(
            collective_id=0, has_side_effects=True, vmem_limit_bytes=VMEM_BYTES
        ),
        name="train",
    )(
        scalars, velocity, w_mix, jnp.asarray(spread, BF16), w_lift.T, jnp.asarray(ahead, BF16),
        b_lift[None], b_mix[None], w_out, b_out[None], jnp.asarray(unspread, BF16), jnp.asarray(pick),
    )
    shapes = ((64, 128), (64, 1728), (54, 64), (1, 64), (1, 64), (2, 64), (1, 2))
    return pl.pallas_call(
        finish_kernel,
        out_shape=tuple(jax.ShapeDtypeStruct(shape, F32) for shape in shapes),
        in_specs=[VMEM],
        out_specs=(VMEM,) * 7,
        compiler_params=pltpu.CompilerParams(vmem_limit_bytes=8 * 2**20),
        name="finish",
    )(out)


def on_device(scalars, velocity, w_lift, b_lift, w_mix, b_mix, w_out, b_out):
    total_cells = scalars.size * lax.axis_size("gx") * lax.axis_size("gy")
    loss_scale = 2.0 / math.sqrt(total_cells)
    adv, mix, lift, liftbias, mixbias, out_grad, outbias = train(
        loss_scale, scalars.reshape(64, 128), velocity.reshape(192, 128),
        w_lift, b_lift, w_mix, b_mix, w_out, b_out,
    )
    return (
        adv.reshape(scalars.shape), lift.T, liftbias[0], mix, mixbias[0], out_grad, outbias[0],
    )


def solution(mesh):
    cells = P("grp", None, ("gx", "gy"), None)
    in_specs = (cells, P(None, None, ("gx", "gy"), None)) + (P(),) * 6
    out_specs = (cells,) + (P(),) * 6
    return jax.shard_map(
        on_device, mesh=mesh, in_specs=in_specs, out_specs=out_specs, check_vma=False
    )
```

```python
import functools
import math

import jax
import jax.numpy as jnp
import numpy as np
from jax import lax
from jax.experimental import pallas as pl
from jax.experimental.pallas import tpu as pltpu
from jax.sharding import PartitionSpec as P

MESH = pl.DeviceIdType.MESH
F32 = jnp.float32
BF16 = jnp.bfloat16
VMEM = pl.BlockSpec(memory_space=pltpu.VMEM)
VMEM_BYTES = 62 * 2**20


def place():
    return lax.axis_index("grp"), lax.axis_index("gx") * 4 + lax.axis_index("gy")


def roll_z(value, step):
    lane = lax.broadcasted_iota(jnp.int32, value.shape, value.ndim - 1)
    edge = 0 if step > 0 else 127
    return jnp.where(lane % 128 == edge, 0.0, pltpu.roll(value, step % 128, value.ndim - 1))


def solver(
    ring, prepare_mix, prepare_lift, prepare_back,
    sc_hbm, sc, vel, adv, net, tgt,
    halo, held, wide, seen, inc, gains,
    a_send, a_recv, b_send, b_recv, n_send, n_recv, c_send, c_recv,
):
    g, s = place()
    diffusivity = jnp.where(g == 0, jnp.float32(0.08), jnp.float32(0.12))

    def device(step, field):
        other = lax.rem(s + step + 128, 128)
        return (field, other // 4, lax.rem(other, 4))

    partners = [(d, f) for d in (-2, 2, -1, 1, 0) for f in (1, 0) if (d, f) != (0, 0)]
    def partner(d, f):
        return device(d, g if f == 0 else 1 - g)

    barrier = pltpu.get_barrier_semaphore()
    ring.greet(barrier)
    for d, f in partners:
        pl.semaphore_signal(barrier, inc=1, device_id=partner(d, f), device_id_type=MESH)
    pl.semaphore_wait(barrier, len(partners) + 23)

    def send(src, dst, ssem, rsem, d, f):
        return pltpu.make_async_remote_copy(
            src, dst, ssem, rsem, device_id=partner(d, f), device_id_type=MESH
        )

    first = [
        send(sc_hbm, halo.at[0], a_send, a_recv, 1, 0),
        send(sc_hbm, halo.at[1], a_send, a_recv, -1, 0),
    ]
    first_all = send(halo, halo, a_send, a_recv, 1, 0)
    for copy in first:
        copy.start()

    prepare_mix()
    speed = [[vel[pl.ds(64 * d + y, 32, stride=2), :] for y in range(2)] for d in range(3)]
    row = lax.broadcasted_iota(jnp.int32, (32, 128), 0)

    def step(centre, below, above, y):
        plus_x = jnp.where(row == 31, 0.0, pltpu.roll(centre, 31, 0))
        minus_x = jnp.where(row == 0, 0.0, pltpu.roll(centre, 1, 0))
        plus_z = roll_z(centre, -1)
        minus_z = roll_z(centre, 1)
        laplace = plus_x + minus_x + above + below + plus_z + minus_z - 6.0 * centre
        advect = (
            speed[0][y] * (plus_x - minus_x)
            + speed[1][y] * (above - below)
            + speed[2][y] * (plus_z - minus_z)
        )
        return centre + diffusivity * laplace - 0.5 * advect

    own = [sc[pl.ds(y, 32, stride=2), :] for y in range(2)]
    first_all.wait_recv()
    below = jnp.where(s == 0, 0.0, halo[0, pl.ds(1, 32, stride=2), :])
    above = jnp.where(s == 127, 0.0, halo[1, pl.ds(0, 32, stride=2), :])
    stepped = [step(own[0], below, own[1], 0), step(own[1], own[0], above, 1)]
    for y in range(2):
        held[y] = stepped[y]
        wide[y] = stepped[y].astype(BF16)

    second = [
        send(held.at[1], gains.at[0], b_send, b_recv, 1, 0),
        send(held.at[0], gains.at[1], b_send, b_recv, -1, 0),
    ]
    second_all = send(gains, gains, b_send, b_recv, 1, 0)
    third = []
    for d, f in partners:
        slot = 2 * (2 - d) + g
        if abs(d) == 2:
            y = 1 if d > 0 else 0
            third.append(send(wide.at[y], seen.at[slot, y], n_send, n_recv, d, f))
        else:
            third.append(send(wide, seen.at[slot], n_send, n_recv, d, f))
    third_all = send(seen.at[pl.ds(0, 7)], seen.at[pl.ds(0, 7)], n_send, n_recv, 1, 0)
    for copy in second:
        copy.start()
    for copy in third:
        copy.start()
    for y in range(2):
        seen[4 + g, y] = wide[y]
    net[pl.ds(0, 48), :] = jnp.zeros((48, 128), F32)
    net[pl.ds(35 * 16, 48), :] = jnp.zeros((48, 128), F32)
    prepare_lift()
    prepare_back()
    second_all.wait_recv()
    below = jnp.where(s == 0, 0.0, gains[0])
    above = jnp.where(s == 127, 0.0, gains[1])
    advanced = [
        step(stepped[0], below, stepped[1], 0),
        step(stepped[1], stepped[0], above, 1),
    ]
    for y in range(2):
        adv[pl.ds(y, 32, stride=2), :] = advanced[y]
        inc[4 * g + 1 + y] = advanced[y] - stepped[y]
    for d, f in [(0, 1), (1, 0), (1, 1), (-1, 0), (-1, 1)]:
        if d == 0:
            part = inc.at[pl.ds(4 * g + 1, 2)]
            send(part, part, c_send, c_recv, d, f).start()
        elif d == 1:
            send(inc.at[4 * g + 2], inc.at[4 * g], c_send, c_recv, d, f).start()
        else:
            send(inc.at[4 * g + 1], inc.at[4 * g + 3], c_send, c_recv, d, f).start()

    fourth_all = send(inc.at[pl.ds(0, 6)], inc.at[pl.ds(0, 6)], c_send, c_recv, 1, 0)


    third_all.wait_recv()
    for field in range(2):
        for yy in range(8):
            slab, y = (yy + 1) // 2, (yy + 1) % 2
            y_at = 2 * s - 3 + yy
            inside = (y_at >= 0) & (y_at < 256)
            value = jnp.where(inside, seen[2 * slab + field, y].astype(F32), 0.0)
            net[pl.ds(48 + field * 8 + yy, 32, stride=16), :] = value

    def targets():
        fourth_all.wait_recv()
        tgt[pl.ds(0, 8), :] = jnp.zeros((8, 128), F32)
        tgt[pl.ds(33 * 8, 8), :] = jnp.zeros((8, 128), F32)
        for field in range(2):
            for yy in range(4):
                tgt[pl.ds(8 + (yy + 3) % 4 * 2 + field, 32, stride=8), :] = inc[4 * field + yy]

    return targets, (first_all, second_all, third_all, fourth_all)


def gelu_parts(v):
    c = math.sqrt(2.0 / math.pi)
    square = v * v
    t = jnp.tanh(v * (c + (c * 0.044715) * square))
    half = 0.5 + 0.5 * t
    value = v * half
    slope = half + (0.5 * v) * (1.0 - t * t) * (c + (3.0 * c * 0.044715) * square)
    return value, slope


def rows_dot(a, b):
    return lax.dot_general(a, b, (((1,), (1,)), ((), ())), preferred_element_type=F32)


class Prepared:
    def __init__(self, w_lift, b_lift, w_mix, b_mix, w_out, b_out, ahead, spread, lift, mix, back, out, outt, bias):
        self.__dict__.update(locals())

    def mix_form(self):
        wide = jnp.concatenate([self.w_mix[...].astype(F32), jnp.zeros((64, 64), F32)], axis=1)
        turned = [wide] + [pltpu.roll(wide, 1792 - oz, 1) for oz in (1, 2)]
        turned = jnp.concatenate([t[:, :1728] for t in turned], axis=0).astype(BF16)
        self.mix[...] = jnp.dot(turned, self.spread[...], preferred_element_type=F32).astype(BF16)

    def lift_form(self):
        flat = self.w_lift[...].astype(F32).T.astype(BF16)
        for y in range(6):
            band = jnp.dot(flat, self.ahead[y], preferred_element_type=F32)
            self.lift[pl.ds(64 * y, 64), :] = band.astype(BF16)
        for index, ref in enumerate((self.b_lift, self.b_mix)):
            self.bias[index] = jnp.broadcast_to(ref[...], (128, 64)).T
        four = jnp.concatenate([self.w_out[...].astype(F32)] * 4, axis=1)
        row = lax.broadcasted_iota(jnp.int32, (16, 256), 0)
        lane = lax.broadcasted_iota(jnp.int32, (16, 256), 1)
        both = jnp.where(row % 2 == 0, four[0:1], four[1:2])
        both = jnp.where(row // 2 == lane // 64, both, 0.0)
        self.out[...] = both.astype(BF16)
        self.outt[...] = both.T.astype(BF16)

    def back_form(self):
        flat = self.mix[...].astype(F32).T
        for oz in range(3):
            tiles = [flat[64 * m : 64 * m + 64, 64 * oz : 64 * oz + 64] for m in range(8, -1, -1)]
            self.back[pl.ds(64 * (2 - oz), 64), :] = jnp.concatenate(tiles, axis=1).astype(BF16)

def network(
    loss_scale, targets, summing, net, tgt, prepared, pick,
    v3, lifted, slope1, mixed, slope2, cot, down, errors, total, small_buf,
):
    g, s = place()
    x0 = g * 16

    def fill(x, _):
        rows = net[pl.ds(pl.multiple_of((x0 + x) * 16, 16), 16), :]
        v3[x, pl.ds(0, 16), :] = roll_z(rows, 1).astype(BF16)
        v3[x, pl.ds(16, 16), :] = rows.astype(BF16)
        v3[x, pl.ds(32, 16), :] = roll_z(rows, -1).astype(BF16)
        return 0

    lax.fori_loop(0, 22, fill, 0, unroll=11)

    def lift(x, _):
        seen = jnp.concatenate(
            [v3[pl.ds(2 * x, 3)].reshape(144, 128), v3[pl.ds(2 * x + 1, 3)].reshape(144, 128)], axis=1
        )
        pre = jnp.dot(prepared.lift[...], seen, preferred_element_type=F32)
        bias = jnp.concatenate([prepared.bias[0]] * 6, axis=0)
        for half in range(2):
            value, slope = gelu_parts(pre[:, half * 128 : half * 128 + 128] + bias)
            lifted[2 * x + half] = value.astype(BF16)
            slope1[2 * x + half] = slope[128:256]
        return 0

    lax.fori_loop(0, 10, lift, 0, unroll=5)

    def clear(ref, first_x, last_x, first_y, last_y):
        @pl.when(g == 0)
        def _():
            for x in first_x:
                ref[x] = jnp.zeros(ref.shape[1:], BF16)

        @pl.when(g == 1)
        def _():
            for x in last_x:
                ref[x] = jnp.zeros(ref.shape[1:], BF16)

        def wipe(rows):
            def body(x, _):
                ref[x, rows, :] = jnp.zeros((rows.size, 128), BF16)
                return 0
            lax.fori_loop(0, ref.shape[0], body, 0)

        @pl.when(s == 0)
        def _():
            wipe(first_y)

        @pl.when(s == 127)
        def _():
            wipe(last_y)

    clear(lifted, (0, 1), (18, 19), pl.ds(0, 128), pl.ds(256, 128))

    def summed_z(u):
        return roll_z(u[:64], 1) + u[64:128] + roll_z(u[128:], -1)

    def around(ref, x, first, rows):
        pieces = [ref[x + ox] for ox in range(3)]
        return jnp.concatenate(
            [
                jnp.concatenate([piece[64 * y : 64 * y + 192] for piece in pieces], axis=0)
                for y in range(first, first + rows)
            ],
            axis=1,
        )

    def mix(x, ys):
        seen = jnp.concatenate([around(lifted, x, y, 1) for y in ys], axis=1)
        u = jnp.dot(prepared.mix[...], seen, preferred_element_type=F32)
        for j, y in enumerate(ys):
            value, slope = gelu_parts(summed_z(u[:, 128 * j : 128 * j + 128]) + prepared.bias[1])
            mixed[x, pl.ds(64 * y, 64), :] = value.astype(BF16)
            slope2[x, pl.ds(64 * y, 64), :] = slope

    def mix_own(x, _):
        mix(x, (1, 2))
        return 0

    def mix_rim(x, _):
        mix(x, (3, 0))
        return 0

    def compare(xs, ys):
        width = 128 * len(xs)
        part = 0 if ys == (1, 2) else 128
        seen = jnp.concatenate(
            [
                jnp.concatenate([mixed[x, pl.ds(64 * y, 64), :] for y in ys], axis=0)
                for x in xs
            ],
            axis=1,
        )
        row = lax.broadcasted_iota(jnp.int32, (16, width), 0)
        bias = jnp.where(row % 2 == 0, prepared.b_out[:, 0:1], prepared.b_out[:, 1:2])
        predicted = jnp.dot(prepared.out[:, part : part + 128], seen, preferred_element_type=F32) + bias
        goal = jnp.concatenate(
            [tgt[pl.ds(pl.multiple_of((x0 + x) * 8, 8), 8), :] for x in xs], axis=1
        )
        goal = jnp.concatenate([goal, jnp.zeros((8, width), F32)], axis=0)
        error = (loss_scale * (predicted - goal)).astype(BF16)
        back = jnp.dot(prepared.outt[part : part + 128, :], error, preferred_element_type=F32)
        for j, x in enumerate(xs):
            for row_at, y in enumerate(ys):
                piece = back[64 * row_at : 64 * row_at + 64, 128 * j : 128 * j + 128]
                cot[x, pl.ds(64 * y, 64), :] = (piece * slope2[x, pl.ds(64 * y, 64), :]).astype(BF16)
        return error

    lax.fori_loop(1, 17, mix_own, 0, unroll=8)
    targets()
    for batch in range(2):
        xs = range(1 + 8 * batch, 9 + 8 * batch)
        error = compare(xs, (1, 2))
        for j, x in enumerate(xs):
            errors[x] = error[:, 128 * j : 128 * j + 128]
    total[...] = jnp.zeros_like(total)

    def mix_grad(x, mixbias):
        here = cot[x + 1, pl.ds(64, 128), :]
        mine = here.astype(F32)
        before = roll_z(mine, -1).astype(BF16)
        after = roll_z(mine, 1).astype(BF16)
        seen = around(lifted, x + 1, 1, 2)
        theirs = jnp.concatenate(
            [
                jnp.concatenate(
                    [
                        part[64 * y + 32 * half : 64 * y + 32 * half + 32]
                        for half in range(2)
                        for part in (before, here, after)
                    ],
                    axis=0,
                )
                for y in range(2)
            ],
            axis=1,
        )
        total[:, pl.ds(0, 576)] += rows_dot(theirs, seen)
        return mixbias + mine[:64] + mine[64:]

    mixbias = lax.fori_loop(0, 16, mix_grad, jnp.zeros((64, 128), F32), unroll=8)

    summing.begin()
    lax.fori_loop(1, 9, mix_rim, 0, unroll=8)
    summing.plane()
    lax.fori_loop(9, 17, mix_rim, 0, unroll=8)
    for x in (0, 17):
        mix(x, (1, 2, 3, 0))
    compare((0, 17), (1, 2))
    compare(range(0, 9), (3, 0))
    compare(range(9, 18), (3, 0))
    clear(cot, (0,), (17,), pl.ds(0, 64), pl.ds(192, 64))

    def backward(x, _):
        u = jnp.dot(prepared.back[...], around(cot, x, 0, 2), preferred_element_type=F32)
        back = jnp.concatenate([summed_z(u[:, :128]), summed_z(u[:, 128:])], axis=0)
        down[x] = (back * slope1[x + 2]).astype(BF16)
        return 0

    lax.fori_loop(0, 16, backward, 0, unroll=8)
    summing.along_z()

    liftbias = jnp.zeros((64, 128), F32)
    outbias = jnp.zeros((8, 128), F32)
    lift_total = jnp.zeros((128, 144), F32)
    out_total = jnp.zeros((128, 16), F32)
    for batch in range(4):
        xs = range(4 * batch, 4 * batch + 4)
        lows = [down[x] for x in xs]
        for low in lows:
            low = low.astype(F32)
            liftbias = liftbias + low[:64] + low[64:]
        ins = jnp.concatenate([v3[x + 2 : x + 5].reshape(144, 128) for x in xs], axis=1)
        lift_total += rows_dot(jnp.concatenate(lows, axis=1), ins)
        errs = [errors[x + 1] for x in xs]
        for err in errs:
            outbias = outbias + err.astype(F32)[:8]
        out_total += rows_dot(
            jnp.concatenate([mixed[x + 1, pl.ds(64, 128), :] for x in xs], axis=1),
            jnp.concatenate(errs, axis=1),
        )

    small = jnp.zeros((64, 128), F32)
    for y in range(2):
        small += jnp.dot(
            lift_total[64 * y : 64 * y + 64], pick[y],
            preferred_element_type=F32, precision=lax.Precision.HIGHEST,
        )
    lane = lax.broadcasted_iota(jnp.int32, (64, 128), 1)
    row = lax.broadcasted_iota(jnp.int32, (64, 128), 0)
    small = jnp.where(lane == 54, jnp.sum(liftbias, axis=1, keepdims=True), small)
    small = jnp.where(lane == 55, jnp.sum(mixbias, axis=1, keepdims=True), small)
    for k in range(2):
        piece = out_total[:64, k : k + 1] + out_total[64:, 2 + k : 3 + k]
        small = jnp.where(lane == 56 + k, piece, small)
    per_row = jnp.sum(outbias, axis=1, keepdims=True)
    pair = per_row[0:2] + per_row[2:4]
    for k in range(2):
        small = jnp.where((lane == 58) & (row == k), pair[k : k + 1], small)
    small = jnp.concatenate([small[:32, :64], small[32:, :64]], axis=1)
    for half in range(2):
        small_buf[half] = small[16 * half : 16 * half + 16]
    summing.small_plane()


class Ring:
    def __init__(self):
        y_lo = lax.axis_index("grp")
        gx = lax.axis_index("gx")
        gy = lax.axis_index("gy")
        self.z, x = lax.div(gx, 4), lax.rem(gx, 4)
        y_hi, core = lax.div(gy, 2), lax.rem(gy, 2)
        self.core, self.place = core, x * 4 + y_hi * 2 + y_lo
        self.sibling = (y_lo, gx, y_hi * 2 + 1 - core)

        def along(at, size):
            steps = [jnp.where(at + j >= size, at + j - size, at + j) for j in range(1, size)]
            return [(0, at)] + [(min(j, size - j), step) for j, step in enumerate(steps, 1)]

        plane = []
        for far_x, to_x in along(x, 4):
            for far_y, to_y in along(y_hi * 2 + y_lo, 4):
                to = (lax.rem(to_y, 2), self.z * 4 + to_x, lax.div(to_y, 2) * 2 + core)
                plane.append((far_x + far_y, to_x * 4 + to_y, to))
        rows = [(far, to_z, (y_lo, to_z * 4 + x, gy)) for far, to_z in along(self.z, 8)]
        self.plane = sorted(plane, key=lambda entry: -entry[0])[:-1]
        self.rows = sorted(rows, key=lambda entry: -entry[0])[:-1]

    def greet(self, barrier):
        for _, _, to in self.rows + self.plane:
            pl.semaphore_signal(barrier, inc=1, device_id=to, device_id_type=MESH)
        pl.semaphore_signal(barrier, inc=1, device_id=self.sibling, device_id_type=MESH)


class Summing:
    def __init__(self, ring, total, unspread, out, from_core, mine, from_plane, from_z, small, s_mine, s_plane, s_z, s_out, s_core, sems):
        self.__dict__.update(locals())
        self.ours = pl.multiple_of(ring.core * 16, 16)

    def copy(self, src, dst, pair, device):
        return pltpu.make_async_remote_copy(
            src, dst, self.sems.at[2 * pair], self.sems.at[2 * pair + 1], device_id=device, device_id_type=MESH
        )

    def begin(self):
        self.swap = self.copy(
            self.total.at[pl.ds(pl.multiple_of((1 - self.ring.core) * 96, 96), 96)], self.from_core, 0, self.ring.sibling
        )
        self.swap.start()

    def spread_plane(self, source, target, pair):
        for _, other, to in self.ring.plane:
            self.copy(source(other), target, pair, to).start()

    def spread_z(self, ref, pair):
        own = ref.at[self.ring.z]
        for _, _, to in self.ring.rows:
            self.copy(own, own, pair, to).start()

    def finish(self, ref, first, count, pair):
        part = ref.at[pl.ds(first, count)]
        self.copy(part, part, pair, self.ring.sibling).wait()

    def plane(self):
        self.swap.wait()
        mine = self.mine
        own = self.total[pl.ds(pl.multiple_of(self.ring.core * 96, 96), 96), pl.ds(0, 576)]
        flat = own + self.from_core[:, pl.ds(0, 576)]
        high = flat.astype(BF16)
        low = (flat - high.astype(F32)).astype(BF16)
        placed = jnp.dot(
            jnp.concatenate([high, low], axis=0), self.unspread[...], preferred_element_type=F32
        )
        placed = placed[:96] + placed[96:]
        full = placed[:32] + pltpu.roll(placed[32:64], 1, 1) + pltpu.roll(placed[64:], 2, 1)
        for c in range(16):
            at, half = 4 * (c // 2), 896 * (c % 2)
            mine[c] = full[at : at + 4, half : half + 896]
        place = self.ring.place
        self.spread_plane(lambda other: mine.at[other], self.from_plane.at[place], 1)
        self.from_plane[place] = mine[place]

    def small_plane(self):
        place, core = self.ring.place, self.ring.core
        swap = self.copy(self.small.at[1 - core], self.s_core, 8, self.ring.sibling)
        swap.start()
        swap.wait()
        self.s_mine[...] = self.small[core] + self.s_core[...]
        self.spread_plane(lambda other: self.s_mine, self.s_plane.at[place], 2)
        self.s_plane[place] = self.s_mine[...]

    def added(self, ref, count):
        value = ref[0]
        for j in range(1, count):
            value = value + ref[j]
        return value

    def along_z(self):
        self.finish(self.from_plane, 0, 15, 1)
        self.from_z[self.ring.z] = self.added(self.from_plane, 16)
        self.spread_z(self.from_z, 3)

    def rest(self):
        place, z = self.ring.place, self.ring.z
        self.finish(self.from_z, 0, 7, 3)
        own = self.out.at[self.ours + place]
        self.out[self.ours + place] = self.added(self.from_z, 8)
        self.spread_plane(lambda other: own, own, 5)
        self.finish(self.s_plane, 0, 15, 2)
        self.s_z[z] = self.added(self.s_plane, 16)
        self.spread_z(self.s_z, 4)

        self.finish(self.out, 0, 15, 5)
        half = self.out.at[pl.ds(self.ours, 16)]
        hand = self.copy(half, half, 7, self.ring.sibling)
        hand.start()
        self.finish(self.s_z, 0, 7, 4)
        core = self.ring.core
        self.s_out[core] = self.added(self.s_z, 8)
        part = self.s_out.at[core]
        give = self.copy(part, part, 6, self.ring.sibling)
        give.start()
        give.wait()
        for block in range(8):
            at = 16 + block
            rows = self.s_out[block // 4, pl.ds(4 * (block % 4), 4), :]
            self.out[32 + at // 7, :, pl.ds(128 * (at % 7), 128)] = rows
        hand.wait()


def picks():
    grad = np.zeros((2, 144, 128), np.float32)
    ahead = np.zeros((6, 54, 144), np.float32)
    for ox in range(3):
        for oz in range(3):
            for ch in range(2):
                for oy in range(3):
                    tap = 27 * ch + 9 * ox + 3 * oy + oz
                    for y in range(2):
                        grad[y, ((ox * 3 + oz) * 2 + ch) * 8 + 2 + y + oy, tap] = 1
                    for y in range(6):
                        ahead[y, tap, ((ox * 3 + oz) * 2 + ch) * 8 + y + oy] = 1
    return grad, ahead


def main_kernel(
    loss_scale,
    sc_hbm, vel_hbm, w_mix_hbm, spread_hbm, w_lift_hbm, ahead_hbm, b_lift_hbm, b_mix_hbm, w_out_hbm, b_out_hbm,
    unspread_hbm, pick_hbm,
    out,
    adv, sc, vel, w_mix, spread, w_lift, ahead, b_lift, b_mix, w_out, b_out, unspread, pick,
    load, lift_w, mix_w, back_w, out_w, outt_w, bias,
    net, tgt, halo, held, wide, seen, inc, gains,
    v3, lifted, slope1, mixed, slope2, cot, down, errors, total,
    from_core, mine, from_plane, from_z, small, s_mine, s_plane, s_z, s_out, s_core,
    a_send, a_recv, b_send, b_recv, n_send, n_recv, c_send, c_recv, sums,
):
    pairs = (
        (sc_hbm, sc), (vel_hbm, vel), (w_mix_hbm, w_mix), (spread_hbm, spread), (w_lift_hbm, w_lift),
        (ahead_hbm, ahead), (b_lift_hbm, b_lift), (b_mix_hbm, b_mix), (w_out_hbm, w_out), (b_out_hbm, b_out),
        (unspread_hbm, unspread), (pick_hbm, pick),
    )
    loads = [pltpu.make_async_copy(*pair, load.at[j]) for j, pair in enumerate(pairs)]
    for copy in loads:
        copy.start()
    ring = Ring()
    prepared = Prepared(
        w_lift, b_lift, w_mix, b_mix, w_out, b_out, ahead, spread, lift_w, mix_w, back_w, out_w, outt_w, bias
    )

    def prepare_mix():
        for copy in loads[2:4]:
            copy.wait()
        prepared.mix_form()
        for copy in loads[:2]:
            copy.wait()

    def prepare_lift():
        for copy in loads[4:10]:
            copy.wait()
        prepared.lift_form()

    targets, sent = solver(
        ring, prepare_mix, prepare_lift, prepared.back_form,
        sc_hbm, sc, vel, adv, net, tgt, halo, held, wide, seen, inc, gains,
        a_send, a_recv, b_send, b_recv, n_send, n_recv, c_send, c_recv,
    )
    for copy in loads[10:]:
        copy.wait()
    summing = Summing(
        ring, total, unspread, out, from_core, mine, from_plane, from_z, small, s_mine, s_plane, s_z, s_out, s_core, sums
    )
    network(
        loss_scale, targets, summing, net, tgt, prepared, pick,
        v3, lifted, slope1, mixed, slope2, cot, down, errors, total, small,
    )
    for copy in sent:
        copy.wait_send()
    for block in range(16):
        out[32 + block // 7, :, pl.ds(128 * (block % 7), 128)] = adv[pl.ds(4 * block, 4), :]
    summing.rest()


def finish_kernel(out, adv, mix, lift, liftbias, mixbias, out_grad, outbias):
    def block(at):
        return out[32 + at // 7, :, pl.ds(128 * (at % 7), 128)]

    for at in range(16):
        adv[pl.ds(4 * at, 4), :] = block(at)
    for r in range(16):
        mix[pl.ds(4 * r, 4), pl.ds(0, 896)] = out[2 * r]
        mix[pl.ds(4 * r, 4), pl.ds(896, 832)] = out[2 * r + 1][:, :832]
    small = jnp.concatenate([block(16 + at) for at in range(8)], axis=0)
    turned = small.T
    turned = jnp.concatenate([turned[:64], turned[64:]], axis=1)
    lift[...] = turned[:54]
    liftbias[...] = turned[54:55]
    mixbias[...] = turned[55:56]
    out_grad[...] = turned[56:58]
    outbias[...] = turned[58:59, :2]


def train(loss_scale, scalars, velocity, w_lift, b_lift, w_mix, b_mix, w_out, b_out):
    dma = pltpu.SemaphoreType.DMA
    hbm = pl.BlockSpec(memory_space=pltpu.HBM)
    pick, ahead = picks()
    spread = np.zeros((64, 9, 3, 9, 64), np.float32)
    for m in range(9):
        for i in range(64):
            spread[i, m, 0, m, i] = 1
    spread = spread.reshape(1728, 576)
    unspread = np.zeros((576, 1792), np.float32)
    unspread[:, :1728] = spread.T
    chunk = (4, 896)

    def vmem(*shape, dtype=F32):
        return pltpu.VMEM(shape, dtype)

    out = pl.pallas_call(
        functools.partial(main_kernel, loss_scale),
        out_shape=jax.ShapeDtypeStruct((36,) + chunk, F32),
        in_specs=[hbm] * 12,
        out_specs=VMEM,
        scratch_shapes=[
            vmem(64, 128),
            vmem(64, 128), vmem(192, 128), vmem(64, 1728, dtype=BF16), vmem(1728, 576, dtype=BF16),
            vmem(54, 64, dtype=BF16), vmem(6, 54, 144, dtype=BF16), vmem(1, 64), vmem(1, 64),
            vmem(2, 64, dtype=BF16), vmem(1, 2), vmem(576, 1792, dtype=BF16), vmem(2, 144, 128), dma((12,)),
            vmem(384, 144, dtype=BF16), vmem(192, 576, dtype=BF16), vmem(192, 576, dtype=BF16),
            vmem(16, 256, dtype=BF16), vmem(256, 16, dtype=BF16), vmem(2, 64, 128),
            vmem(38 * 16, 128), vmem(34 * 8, 128),
            vmem(2, 64, 128), vmem(2, 32, 128), vmem(2, 32, 128, dtype=BF16),
            vmem(10, 2, 32, 128, dtype=BF16), vmem(8, 32, 128), vmem(2, 32, 128),
            vmem(22, 48, 128, dtype=BF16), vmem(20, 384, 128, dtype=BF16), vmem(20, 128, 128),
            vmem(18, 256, 128, dtype=BF16), vmem(18, 256, 128), vmem(18, 256, 128, dtype=BF16),
            vmem(16, 128, 128, dtype=BF16), vmem(18, 16, 128, dtype=BF16), vmem(192, 640),
            vmem(96, 640), vmem(16, *chunk), vmem(16, *chunk), vmem(8, *chunk),
            vmem(2, 16, 128), vmem(16, 128), vmem(16, 16, 128), vmem(8, 16, 128), vmem(2, 16, 128), vmem(16, 128),
            dma, dma, dma, dma, dma, dma, dma, dma, dma((18,)),
        ],
        compiler_params=pltpu.CompilerParams(
            collective_id=0, has_side_effects=True, vmem_limit_bytes=VMEM_BYTES
        ),
        name="train",
    )(
        scalars, velocity, w_mix, jnp.asarray(spread, BF16), w_lift.T, jnp.asarray(ahead, BF16),
        b_lift[None], b_mix[None], w_out, b_out[None], jnp.asarray(unspread, BF16), jnp.asarray(pick),
    )
    shapes = ((64, 128), (64, 1728), (54, 64), (1, 64), (1, 64), (2, 64), (1, 2))
    return pl.pallas_call(
        finish_kernel,
        out_shape=tuple(jax.ShapeDtypeStruct(shape, F32) for shape in shapes),
        in_specs=[VMEM],
        out_specs=(VMEM,) * 7,
        compiler_params=pltpu.CompilerParams(vmem_limit_bytes=8 * 2**20),
        name="finish",
    )(out)


def on_device(scalars, velocity, w_lift, b_lift, w_mix, b_mix, w_out, b_out):
    total_cells = scalars.size * lax.axis_size("gx") * lax.axis_size("gy")
    loss_scale = 2.0 / math.sqrt(total_cells)
    adv, mix, lift, liftbias, mixbias, out_grad, outbias = train(
        loss_scale, scalars.reshape(64, 128), velocity.reshape(192, 128),
        w_lift, b_lift, w_mix, b_mix, w_out, b_out,
    )
    return (
        adv.reshape(scalars.shape), lift.T, liftbias[0], mix, mixbias[0], out_grad, outbias[0],
    )


def solution(mesh):
    cells = P("grp", None, ("gx", "gy"), None)
    in_specs = (cells, P(None, None, ("gx", "gy"), None)) + (P(),) * 6
    out_specs = (cells,) + (P(),) * 6
    return jax.shard_map(
        on_device, mesh=mesh, in_specs=in_specs, out_specs=out_specs, check_vma=False
    )
```

```python
import functools
import math

import jax
import jax.numpy as jnp
import numpy as np
from jax import lax
from jax.experimental import pallas as pl
from jax.experimental.pallas import tpu as pltpu
from jax.sharding import PartitionSpec as P

MESH = pl.DeviceIdType.MESH
F32 = jnp.float32
BF16 = jnp.bfloat16
VMEM = pl.BlockSpec(memory_space=pltpu.VMEM)
VMEM_BYTES = 62 * 2**20


def place():
    return lax.axis_index("grp"), lax.axis_index("gx") * 4 + lax.axis_index("gy")


def roll_z(value, step):
    lane = lax.broadcasted_iota(jnp.int32, value.shape, value.ndim - 1)
    edge = 0 if step > 0 else 127
    return jnp.where(lane % 128 == edge, 0.0, pltpu.roll(value, step % 128, value.ndim - 1))


def solver(
    ring, prepare_mix, prepare_lift, prepare_back,
    sc_hbm, sc, vel, adv, net, tgt,
    halo, held, wide, seen, inc, gains,
    a_send, a_recv, b_send, b_recv, n_send, n_recv, c_send, c_recv,
):
    g, s = place()
    diffusivity = jnp.where(g == 0, jnp.float32(0.08), jnp.float32(0.12))

    def device(step, field):
        other = lax.rem(s + step + 128, 128)
        return (field, other // 4, lax.rem(other, 4))

    partners = [(d, f) for d in (-2, 2, -1, 1, 0) for f in (1, 0) if (d, f) != (0, 0)]
    def partner(d, f):
        return device(d, g if f == 0 else 1 - g)

    barrier = pltpu.get_barrier_semaphore()
    ring.greet(barrier)
    for d, f in partners:
        pl.semaphore_signal(barrier, inc=1, device_id=partner(d, f), device_id_type=MESH)
    pl.semaphore_wait(barrier, len(partners) + 23)

    def send(src, dst, ssem, rsem, d, f):
        return pltpu.make_async_remote_copy(
            src, dst, ssem, rsem, device_id=partner(d, f), device_id_type=MESH
        )

    first = [
        send(sc_hbm, halo.at[0], a_send, a_recv, 1, 0),
        send(sc_hbm, halo.at[1], a_send, a_recv, -1, 0),
    ]
    first_all = send(halo, halo, a_send, a_recv, 1, 0)
    for copy in first:
        copy.start()

    prepare_mix()
    speed = [[vel[pl.ds(64 * d + y, 32, stride=2), :] for y in range(2)] for d in range(3)]
    row = lax.broadcasted_iota(jnp.int32, (32, 128), 0)

    def step(centre, below, above, y):
        plus_x = jnp.where(row == 31, 0.0, pltpu.roll(centre, 31, 0))
        minus_x = jnp.where(row == 0, 0.0, pltpu.roll(centre, 1, 0))
        plus_z = roll_z(centre, -1)
        minus_z = roll_z(centre, 1)
        laplace = plus_x + minus_x + above + below + plus_z + minus_z - 6.0 * centre
        advect = (
            speed[0][y] * (plus_x - minus_x)
            + speed[1][y] * (above - below)
            + speed[2][y] * (plus_z - minus_z)
        )
        return centre + diffusivity * laplace - 0.5 * advect

    own = [sc[pl.ds(y, 32, stride=2), :] for y in range(2)]
    first_all.wait_recv()
    below = jnp.where(s == 0, 0.0, halo[0, pl.ds(1, 32, stride=2), :])
    above = jnp.where(s == 127, 0.0, halo[1, pl.ds(0, 32, stride=2), :])
    stepped = [step(own[0], below, own[1], 0), step(own[1], own[0], above, 1)]
    for y in range(2):
        held[y] = stepped[y]
        wide[y] = stepped[y].astype(BF16)

    second = [
        send(held.at[1], gains.at[0], b_send, b_recv, 1, 0),
        send(held.at[0], gains.at[1], b_send, b_recv, -1, 0),
    ]
    second_all = send(gains, gains, b_send, b_recv, 1, 0)
    third = []
    for d, f in partners:
        slot = 2 * (2 - d) + g
        if abs(d) == 2:
            y = 1 if d > 0 else 0
            third.append(send(wide.at[y], seen.at[slot, y], n_send, n_recv, d, f))
        else:
            third.append(send(wide, seen.at[slot], n_send, n_recv, d, f))
    third_all = send(seen.at[pl.ds(0, 7)], seen.at[pl.ds(0, 7)], n_send, n_recv, 1, 0)
    for copy in second:
        copy.start()
    for copy in third:
        copy.start()
    for y in range(2):
        seen[4 + g, y] = wide[y]
    net[pl.ds(0, 48), :] = jnp.zeros((48, 128), F32)
    net[pl.ds(35 * 16, 48), :] = jnp.zeros((48, 128), F32)
    prepare_lift()
    prepare_back()
    second_all.wait_recv()
    below = jnp.where(s == 0, 0.0, gains[0])
    above = jnp.where(s == 127, 0.0, gains[1])
    advanced = [
        step(stepped[0], below, stepped[1], 0),
        step(stepped[1], stepped[0], above, 1),
    ]
    for y in range(2):
        adv[pl.ds(y, 32, stride=2), :] = advanced[y]
        inc[4 * g + 1 + y] = advanced[y] - stepped[y]
    for d, f in [(0, 1), (1, 0), (1, 1), (-1, 0), (-1, 1)]:
        if d == 0:
            part = inc.at[pl.ds(4 * g + 1, 2)]
            send(part, part, c_send, c_recv, d, f).start()
        elif d == 1:
            send(inc.at[4 * g + 2], inc.at[4 * g], c_send, c_recv, d, f).start()
        else:
            send(inc.at[4 * g + 1], inc.at[4 * g + 3], c_send, c_recv, d, f).start()

    fourth_all = send(inc.at[pl.ds(0, 6)], inc.at[pl.ds(0, 6)], c_send, c_recv, 1, 0)


    third_all.wait_recv()
    for field in range(2):
        for yy in range(8):
            slab, y = (yy + 1) // 2, (yy + 1) % 2
            y_at = 2 * s - 3 + yy
            inside = (y_at >= 0) & (y_at < 256)
            value = jnp.where(inside, seen[2 * slab + field, y].astype(F32), 0.0)
            net[pl.ds(48 + field * 8 + yy, 32, stride=16), :] = value

    def targets():
        fourth_all.wait_recv()
        tgt[pl.ds(0, 8), :] = jnp.zeros((8, 128), F32)
        tgt[pl.ds(33 * 8, 8), :] = jnp.zeros((8, 128), F32)
        for field in range(2):
            for yy in range(4):
                tgt[pl.ds(8 + (yy + 3) % 4 * 2 + field, 32, stride=8), :] = inc[4 * field + yy]

    return targets, (first_all, second_all, third_all, fourth_all)


def gelu_parts(v):
    c = math.sqrt(2.0 / math.pi)
    square = v * v
    t = jnp.tanh(v * (c + (c * 0.044715) * square))
    half = 0.5 + 0.5 * t
    value = v * half
    slope = half + (0.5 * v) * (1.0 - t * t) * (c + (3.0 * c * 0.044715) * square)
    return value, slope


def rows_dot(a, b):
    return lax.dot_general(a, b, (((1,), (1,)), ((), ())), preferred_element_type=F32)


class Prepared:
    def __init__(self, w_lift, b_lift, w_mix, b_mix, w_out, b_out, ahead, spread, lift, mix, back, out, outt, bias):
        self.__dict__.update(locals())

    def mix_form(self):
        wide = jnp.concatenate([self.w_mix[...].astype(F32), jnp.zeros((64, 64), F32)], axis=1)
        turned = [wide] + [pltpu.roll(wide, 1792 - oz, 1) for oz in (1, 2)]
        turned = jnp.concatenate([t[:, :1728] for t in turned], axis=0).astype(BF16)
        self.mix[...] = jnp.dot(turned, self.spread[...], preferred_element_type=F32).astype(BF16)

    def lift_form(self):
        flat = self.w_lift[...].astype(F32).T.astype(BF16)
        for y in range(6):
            band = jnp.dot(flat, self.ahead[y], preferred_element_type=F32)
            self.lift[pl.ds(64 * y, 64), :] = band.astype(BF16)
        for index, ref in enumerate((self.b_lift, self.b_mix)):
            self.bias[index] = jnp.broadcast_to(ref[...], (128, 64)).T
        four = jnp.concatenate([self.w_out[...].astype(F32)] * 4, axis=1)
        row = lax.broadcasted_iota(jnp.int32, (16, 256), 0)
        lane = lax.broadcasted_iota(jnp.int32, (16, 256), 1)
        both = jnp.where(row % 2 == 0, four[0:1], four[1:2])
        both = jnp.where(row // 2 == lane // 64, both, 0.0)
        self.out[...] = both.astype(BF16)
        self.outt[...] = both.T.astype(BF16)

    def back_form(self):
        flat = self.mix[...].astype(F32).T
        for oz in range(3):
            tiles = [flat[64 * m : 64 * m + 64, 64 * oz : 64 * oz + 64] for m in range(8, -1, -1)]
            self.back[pl.ds(64 * (2 - oz), 64), :] = jnp.concatenate(tiles, axis=1).astype(BF16)

def network(
    loss_scale, targets, summing, net, tgt, prepared, pick,
    v3, lifted, slope1, mixed, slope2, cot, down, errors, total, small_buf,
):
    g, s = place()
    x0 = g * 16

    def fill(x, _):
        rows = net[pl.ds(pl.multiple_of((x0 + x) * 16, 16), 16), :]
        v3[x, pl.ds(0, 16), :] = roll_z(rows, 1).astype(BF16)
        v3[x, pl.ds(16, 16), :] = rows.astype(BF16)
        v3[x, pl.ds(32, 16), :] = roll_z(rows, -1).astype(BF16)
        return 0

    lax.fori_loop(0, 22, fill, 0, unroll=11)

    def lift(x, _):
        seen = jnp.concatenate(
            [v3[pl.ds(2 * x, 3)].reshape(144, 128), v3[pl.ds(2 * x + 1, 3)].reshape(144, 128)], axis=1
        )
        pre = jnp.dot(prepared.lift[...], seen, preferred_element_type=F32)
        bias = jnp.concatenate([prepared.bias[0]] * 6, axis=0)
        for half in range(2):
            value, slope = gelu_parts(pre[:, half * 128 : half * 128 + 128] + bias)
            lifted[2 * x + half] = value.astype(BF16)
            slope1[2 * x + half] = slope[128:256]
        return 0

    lax.fori_loop(0, 10, lift, 0, unroll=5)

    def clear(ref, first_x, last_x, first_y, last_y):
        @pl.when(g == 0)
        def _():
            for x in first_x:
                ref[x] = jnp.zeros(ref.shape[1:], BF16)

        @pl.when(g == 1)
        def _():
            for x in last_x:
                ref[x] = jnp.zeros(ref.shape[1:], BF16)

        def wipe(rows):
            def body(x, _):
                ref[x, rows, :] = jnp.zeros((rows.size, 128), BF16)
                return 0
            lax.fori_loop(0, ref.shape[0], body, 0)

        @pl.when(s == 0)
        def _():
            wipe(first_y)

        @pl.when(s == 127)
        def _():
            wipe(last_y)

    clear(lifted, (0, 1), (18, 19), pl.ds(0, 128), pl.ds(256, 128))

    def summed_z(u):
        return roll_z(u[:64], 1) + u[64:128] + roll_z(u[128:], -1)

    def around(ref, x, first, rows):
        pieces = [ref[x + ox] for ox in range(3)]
        return jnp.concatenate(
            [
                jnp.concatenate([piece[64 * y : 64 * y + 192] for piece in pieces], axis=0)
                for y in range(first, first + rows)
            ],
            axis=1,
        )

    def mix(x, ys):
        seen = jnp.concatenate([around(lifted, x, y, 1) for y in ys], axis=1)
        u = jnp.dot(prepared.mix[...], seen, preferred_element_type=F32)
        for j, y in enumerate(ys):
            value, slope = gelu_parts(summed_z(u[:, 128 * j : 128 * j + 128]) + prepared.bias[1])
            mixed[x, pl.ds(64 * y, 64), :] = value.astype(BF16)
            slope2[x, pl.ds(64 * y, 64), :] = slope

    def mix_own(x, _):
        mix(x, (1, 2))
        return 0

    def mix_rim(x, _):
        mix(x, (3, 0))
        return 0

    def compare(xs, ys):
        width = 128 * len(xs)
        part = 0 if ys == (1, 2) else 128
        seen = jnp.concatenate(
            [
                jnp.concatenate([mixed[x, pl.ds(64 * y, 64), :] for y in ys], axis=0)
                for x in xs
            ],
            axis=1,
        )
        row = lax.broadcasted_iota(jnp.int32, (16, width), 0)
        bias = jnp.where(row % 2 == 0, prepared.b_out[:, 0:1], prepared.b_out[:, 1:2])
        predicted = jnp.dot(prepared.out[:, part : part + 128], seen, preferred_element_type=F32) + bias
        goal = jnp.concatenate(
            [tgt[pl.ds(pl.multiple_of((x0 + x) * 8, 8), 8), :] for x in xs], axis=1
        )
        goal = jnp.concatenate([goal, jnp.zeros((8, width), F32)], axis=0)
        error = (loss_scale * (predicted - goal)).astype(BF16)
        back = jnp.dot(prepared.outt[part : part + 128, :], error, preferred_element_type=F32)
        for j, x in enumerate(xs):
            for row_at, y in enumerate(ys):
                piece = back[64 * row_at : 64 * row_at + 64, 128 * j : 128 * j + 128]
                cot[x, pl.ds(64 * y, 64), :] = (piece * slope2[x, pl.ds(64 * y, 64), :]).astype(BF16)
        return error

    lax.fori_loop(1, 17, mix_own, 0, unroll=8)
    targets()
    for batch in range(2):
        xs = range(1 + 8 * batch, 9 + 8 * batch)
        error = compare(xs, (1, 2))
        for j, x in enumerate(xs):
            errors[x] = error[:, 128 * j : 128 * j + 128]
    total[...] = jnp.zeros_like(total)

    def mix_grad(x, mixbias):
        here = cot[x + 1, pl.ds(64, 128), :]
        mine = here.astype(F32)
        before = roll_z(mine, -1).astype(BF16)
        after = roll_z(mine, 1).astype(BF16)
        seen = around(lifted, x + 1, 1, 2)
        theirs = jnp.concatenate(
            [
                jnp.concatenate(
                    [
                        part[64 * y + 32 * half : 64 * y + 32 * half + 32]
                        for half in range(2)
                        for part in (before, here, after)
                    ],
                    axis=0,
                )
                for y in range(2)
            ],
            axis=1,
        )
        total[:, pl.ds(0, 576)] += rows_dot(theirs, seen)
        return mixbias + mine[:64] + mine[64:]

    mixbias = lax.fori_loop(0, 16, mix_grad, jnp.zeros((64, 128), F32), unroll=8)

    summing.begin()
    lax.fori_loop(1, 9, mix_rim, 0, unroll=8)
    summing.plane()
    lax.fori_loop(9, 17, mix_rim, 0, unroll=8)
    for x in (0, 17):
        mix(x, (1, 2, 3, 0))
    compare((0, 17), (1, 2))
    compare(range(0, 9), (3, 0))
    compare(range(9, 18), (3, 0))
    clear(cot, (0,), (17,), pl.ds(0, 64), pl.ds(192, 64))

    def backward(x, _):
        u = jnp.dot(prepared.back[...], around(cot, x, 0, 2), preferred_element_type=F32)
        back = jnp.concatenate([summed_z(u[:, :128]), summed_z(u[:, 128:])], axis=0)
        down[x] = (back * slope1[x + 2]).astype(BF16)
        return 0

    lax.fori_loop(0, 16, backward, 0, unroll=8)
    summing.along_z()

    liftbias = jnp.zeros((64, 128), F32)
    outbias = jnp.zeros((8, 128), F32)
    lift_total = jnp.zeros((128, 144), F32)
    out_total = jnp.zeros((128, 16), F32)
    for batch in range(4):
        xs = range(4 * batch, 4 * batch + 4)
        lows = [down[x] for x in xs]
        for low in lows:
            low = low.astype(F32)
            liftbias = liftbias + low[:64] + low[64:]
        ins = jnp.concatenate([v3[x + 2 : x + 5].reshape(144, 128) for x in xs], axis=1)
        lift_total += rows_dot(jnp.concatenate(lows, axis=1), ins)
        errs = [errors[x + 1] for x in xs]
        for err in errs:
            outbias = outbias + err.astype(F32)[:8]
        out_total += rows_dot(
            jnp.concatenate([mixed[x + 1, pl.ds(64, 128), :] for x in xs], axis=1),
            jnp.concatenate(errs, axis=1),
        )

    small = jnp.zeros((64, 128), F32)
    for y in range(2):
        small += jnp.dot(
            lift_total[64 * y : 64 * y + 64], pick[y],
            preferred_element_type=F32, precision=lax.Precision.HIGHEST,
        )
    lane = lax.broadcasted_iota(jnp.int32, (64, 128), 1)
    row = lax.broadcasted_iota(jnp.int32, (64, 128), 0)
    small = jnp.where(lane == 54, jnp.sum(liftbias, axis=1, keepdims=True), small)
    small = jnp.where(lane == 55, jnp.sum(mixbias, axis=1, keepdims=True), small)
    for k in range(2):
        piece = out_total[:64, k : k + 1] + out_total[64:, 2 + k : 3 + k]
        small = jnp.where(lane == 56 + k, piece, small)
    per_row = jnp.sum(outbias, axis=1, keepdims=True)
    pair = per_row[0:2] + per_row[2:4]
    for k in range(2):
        small = jnp.where((lane == 58) & (row == k), pair[k : k + 1], small)
    small_buf[...] = jnp.concatenate([small[:32, :64], small[32:, :64]], axis=1)
    summing.small_plane()


class Ring:
    def __init__(self):
        y_lo = lax.axis_index("grp")
        gx = lax.axis_index("gx")
        gy = lax.axis_index("gy")
        self.z, x = lax.div(gx, 4), lax.rem(gx, 4)
        y_hi, core = lax.div(gy, 2), lax.rem(gy, 2)
        self.core, self.place = core, x * 4 + y_hi * 2 + y_lo
        self.sibling = (y_lo, gx, y_hi * 2 + 1 - core)

        def along(at, size):
            steps = [jnp.where(at + j >= size, at + j - size, at + j) for j in range(1, size)]
            return [(0, at)] + [(min(j, size - j), step) for j, step in enumerate(steps, 1)]

        plane = []
        for far_x, to_x in along(x, 4):
            for far_y, to_y in along(y_hi * 2 + y_lo, 4):
                to = (lax.rem(to_y, 2), self.z * 4 + to_x, lax.div(to_y, 2) * 2 + core)
                plane.append((far_x + far_y, to_x * 4 + to_y, to))
        rows = [(far, to_z, (y_lo, to_z * 4 + x, gy)) for far, to_z in along(self.z, 8)]
        self.plane = sorted(plane, key=lambda entry: -entry[0])[:-1]
        self.rows = sorted(rows, key=lambda entry: -entry[0])[:-1]

    def greet(self, barrier):
        for _, _, to in self.rows + self.plane:
            pl.semaphore_signal(barrier, inc=1, device_id=to, device_id_type=MESH)
        pl.semaphore_signal(barrier, inc=1, device_id=self.sibling, device_id_type=MESH)


class Summing:
    def __init__(self, ring, total, unspread, out, from_core, mine, from_plane, from_z, small, s_mine, s_plane, s_z, s_core, sems):
        self.__dict__.update(locals())
        self.ours = pl.multiple_of(ring.core * 16, 16)

    def copy(self, src, dst, pair, device):
        return pltpu.make_async_remote_copy(
            src, dst, self.sems.at[2 * pair], self.sems.at[2 * pair + 1], device_id=device, device_id_type=MESH
        )

    def begin(self):
        self.swap = self.copy(
            self.total.at[pl.ds(pl.multiple_of((1 - self.ring.core) * 96, 96), 96)], self.from_core, 0, self.ring.sibling
        )
        self.swap.start()

    def spread_plane(self, source, target, pair):
        for _, other, to in self.ring.plane:
            self.copy(source(other), target, pair, to).start()

    def spread_z(self, ref, pair):
        own = ref.at[self.ring.z]
        for _, _, to in self.ring.rows:
            self.copy(own, own, pair, to).start()

    def finish(self, ref, first, count, pair):
        part = ref.at[pl.ds(first, count)]
        self.copy(part, part, pair, self.ring.sibling).wait()

    def plane(self):
        self.swap.wait()
        mine = self.mine
        own = self.total[pl.ds(pl.multiple_of(self.ring.core * 96, 96), 96), pl.ds(0, 576)]
        flat = own + self.from_core[:, pl.ds(0, 576)]
        high = flat.astype(BF16)
        low = (flat - high.astype(F32)).astype(BF16)
        placed = jnp.dot(
            jnp.concatenate([high, low], axis=0), self.unspread[...], preferred_element_type=F32
        )
        placed = placed[:96] + placed[96:]
        full = placed[:32] + pltpu.roll(placed[32:64], 1, 1) + pltpu.roll(placed[64:], 2, 1)
        for c in range(16):
            at, half = 4 * (c // 2), 896 * (c % 2)
            mine[c] = full[at : at + 4, half : half + 896]
        place = self.ring.place
        self.spread_plane(lambda other: mine.at[other], self.from_plane.at[place], 1)
        self.from_plane[place] = mine[place]

    def small_plane(self):
        place = self.ring.place
        swap = self.copy(self.small, self.s_core, 8, self.ring.sibling)
        swap.start()
        swap.wait()
        self.s_mine[...] = self.small[...] + self.s_core[...]
        self.spread_plane(lambda other: self.s_mine, self.s_plane.at[place], 2)
        self.s_plane[place] = self.s_mine[...]

    def added(self, ref, count):
        value = ref[0]
        for j in range(1, count):
            value = value + ref[j]
        return value

    def along_z(self):
        self.finish(self.from_plane, 0, 15, 1)
        self.from_z[self.ring.z] = self.added(self.from_plane, 16)
        self.spread_z(self.from_z, 3)

    def rest(self):
        place, z = self.ring.place, self.ring.z
        self.finish(self.from_z, 0, 7, 3)
        own = self.out.at[self.ours + place]
        self.out[self.ours + place] = self.added(self.from_z, 8)
        self.spread_plane(lambda other: own, own, 5)
        self.finish(self.s_plane, 0, 15, 2)
        self.s_z[z] = self.added(self.s_plane, 16)
        self.spread_z(self.s_z, 4)

        self.finish(self.out, 0, 15, 5)
        half = self.out.at[pl.ds(self.ours, 16)]
        hand = self.copy(half, half, 7, self.ring.sibling)
        hand.start()
        self.finish(self.s_z, 0, 7, 4)
        both = self.added(self.s_z, 8)
        for block in range(8):
            at = 16 + block
            self.out[32 + at // 7, :, pl.ds(128 * (at % 7), 128)] = both[4 * block : 4 * block + 4]
        hand.wait()


def picks():
    grad = np.zeros((2, 144, 128), np.float32)
    ahead = np.zeros((6, 54, 144), np.float32)
    for ox in range(3):
        for oz in range(3):
            for ch in range(2):
                for oy in range(3):
                    tap = 27 * ch + 9 * ox + 3 * oy + oz
                    for y in range(2):
                        grad[y, ((ox * 3 + oz) * 2 + ch) * 8 + 2 + y + oy, tap] = 1
                    for y in range(6):
                        ahead[y, tap, ((ox * 3 + oz) * 2 + ch) * 8 + y + oy] = 1
    return grad, ahead


def main_kernel(
    loss_scale,
    sc_hbm, vel_hbm, w_mix_hbm, spread_hbm, w_lift_hbm, ahead_hbm, b_lift_hbm, b_mix_hbm, w_out_hbm, b_out_hbm,
    unspread_hbm, pick_hbm,
    out,
    adv, sc, vel, w_mix, spread, w_lift, ahead, b_lift, b_mix, w_out, b_out, unspread, pick,
    load, lift_w, mix_w, back_w, out_w, outt_w, bias,
    net, tgt, halo, held, wide, seen, inc, gains,
    v3, lifted, slope1, mixed, slope2, cot, down, errors, total,
    from_core, mine, from_plane, from_z, small, s_mine, s_plane, s_z, s_core,
    a_send, a_recv, b_send, b_recv, n_send, n_recv, c_send, c_recv, sums,
):
    pairs = (
        (sc_hbm, sc), (vel_hbm, vel), (w_mix_hbm, w_mix), (spread_hbm, spread), (w_lift_hbm, w_lift),
        (ahead_hbm, ahead), (b_lift_hbm, b_lift), (b_mix_hbm, b_mix), (w_out_hbm, w_out), (b_out_hbm, b_out),
        (unspread_hbm, unspread), (pick_hbm, pick),
    )
    loads = [pltpu.make_async_copy(*pair, load.at[j]) for j, pair in enumerate(pairs)]
    for copy in loads:
        copy.start()
    ring = Ring()
    prepared = Prepared(
        w_lift, b_lift, w_mix, b_mix, w_out, b_out, ahead, spread, lift_w, mix_w, back_w, out_w, outt_w, bias
    )

    def prepare_mix():
        for copy in loads[2:4]:
            copy.wait()
        prepared.mix_form()
        for copy in loads[:2]:
            copy.wait()

    def prepare_lift():
        for copy in loads[4:10]:
            copy.wait()
        prepared.lift_form()

    targets, sent = solver(
        ring, prepare_mix, prepare_lift, prepared.back_form,
        sc_hbm, sc, vel, adv, net, tgt, halo, held, wide, seen, inc, gains,
        a_send, a_recv, b_send, b_recv, n_send, n_recv, c_send, c_recv,
    )
    for copy in loads[10:]:
        copy.wait()
    summing = Summing(
        ring, total, unspread, out, from_core, mine, from_plane, from_z, small, s_mine, s_plane, s_z, s_core, sums
    )
    network(
        loss_scale, targets, summing, net, tgt, prepared, pick,
        v3, lifted, slope1, mixed, slope2, cot, down, errors, total, small,
    )
    for copy in sent:
        copy.wait_send()
    for block in range(16):
        out[32 + block // 7, :, pl.ds(128 * (block % 7), 128)] = adv[pl.ds(4 * block, 4), :]
    summing.rest()


def finish_kernel(out, adv, mix, lift, liftbias, mixbias, out_grad, outbias):
    def block(at):
        return out[32 + at // 7, :, pl.ds(128 * (at % 7), 128)]

    for at in range(16):
        adv[pl.ds(4 * at, 4), :] = block(at)
    for r in range(16):
        mix[pl.ds(4 * r, 4), pl.ds(0, 896)] = out[2 * r]
        mix[pl.ds(4 * r, 4), pl.ds(896, 832)] = out[2 * r + 1][:, :832]
    small = jnp.concatenate([block(16 + at) for at in range(8)], axis=0)
    turned = small.T
    turned = jnp.concatenate([turned[:64], turned[64:]], axis=1)
    lift[...] = turned[:54]
    liftbias[...] = turned[54:55]
    mixbias[...] = turned[55:56]
    out_grad[...] = turned[56:58]
    outbias[...] = turned[58:59, :2]


def train(loss_scale, scalars, velocity, w_lift, b_lift, w_mix, b_mix, w_out, b_out):
    dma = pltpu.SemaphoreType.DMA
    hbm = pl.BlockSpec(memory_space=pltpu.HBM)
    pick, ahead = picks()
    spread = np.zeros((64, 9, 3, 9, 64), np.float32)
    for m in range(9):
        for i in range(64):
            spread[i, m, 0, m, i] = 1
    spread = spread.reshape(1728, 576)
    unspread = np.zeros((576, 1792), np.float32)
    unspread[:, :1728] = spread.T
    chunk = (4, 896)

    def vmem(*shape, dtype=F32):
        return pltpu.VMEM(shape, dtype)

    out = pl.pallas_call(
        functools.partial(main_kernel, loss_scale),
        out_shape=jax.ShapeDtypeStruct((36,) + chunk, F32),
        in_specs=[hbm] * 12,
        out_specs=VMEM,
        scratch_shapes=[
            vmem(64, 128),
            vmem(64, 128), vmem(192, 128), vmem(64, 1728, dtype=BF16), vmem(1728, 576, dtype=BF16),
            vmem(54, 64, dtype=BF16), vmem(6, 54, 144, dtype=BF16), vmem(1, 64), vmem(1, 64),
            vmem(2, 64, dtype=BF16), vmem(1, 2), vmem(576, 1792, dtype=BF16), vmem(2, 144, 128), dma((12,)),
            vmem(384, 144, dtype=BF16), vmem(192, 576, dtype=BF16), vmem(192, 576, dtype=BF16),
            vmem(16, 256, dtype=BF16), vmem(256, 16, dtype=BF16), vmem(2, 64, 128),
            vmem(38 * 16, 128), vmem(34 * 8, 128),
            vmem(2, 64, 128), vmem(2, 32, 128), vmem(2, 32, 128, dtype=BF16),
            vmem(10, 2, 32, 128, dtype=BF16), vmem(8, 32, 128), vmem(2, 32, 128),
            vmem(22, 48, 128, dtype=BF16), vmem(20, 384, 128, dtype=BF16), vmem(20, 128, 128),
            vmem(18, 256, 128, dtype=BF16), vmem(18, 256, 128), vmem(18, 256, 128, dtype=BF16),
            vmem(16, 128, 128, dtype=BF16), vmem(18, 16, 128, dtype=BF16), vmem(192, 640),
            vmem(96, 640), vmem(16, *chunk), vmem(16, *chunk), vmem(8, *chunk),
            vmem(32, 128), vmem(32, 128), vmem(16, 32, 128), vmem(8, 32, 128), vmem(32, 128),
            dma, dma, dma, dma, dma, dma, dma, dma, dma((18,)),
        ],
        compiler_params=pltpu.CompilerParams(
            collective_id=0, has_side_effects=True, vmem_limit_bytes=VMEM_BYTES
        ),
        name="train",
    )(
        scalars, velocity, w_mix, jnp.asarray(spread, BF16), w_lift.T, jnp.asarray(ahead, BF16),
        b_lift[None], b_mix[None], w_out, b_out[None], jnp.asarray(unspread, BF16), jnp.asarray(pick),
    )
    shapes = ((64, 128), (64, 1728), (54, 64), (1, 64), (1, 64), (2, 64), (1, 2))
    return pl.pallas_call(
        finish_kernel,
        out_shape=tuple(jax.ShapeDtypeStruct(shape, F32) for shape in shapes),
        in_specs=[VMEM],
        out_specs=(VMEM,) * 7,
        compiler_params=pltpu.CompilerParams(vmem_limit_bytes=8 * 2**20),
        name="finish",
    )(out)


def on_device(scalars, velocity, w_lift, b_lift, w_mix, b_mix, w_out, b_out):
    total_cells = scalars.size * lax.axis_size("gx") * lax.axis_size("gy")
    loss_scale = 2.0 / math.sqrt(total_cells)
    adv, mix, lift, liftbias, mixbias, out_grad, outbias = train(
        loss_scale, scalars.reshape(64, 128), velocity.reshape(192, 128),
        w_lift, b_lift, w_mix, b_mix, w_out, b_out,
    )
    return (
        adv.reshape(scalars.shape), lift.T, liftbias[0], mix, mixbias[0], out_grad, outbias[0],
    )


def solution(mesh):
    cells = P("grp", None, ("gx", "gy"), None)
    in_specs = (cells, P(None, None, ("gx", "gy"), None)) + (P(),) * 6
    out_specs = (cells,) + (P(),) * 6
    return jax.shard_map(
        on_device, mesh=mesh, in_specs=in_specs, out_specs=out_specs, check_vma=False
    )
```
